128 devices in a mesh: exp: 32 (over z, y, core), tp: 4 (over x).
Axes of the slice: x: 4, y: 4, z: 4, core: 2. Of those that a mesh axis runs over, the one named last changes fastest.
Arguments:
- layer_in: bfloat16 [32768, 768], P('exp'), may hold values from -6 to 6
- expert_ids: int32 [32768, 1], P('exp'), may hold values from 0 to 31; in each aligned block of 1024 rows (0 to 1023, 1024 to 2047, ...) at most 40 rows name the same one
- rel_buckets: int32 [2047], replicated, may hold values from 0 to 31
- first_gain: float32 [768], replicated, may hold values from 0.5 to 1.5
- query_weight: bfloat16 [768, 768], P(None, 'tp'), may hold values from -0.02734375 to 0.02734375
- key_weight: bfloat16 [768, 768], P(None, 'tp'), may hold values from -0.21875 to 0.21875
- value_weight: bfloat16 [768, 768], P(None, 'tp'), may hold values from -0.21875 to 0.21875
- proj_weight: bfloat16 [768, 768], P('tp'), may hold values from -2.5 to 2.5
- rel_table: float32 [32, 12], P(None, 'tp'), may hold values from -6 to 6
- second_gain: float32 [768], replicated, may hold values from 0.5 to 1.5
- router_weight: bfloat16 [768, 32], replicated, may hold values from -0.109375 to 0.109375
- expert_in: bfloat16 [32, 768, 3072], P('exp', None, 'tp'), may hold values from -0.21875 to 0.21875
- expert_out: bfloat16 [32, 3072, 768], P('exp', 'tp'), may hold values from -6 to 6
- cotangent: bfloat16 [32768, 768], P('exp'), may hold values from -6 to 6
Outputs:
- layer_out: bfloat16 [32768, 768], P('exp')
- input_grad: float32 [32768, 768], P('exp')
- first_gain_grad: float32 [768], replicated
- query_grad: float32 [768, 768], P(None, 'tp')
- key_grad: float32 [768, 768], P(None, 'tp')
- value_grad: float32 [768, 768], P(None, 'tp')
- proj_grad: float32 [768, 768], P('tp')
- table_grad: float32 [32, 12], P(None, 'tp')
- second_gain_grad: float32 [768], replicated
- router_grad: float32 [768, 32], replicated
- expert_in_grad: float32 [32, 768, 3072], P('exp', None, 'tp')
- expert_out_grad: float32 [32, 3072, 768], P('exp', 'tp')
The draws below stay inside these ranges and needn't reach their ends.
Inputs may be any that keep to these rules, and one draw needn't show every extreme that they name: `expert_ids`: in the 1024 rows of one index of exp (aligned blocks) no expert is named by more than 40 rows, a bound that some block reaches. `rel_buckets`: entry m is the bucket of the offset m - 1023.
All inputs are finite; a program needn't handle non-finite values.
Results may differ from the reference program's by a relative error of at most 0.025.
Values may be sent and summed in bfloat16 or wider, within the bound.
A program may use at most 192 MiB of HBM per device.

```python
import math
import jax
import jax.numpy as jnp
import numpy as np
from jax import lax

D = 768
FF = 3072
HEADS = 12
HD = 64
BUCKETS = 32
LEN = 1024
TOK_EXP = 1024
TOKENS = 32768
EXPERTS = 32
CAP = 40
N_EXP = 32


def plant(entries, rng, least, high):
    longest = entries.shape.index(max(entries.shape))
    spots = []
    for shift in (0, 1):
        where = [jax.random.randint(jax.random.fold_in(rng, axis), (), 0, length) for axis, length in enumerate(entries.shape)]
        where[longest] = (where[longest] + shift) % entries.shape[longest]
        spots.append(tuple(where))
    return entries.at[spots[0]].set(least).at[spots[1]].set(high)


def level_of(rng, dims, cuts, least, high):
    loudness = 1.0
    for axis_at, parts in cuts:
        draws = jax.random.uniform(jax.random.fold_in(jax.random.fold_in(rng, 6), axis_at), (parts,), jnp.float32, least / len(cuts), high / len(cuts))
        loudness = loudness * jnp.repeat(jnp.exp(draws), dims[axis_at] // parts).reshape((-1,) + (1,) * (len(dims) - 1 - axis_at))
    return loudness


def shared_out(own_key, own, number, rows, number_of, top, reach, skew):
    ranking = jax.random.permutation(own_key, number_of)
    heavy_load, common = portions_of(number_of, rows * top, reach, skew, True), portions_of(number_of, rows * top, reach, skew, False)
    places = jnp.arange(number_of)

    def named(sizes, rotation):
        used = int((sizes > 0).sum())
        fixed = max(1, used // 4)
        moved = fixed + (places - fixed + rotation * (used - fixed)) % max(1, number_of - fixed)
        return jnp.zeros((number_of,), jnp.int32).at[ranking[jnp.where(places < fixed, places, moved)]].set(jnp.asarray(sizes, jnp.int32))

    sizes = jnp.where(number % 4 == 0, named(heavy_load, number // 4), named(common, number - number // 4 - 1))
    mixed = jax.random.permutation(jax.random.fold_in(own, 3), number_of)
    source_of, sink = mixed[0:number_of // 2 * 2:2], mixed[1:number_of // 2 * 2:2]
    margin = jnp.minimum(sizes[source_of] - 1, reach - sizes[sink]) // 2
    margin = jnp.where((source_of == ranking[0]) | (sink == ranking[0]) | (sizes[sink] == 0), 0, jnp.maximum(margin, 0))
    moved = jax.random.randint(jax.random.fold_in(own, 4), (number_of // 2,), 0, 1 << 20) % (margin + 1)
    sizes = sizes.at[source_of].add(-moved).at[sink].add(moved)
    members = jnp.searchsorted(jnp.cumsum(sizes), jnp.arange(rows * top), side="right").astype(jnp.int32)
    table = members.reshape(top, rows).T
    table = table[jax.random.permutation(jax.random.fold_in(own, 1), rows)]
    rotation = jax.random.randint(jax.random.fold_in(own, 2), (rows, 1), 0, top)
    return jnp.take_along_axis(table, (jnp.arange(top)[None, :] + rotation) % top, axis=1)


def portions_of(number_of, total, limit, skew, full):
    weights = [(1 << 20) // math.isqrt(rank ** skew) + 1 for rank in range(1, number_of + 1)]
    largest = limit if full else min(limit, max(-(-total // number_of), total * weights[0] // sum(weights)))
    least = 1 if total - largest >= number_of - 1 else 0
    given, spare = [largest] + [least] * (number_of - 1), total - largest - least * (number_of - 1)
    while spare > 0:
        candidates = [i for i in range(1, number_of) if given[i] < largest] or [i for i in range(1, number_of) if given[i] < limit]
        whole, remaining = sum([weights[i] for i in candidates]), spare
        for i in candidates:
            more = min(limit - given[i], max(1, remaining * weights[i] // whole), spare)
            given[i] = given[i] + more
            spare = spare - more
    return np.array(given)


def normal_values(own_key, dims, width, bound, cuts=(), kind=jnp.bfloat16):
    values = width * jax.random.normal(own_key, dims, jnp.float32)
    if cuts:
        values = values * level_of(own_key, dims, cuts, -0.22, 0.18)
    return jnp.clip(values, -bound, bound).astype(kind)


def setup_inputs(seed: int = 0) -> dict:
    key_of = jax.random.split(jax.random.key(seed), 15)
    layer_in = normal_values(key_of[0], (TOKENS, D), 1.0, 6.0, ((0, 32),))
    expert_ids_keys = jax.random.split(jax.random.fold_in(key_of[1], 1), TOKENS // TOK_EXP)
    expert_ids_turns = jax.random.permutation(jax.random.fold_in(key_of[1], 3), TOKENS // TOK_EXP)
    expert_ids = jax.vmap(lambda own, number: shared_out(jax.random.fold_in(key_of[1], 2), own, number, TOK_EXP, EXPERTS, 1, CAP, 1))(expert_ids_keys, expert_ids_turns).reshape((TOKENS, 1))
    rel_buckets = plant(jax.random.randint(key_of[2], (2 * LEN - 1,), 0, BUCKETS), jax.random.fold_in(key_of[2], 1), 0, BUCKETS - 1).astype(jnp.int32)
    first_gain = jnp.clip(1.0 + 0.1 * jax.random.normal(key_of[3], (D,), jnp.float32), 0.5, 1.5)
    query_weight = normal_values(key_of[4], (D, HEADS * HD), (D * HD) ** -0.5, 0.02734375, ((1, 4),))
    key_weight = normal_values(key_of[5], (D, HEADS * HD), D ** -0.5, 0.21875, ((1, 4),))
    value_weight = normal_values(key_of[6], (D, HEADS * HD), D ** -0.5, 0.21875, ((1, 4),))
    proj_weight = normal_values(key_of[7], (HEADS * HD, D), (max(D // 128, 1)) ** -0.5, 2.5, ((0, 4),))
    rel_table = normal_values(key_of[8], (BUCKETS, HEADS), 1.0, 6.0, ((1, 4),), jnp.float32)
    second_gain = jnp.clip(1.0 + 0.1 * jax.random.normal(key_of[9], (D,), jnp.float32), 0.5, 1.5)
    router_weight = normal_values(key_of[10], (D, EXPERTS), (4 * D) ** -0.5, 0.109375)
    expert_in = normal_values(key_of[11], (EXPERTS, D, FF), D ** -0.5, 0.21875, ((0, 32), (2, 4)))
    expert_out = normal_values(key_of[12], (EXPERTS, FF, D), (max(FF // (2 * EXPERTS * EXPERTS), 1)) ** -0.5, 6.0, ((0, 32), (1, 4)))
    cotangent = normal_values(key_of[13], (TOKENS, D), 1.0, 6.0, ((0, 32),))
    return {"layer_in": layer_in, "expert_ids": expert_ids, "rel_buckets": rel_buckets, "first_gain": first_gain, "query_weight": query_weight, "key_weight": key_weight, "value_weight": value_weight, "proj_weight": proj_weight, "rel_table": rel_table, "second_gain": second_gain, "router_weight": router_weight, "expert_in": expert_in, "expert_out": expert_out, "cotangent": cotangent}


epsilon = 1e-06
gelu_root = 0.7978845608028654
gelu_cube = 0.044715

@jax.custom_vjp
def low(v):
    return lax.optimization_barrier(v.astype(jnp.bfloat16)).astype(jnp.float32)

@jax.custom_vjp
def low_back(v):
    return v

def low_keep(v):
    return (low(v), None)

def low_pass(kept, grad):
    return (grad,)

def back_keep(v):
    return (v, None)

def back_low(kept, grad):
    return (low(grad),)
low.defvjp(low_keep, low_pass)
low_back.defvjp(back_keep, back_low)

def rms_norm(values, gain_vector):
    return values * lax.rsqrt(lax.optimization_barrier(jnp.mean(values * values, axis=-1, keepdims=True)) + epsilon) * gain_vector

def gelu_tanh(values):
    return 0.5 * values * (1.0 + jnp.tanh(gelu_root * (values + gelu_cube * values * values * values)))

def product(left_side, right_side):
    return jnp.dot(left_side, right_side, precision=lax.Precision.HIGHEST)

def softmax_rows(scores):
    shifted = scores - lax.optimization_barrier(jnp.max(scores, axis=-1, keepdims=True))
    weights = jnp.exp(shifted)
    return weights / lax.optimization_barrier(jnp.sum(weights, axis=-1, keepdims=True))

def place_rows(rows_group, slot_ids):
    return jnp.zeros((EXPERTS * CAP, D), jnp.float32).at[slot_ids].add(rows_group)

def pick_rows(table_rows, slot_ids):
    return table_rows[slot_ids]

def reference(layer_in, expert_ids, rel_buckets, first_gain, query_weight, key_weight, value_weight, proj_weight, rel_table, second_gain, router_weight, expert_in, expert_out, cotangent):
    chosen = expert_ids[:, 0].reshape(N_EXP, TOK_EXP)
    expert_hot = chosen[:, :, None] == jnp.arange(EXPERTS, dtype=jnp.int32)[None, None, :]
    counts = jnp.cumsum(expert_hot.astype(jnp.int32), axis=1)
    position = lax.optimization_barrier(jnp.sum(jnp.where(expert_hot, counts - 1, 0), axis=2)).astype(jnp.int32)
    token_slot = (chosen * CAP + position).astype(jnp.int32)
    hot_flat = expert_hot.reshape(TOKENS, EXPERTS)
    offset_index = (jnp.arange(LEN, dtype=jnp.int32)[None, :] - jnp.arange(LEN, dtype=jnp.int32)[:, None] + LEN - 1).astype(jnp.int32)
    bucket_grid = rel_buckets[offset_index]

    def forward(inputs, gain_one, query_param, key_param, value_param, proj_param, rel_weights, gain_two, router_param, inner_param, outer_param):
        normed = low(rms_norm(inputs, gain_one))

        def to_heads(weight_matrix):
            return low(low_back(product(normed, weight_matrix))).reshape(TOKENS // LEN, LEN, HEADS, HD)
        query_all = to_heads(query_param)
        key_all = to_heads(key_param)
        value_all = to_heads(value_param)
        rel_bias = jnp.transpose(rel_weights[bucket_grid], (2, 0, 1))

        def attend(pieces):
            query_seq, key_seq, value_seq = pieces
            scores = jnp.einsum('qhd,khd->hqk', query_seq, key_seq, precision=lax.Precision.HIGHEST) + rel_bias
            probs_low = low(softmax_rows(low_back(scores)))
            return jnp.einsum('hqk,khd->qhd', probs_low, value_seq, precision=lax.Precision.HIGHEST)
        attended = lax.map(jax.checkpoint(attend), (query_all, key_all, value_all))
        mixed = low(low_back(attended.reshape(TOKENS, HEADS * HD)))
        residual = inputs + low_back(product(mixed, proj_param))
        hidden_in = low(rms_norm(residual, gain_two))
        router_probs = softmax_rows(low_back(product(hidden_in, router_param)))
        gate_value = lax.optimization_barrier(jnp.sum(jnp.where(hot_flat, router_probs, 0.0), axis=1))
        groups = hidden_in.reshape(N_EXP, TOK_EXP, D)
        slots_all = low_back(jax.vmap(place_rows)(groups, token_slot))
        by_expert = jnp.transpose(slots_all.reshape(N_EXP, EXPERTS, CAP, D), (1, 0, 2, 3)).reshape(EXPERTS, N_EXP * CAP, D)

        def expert(pieces):
            slot_rows, weight_in, weight_out = pieces
            pre_act = low_back(product(slot_rows, weight_in))
            return low(low_back(product(low(gelu_tanh(pre_act)), weight_out)))
        expert_rows = lax.map(jax.checkpoint(expert), (by_expert, inner_param, outer_param))
        back_slots = jnp.transpose(expert_rows.reshape(EXPERTS, N_EXP, CAP, D), (1, 0, 2, 3)).reshape(N_EXP, EXPERTS * CAP, D)
        token_rows = jax.vmap(pick_rows)(back_slots, token_slot).reshape(TOKENS, D)
        return residual + gate_value[:, None] * token_rows
    output, pullback = jax.vjp(forward, layer_in.astype(jnp.float32), first_gain, query_weight.astype(jnp.float32), key_weight.astype(jnp.float32), value_weight.astype(jnp.float32), proj_weight.astype(jnp.float32), rel_table, second_gain, router_weight.astype(jnp.float32), expert_in.astype(jnp.float32), expert_out.astype(jnp.float32))
    gradients = pullback(cotangent.astype(jnp.float32))
    return (output.astype(jnp.bfloat16), gradients[0], gradients[1], gradients[2], gradients[3], gradients[4], gradients[5], gradients[6], gradients[7], gradients[8], gradients[9], gradients[10])
```

```python
import functools

import jax
import jax.numpy as jnp
from jax import lax
from jax.experimental import pallas as pl
from jax.experimental.pallas import tpu as pltpu
from jax.sharding import PartitionSpec as P

epsilon = 1e-06
gelu_root = 0.7978845608028654
gelu_cube = 0.044715
BF = jnp.bfloat16
F32 = jnp.float32
BLOCK = 128
MIB = 1024 * 1024


def product(left, right):
    return jnp.dot(left, right, preferred_element_type=F32)


def rows_product(left, right):
    return lax.dot_general(left, right, (((0,), (0,)), ((), ())), preferred_element_type=F32)


def cols_product(left, right):
    return lax.dot_general(left, right, (((1,), (1,)), ((), ())), preferred_element_type=F32)


def inverse_rms(values):
    return lax.rsqrt(jnp.mean(values * values, axis=-1, keepdims=True) + epsilon)


def call(body, name, outs, scratch, *operands, mib=48):
    vmem = pl.BlockSpec(memory_space=pltpu.VMEM)
    return pl.pallas_call(
        body,
        name=name,
        out_shape=[jax.ShapeDtypeStruct(shape, dtype) for shape, dtype in outs],
        in_specs=[vmem] * len(operands),
        out_specs=[vmem] * len(outs),
        scratch_shapes=scratch,
        compiler_params=pltpu.CompilerParams(vmem_limit_bytes=mib * MIB),
    )(*operands)


def head_mask(head, head_width, width):
    lane = lax.broadcasted_iota(jnp.int32, (1, width), 1)
    return jnp.where(lane // head_width == head, 1.0, 0.0)


def fill_bias(bias, buckets, table):
    heads, block, width = bias.shape
    padded = buckets.shape[1]
    number = lax.broadcasted_iota(jnp.int32, (table.shape[0], padded), 0)
    hot = jnp.where(buckets[...] == number, 1.0, 0.0)
    offsets = lax.dot_general(
        table[...],
        hot,
        (((0,), (0,)), ((), ())),
        precision=lax.Precision.HIGHEST,
        preferred_element_type=F32,
    )
    for head in range(heads):
        spread = jnp.broadcast_to(offsets[head : head + 1, :], (block, padded))
        rolled = pltpu.roll(spread, padded - (block - 1), 1, stride=1, stride_axis=0)
        bias[head] = rolled[:, :width]


def attend_body(
    head_width, rows, gain, query_w, key_w, value_w, buckets, table,
    mixed, normed, query, query_t, key, key_t, value_t, logsum, bias, value,
):
    heads = bias.shape[0]
    tokens = rows.shape[0]
    width = query.shape[1]
    blocks = tokens // BLOCK
    inputs = rows[...].astype(F32)
    low = (inputs * inverse_rms(inputs) * gain[...]).astype(BF)
    normed[...] = low
    query_full = product(low, query_w[...])
    key_full = product(low, key_w[...])
    value_full = product(low, value_w[...])
    query[...] = query_full.astype(BF)
    key[...] = key_full.astype(BF)
    value[...] = value_full.astype(BF)
    query_t[...] = query_full.T.astype(BF)
    key_t[...] = key_full.T.astype(BF)
    value_t[...] = value_full.T.astype(BF)
    fill_bias(bias, buckets, table)

    def step(block, carry):
        first = pl.multiple_of(block * BLOCK, BLOCK)
        shift = pl.multiple_of((blocks - 1 - block) * BLOCK, BLOCK)
        query_rows = query[pl.ds(first, BLOCK), :]
        total = jnp.zeros((BLOCK, width), F32)
        for head in range(heads):
            mask = head_mask(head, head_width, width)
            scores = product(query_rows * mask.astype(BF), key_t[...])
            scores = scores + bias[head, :, pl.ds(shift, tokens)]
            highest = jnp.max(scores, axis=-1, keepdims=True)
            weights = jnp.exp(scores - highest)
            summed = jnp.sum(weights, axis=-1, keepdims=True)
            part = product(weights.astype(BF), value[...]) / summed
            total = total + part * mask
            logsum[pl.ds(first, BLOCK), head : head + 1] = highest + jnp.log(summed)
        mixed[pl.ds(first, BLOCK), :] = total.astype(BF)
        return carry

    lax.fori_loop(0, blocks, step, 0)


def pack(first, second, third, experts):
    half = third.shape[1] // 2
    split = third.reshape(experts, 8, 2 * half)
    split = jnp.concatenate([split[:, :, :half], split[:, :, half:]], axis=1)
    return first, second, split.reshape(experts * 16, half)


def unpack_third(tail, runs):
    half = tail.shape[1]
    split = tail.astype(F32).reshape(runs, 16, half)
    return jnp.concatenate([split[:, :8], split[:, 8:]], axis=2).reshape(runs * 8, 2 * half)


def slot_of_row(row, experts, capacity):
    body = 16 * experts
    first = (row // 16) * capacity + row % 16
    second = ((row - body) // 16) * capacity + 16 + (row - body) % 16
    third = ((row - 2 * body) // 8) * capacity + 32 + (row - 2 * body) % 8
    return jnp.where(row < body, first, jnp.where(row < 2 * body, second, third))


def route_body(
    capacity, rows, mixed, proj, gain, router_w, ids, ids_row, cotangent,
    residual, hidden, probs, send_rows, send_grads, slots, gates,
):
    tokens, width = rows.shape
    experts = router_w.shape[1]
    body = 16 * experts
    res = rows[...].astype(F32) + product(mixed[...], proj[...])
    residual[...] = res
    low = (res * inverse_rms(res) * gain[...]).astype(BF)
    hidden[...] = low
    logits = product(low, router_w[...])
    shifted = jnp.exp(logits - jnp.max(logits, axis=-1, keepdims=True))
    chances = shifted / jnp.sum(shifted, axis=-1, keepdims=True)
    probs[...] = chances
    hot = ids[...] == lax.broadcasted_iota(jnp.int32, (tokens, experts), 1)
    hot_t = ids_row[...] == lax.broadcasted_iota(jnp.int32, (experts, tokens), 0)
    gate = jnp.sum(jnp.where(hot, chances, 0.0), axis=1, keepdims=True)
    gates[...] = gate
    across = lax.broadcasted_iota(jnp.int32, (tokens, tokens), 0)
    along = lax.broadcasted_iota(jnp.int32, (tokens, tokens), 1)
    lower = jnp.where(across >= along, 1.0, 0.0).astype(BF)
    upper = jnp.where(across <= along, 1.0, 0.0).astype(BF)
    counts = product(lower, jnp.where(hot, 1.0, 0.0).astype(BF))
    counts_t = product(jnp.where(hot_t, 1.0, 0.0).astype(BF), upper)
    position = jnp.sum(jnp.where(hot, counts - 1.0, 0.0), axis=1, keepdims=True)
    position_t = jnp.sum(jnp.where(hot_t, counts_t - 1.0, 0.0), axis=0, keepdims=True)
    slots[...] = ids[...] * capacity + position.astype(jnp.int32)
    slots_t = ids_row[...] * capacity + position_t.astype(jnp.int32)
    grads = (gate * cotangent[...].astype(F32)).astype(BF)

    def group(begin, count):
        number = slot_of_row(
            lax.broadcasted_iota(jnp.int32, (count, 1), 0) + begin, experts, capacity
        )
        return jnp.where(number == slots_t, 1.0, 0.0).astype(BF)

    for begin, count, lane in ((0, body, 0), (body, body, width)):
        place = group(begin, count)
        send_rows[:, lane : lane + width] = product(place, low).astype(BF)
        send_grads[:, lane : lane + width] = product(place, grads).astype(BF)
    place = group(2 * body, body // 2)
    send_rows[:, 2 * width :] = pack(0, 0, product(place, low), experts)[2].astype(BF)
    send_grads[:, 2 * width :] = pack(0, 0, product(place, grads), experts)[2].astype(BF)


def expert_body(
    rows, grads, weight_in, weight_out,
    value, back, in_grad, out_grad, tail_rows, tail_grads, tail_value, tail_back, tail_dot,
):
    width = weight_in.shape[0]
    body = rows.shape[0]
    runs = body // 16
    tail_rows[...] = unpack_third(rows[:, 2 * width :], runs).astype(BF)
    tail_grads[...] = unpack_third(grads[:, 2 * width :], runs).astype(BF)
    in_grad[...] = jnp.zeros(in_grad.shape, F32)
    out_grad[...] = jnp.zeros(out_grad.shape, F32)

    def chunk(x, g):
        pre = product(x, weight_in[...])
        inner = jnp.tanh(gelu_root * (pre + gelu_cube * pre * pre * pre))
        act = (0.5 * pre * (1.0 + inner)).astype(BF)
        slope = 0.5 * (1.0 + inner) + 0.5 * pre * (1.0 - inner * inner) * (
            gelu_root * (1.0 + 3.0 * gelu_cube * pre * pre)
        )
        out = product(act, weight_out[...])
        dots = jnp.sum(out * g.astype(F32), axis=1, keepdims=True)
        out_grad[...] += rows_product(act, g)
        act_grad = cols_product(g, weight_out[...])
        pre_grad = (act_grad * slope).astype(BF)
        in_grad[...] += rows_product(x, pre_grad)
        rows_back = cols_product(pre_grad, weight_in[...])
        return out, dots, rows_back

    lane = lax.broadcasted_iota(jnp.int32, (1, 128), 1)
    part = 256
    for begin in range(0, body, part):
        spot = pl.ds(begin, part)
        marks = jnp.zeros((part, 128), F32)
        for side in (0, 1):
            lanes = slice(side * width, (side + 1) * width)
            out, dots, rows_back = chunk(rows[spot, lanes], grads[spot, lanes])
            value[spot, lanes] = out.astype(BF)
            back[spot, lanes] = rows_back.astype(BF)
            marks = marks + jnp.where(lane == side, dots, 0.0)
        back[spot, 2 * width + width // 2 :] = marks.astype(BF)
    out, dots, rows_back = chunk(tail_rows[...], tail_grads[...])
    value[:, 2 * width :] = pack(0, 0, out, runs)[2].astype(BF)
    back[:, 2 * width : 2 * width + width // 2] = pack(0, 0, rows_back, runs)[2].astype(BF)
    spread = jnp.where(lane == 2, dots, 0.0).reshape(runs, 8, 128)
    spread = jnp.concatenate([spread, jnp.zeros_like(spread)], axis=1).reshape(body, 128)
    marks = back[:, 2 * width + width // 2 :].astype(F32) + spread
    back[:, 2 * width + width // 2 :] = marks.astype(BF)


def place_of(slots, experts, capacity, rows):
    number = slot_of_row(lax.broadcasted_iota(jnp.int32, (1, rows), 1), experts, capacity)
    return jnp.where(slots == number, 1.0, 0.0).astype(BF)


def token_body(
    capacity, returned, back, slots, gates, residual, hidden, probs, ids, gain, router_w,
    cotangent, mixed, proj,
    output, router_grad, gain_grad, residual_grad, proj_grad, mixed_grad, mixed_grad_t,
):
    tokens, width = residual.shape
    experts = router_w.shape[1]
    body = 16 * experts
    place = place_of(slots[...], experts, capacity, 5 * body // 2)

    def fetch(ref):
        picked = product(place[:, :body], ref[:, :width])
        picked = picked + product(place[:, body : 2 * body], ref[:, width : 2 * width])
        tail = unpack_third(ref[:, 2 * width : 2 * width + width // 2], experts).astype(BF)
        return picked + product(place[:, 2 * body :], tail)

    token_rows = fetch(returned)
    upstream = cotangent[...].astype(F32)
    res = residual[...]
    output[...] = (res + gates[...] * token_rows).astype(BF)
    marks = back[:, 2 * width + width // 2 :]
    lane = lax.broadcasted_iota(jnp.int32, (1, 128), 1)
    tail = marks.astype(F32).reshape(experts, 16, 128)[:, :8].reshape(experts * 8, 128).astype(BF)
    dots = jnp.where(lane == 0, product(place[:, :body], marks), 0.0)
    dots = dots + jnp.where(lane == 1, product(place[:, body : 2 * body], marks), 0.0)
    dots = dots + jnp.where(lane == 2, product(place[:, 2 * body :], tail), 0.0)
    weighted = jnp.sum(dots, axis=1, keepdims=True)
    hot = ids[...] == lax.broadcasted_iota(jnp.int32, (tokens, experts), 1)
    logit_grad = (jnp.where(hot, weighted, 0.0) - probs[...] * weighted).astype(BF)
    router_grad[...] = rows_product(hidden[...], logit_grad).astype(BF)
    hidden_grad = fetch(back) + cols_product(logit_grad, router_w[...])
    scale = inverse_rms(res)
    gain_grad[...] = jnp.sum(hidden_grad * res * scale, axis=0, keepdims=True).astype(BF)
    scaled = gain[...] * hidden_grad
    middle = jnp.mean(scaled * res, axis=-1, keepdims=True)
    total = upstream + scale * scaled - res * (scale * scale * scale * middle)
    low = total.astype(BF)
    residual_grad[...] = total
    proj_grad[...] = rows_product(mixed[...], low).astype(BF)
    mixed_grad[...] = cols_product(low, proj[...]).astype(BF)
    mixed_grad_t[...] = cols_product(proj[...], low).astype(BF)


def attend_back_body(
    head_width, normed, query, query_t, key, key_t, value_t, logsum, grad, grad_t,
    query_w, key_w, value_w, buckets, table,
    normed_part, query_grad, key_grad, value_grad, table_grad,
    bias, sums, query_back, key_acc, value_acc,
):
    heads = bias.shape[0]
    tokens, width = query.shape
    blocks = tokens // BLOCK
    fill_bias(bias, buckets, table)
    sums[...] = jnp.zeros(sums.shape, F32)
    key_acc[...] = jnp.zeros(key_acc.shape, F32)
    value_acc[...] = jnp.zeros(value_acc.shape, F32)

    def step(block, carry):
        first = pl.multiple_of(block * BLOCK, BLOCK)
        shift = pl.multiple_of((blocks - 1 - block) * BLOCK, BLOCK)
        query_rows = query[pl.ds(first, BLOCK), :]
        grad_rows = grad[pl.ds(first, BLOCK), :]
        total = jnp.zeros((BLOCK, width), F32)
        for head in range(heads):
            mask = head_mask(head, head_width, width)
            span = slice(head * head_width, (head + 1) * head_width)
            scores = product(query_rows * mask.astype(BF), key_t[...])
            scores = scores + bias[head, :, pl.ds(shift, tokens)]
            probs = jnp.exp(scores - logsum[pl.ds(first, BLOCK), head : head + 1])
            prob_grad = product(grad_rows * mask.astype(BF), value_t[...])
            middle = jnp.sum(probs * prob_grad, axis=-1, keepdims=True)
            score_grad = probs * (prob_grad - middle)
            low = score_grad.astype(BF)
            sums[head, :, pl.ds(shift, tokens)] += score_grad
            total = total + product(low, key[...]) * mask
            key_acc[span, :] += product(query_t[span, pl.ds(first, BLOCK)], low)
            value_acc[span, :] += product(grad_t[span, pl.ds(first, BLOCK)], probs.astype(BF))
        query_back[pl.ds(first, BLOCK), :] = total.astype(BF)
        return carry

    lax.fori_loop(0, blocks, step, 0)
    key_back = key_acc[...].T.astype(BF)
    value_back = value_acc[...].T.astype(BF)
    normed_part[...] = (
        cols_product(query_back[...], query_w[...])
        + cols_product(key_back, key_w[...])
        + cols_product(value_back, value_w[...])
    ).astype(BF)
    query_grad[...] = rows_product(normed[...], query_back[...]).astype(BF)
    key_grad[...] = rows_product(normed[...], key_back).astype(BF)
    value_grad[...] = rows_product(normed[...], value_back).astype(BF)

    padded = buckets.shape[1]
    lines = []
    for head in range(heads):
        wide = jnp.concatenate(
            [sums[head], jnp.zeros((BLOCK, padded - sums.shape[2]), F32)], axis=1
        )
        gathered = jnp.zeros((8, padded), F32)
        for part in range(BLOCK // 8):
            piece = wide[part * 8 : part * 8 + 8, :]
            gathered = gathered + pltpu.roll(piece, (BLOCK - 1 - part * 8) % padded, 1)
        line = jnp.zeros((1, padded), F32)
        for row in range(8):
            line = line + pltpu.roll(gathered, (padded - row) % padded, 1)[row : row + 1, :]
        lines.append(line)
    number = lax.broadcasted_iota(jnp.int32, (table.shape[0], padded), 0)
    hot = buckets[...] == number
    for head in range(heads):
        table_grad[:, head : head + 1] = jnp.sum(
            jnp.where(hot, lines[head], 0.0), axis=1, keepdims=True
        ).astype(BF)


def per_device(
    layer_in, expert_ids, rel_buckets, first_gain, query_weight, key_weight, value_weight,
    proj_weight, rel_table, second_gain, router_weight, expert_in, expert_out, cotangent,
):
    tokens, width = layer_in.shape
    heads = rel_table.shape[1]
    here = query_weight.shape[1]
    head_width = here // heads
    experts = router_weight.shape[1]
    capacity = 5 * tokens // (4 * experts)
    body = 16 * experts
    packed = 2 * width + width // 2
    padded = rel_buckets.shape[0] + 1
    span = 2 * tokens - BLOCK
    gain_one = first_gain[None, :]
    gain_two = second_gain[None, :]
    buckets = jnp.pad(rel_buckets, (0, 1), constant_values=-1)[None, :]
    proj_full = lax.all_gather(proj_weight, "tp", axis=0, tiled=True)

    mixed, normed, query, query_t, key, key_t, value_t, logsum = call(
        functools.partial(attend_body, head_width),
        "attend",
        [
            ((tokens, here), BF),
            ((tokens, width), BF),
            ((tokens, here), BF),
            ((here, tokens), BF),
            ((tokens, here), BF),
            ((here, tokens), BF),
            ((here, tokens), BF),
            ((tokens, 128), F32),
        ],
        [pltpu.VMEM((heads, BLOCK, span), F32), pltpu.VMEM((tokens, here), BF)],
        layer_in, gain_one, query_weight, key_weight, value_weight, buckets, rel_table,
    )
    mixed_full = lax.all_gather(mixed, "tp", axis=1, tiled=True)
    residual, hidden, probs, send_rows, send_grads, slots, gates = call(
        functools.partial(route_body, capacity),
        "route",
        [
            ((tokens, width), F32),
            ((tokens, width), BF),
            ((tokens, experts), F32),
            ((body, packed), BF),
            ((body, packed), BF),
            ((tokens, 1), jnp.int32),
            ((tokens, 1), F32),
        ],
        [],
        layer_in, mixed_full, proj_full, gain_two, router_weight, expert_ids,
        expert_ids.reshape(1, tokens), cotangent,
    )

    def exchange(array):
        split = array.reshape(experts, 16, array.shape[1])
        moved = lax.all_to_all(split, "exp", split_axis=0, concat_axis=0, tiled=True)
        return moved.reshape(array.shape)

    value, back, in_grad, out_grad = call(
        expert_body,
        "expert",
        [
            ((body, packed), BF),
            ((body, packed + 128), BF),
            ((width, expert_in.shape[2]), F32),
            ((expert_out.shape[1], width), F32),
        ],
        [pltpu.VMEM((body // 2, width), BF)] * 2 + [pltpu.VMEM((8, 128), F32)] * 3,
        exchange(send_rows), exchange(send_grads), expert_in[0], expert_out[0],
    )
    back_sum = exchange(lax.psum(back, "tp"))
    value_sum = exchange(lax.psum(value, "tp"))
    (
        output, router_grad, second_gain_grad, residual_grad, proj_grad, mixed_grad, mixed_grad_t
    ) = call(
        functools.partial(token_body, capacity),
        "token",
        [
            ((tokens, width), BF),
            ((width, experts), BF),
            ((1, width), BF),
            ((tokens, width), F32),
            ((here, width), BF),
            ((tokens, here), BF),
            ((here, tokens), BF),
        ],
        [],
        value_sum, back_sum, slots, gates, residual, hidden, probs, expert_ids, gain_two,
        router_weight, cotangent, mixed, proj_weight,
    )
    normed_part, query_grad, key_grad, value_grad, table_grad = call(
        functools.partial(attend_back_body, head_width),
        "attend_back",
        [
            ((tokens, width), BF),
            ((width, here), BF),
            ((width, here), BF),
            ((width, here), BF),
            ((rel_table.shape[0], heads), BF),
        ],
        [
            pltpu.VMEM((heads, BLOCK, span), F32),
            pltpu.VMEM((heads, BLOCK, span), F32),
            pltpu.VMEM((tokens, here), BF),
            pltpu.VMEM((here, tokens), F32),
            pltpu.VMEM((here, tokens), F32),
        ],
        normed, query, query_t, key, key_t, value_t, logsum, mixed_grad, mixed_grad_t,
        query_weight, key_weight, value_weight, buckets, rel_table,
    )
    normed_grad = lax.psum(normed_part, "tp").astype(F32)
    inputs = layer_in.astype(F32)
    scale = inverse_rms(inputs)
    first_gain_grad = jnp.sum(normed_grad * inputs * scale, axis=0)
    scaled = normed_grad * first_gain
    middle = jnp.mean(scaled * inputs, axis=-1, keepdims=True)
    input_grad = residual_grad + scale * scaled - inputs * (scale * scale * scale * middle)

    def over_batch(part):
        return lax.psum(part.astype(BF), "exp").astype(F32)

    return (
        output,
        input_grad,
        over_batch(first_gain_grad),
        over_batch(query_grad),
        over_batch(key_grad),
        over_batch(value_grad),
        over_batch(proj_grad),
        over_batch(table_grad),
        over_batch(second_gain_grad)[0],
        over_batch(router_grad),
        in_grad[None],
        out_grad[None],
    )


def solution(mesh):
    return jax.shard_map(
        per_device,
        mesh=mesh,
        in_specs=(
            P("exp", None),
            P("exp", None),
            P(),
            P(),
            P(None, "tp"),
            P(None, "tp"),
            P(None, "tp"),
            P("tp", None),
            P(None, "tp"),
            P(),
            P(),
            P("exp", None, "tp"),
            P("exp", "tp", None),
            P("exp", None),
        ),
        out_specs=(
            P("exp", None),
            P("exp", None),
            P(),
            P(None, "tp"),
            P(None, "tp"),
            P(None, "tp"),
            P("tp", None),
            P(None, "tp"),
            P(),
            P(),
            P("exp", None, "tp"),
            P("exp", "tp", None),
        ),
        check_vma=False,
    )
```

```python
import functools

import jax
import jax.numpy as jnp
from jax import lax
from jax.experimental import pallas as pl
from jax.experimental.pallas import tpu as pltpu
from jax.sharding import PartitionSpec as P

epsilon = 1e-06
gelu_root = 0.7978845608028654
gelu_cube = 0.044715
BF = jnp.bfloat16
F32 = jnp.float32
BLOCK = 128
MIB = 1024 * 1024
GROUPS = 4
MESH = pl.DeviceIdType.MESH


def product(left, right):
    return jnp.dot(left, right, preferred_element_type=F32)


def rows_product(left, right):
    return lax.dot_general(left, right, (((0,), (0,)), ((), ())), preferred_element_type=F32)


def cols_product(left, right):
    return lax.dot_general(left, right, (((1,), (1,)), ((), ())), preferred_element_type=F32)


def inverse_rms(values):
    return lax.rsqrt(jnp.mean(values * values, axis=-1, keepdims=True) + epsilon)


def call(body, name, outs, scratch, *operands, mib=48, number=None):
    vmem = pl.BlockSpec(memory_space=pltpu.VMEM)
    extra = {} if number is None else {"collective_id": number, "has_side_effects": True}
    return pl.pallas_call(
        body,
        name=name,
        out_shape=[jax.ShapeDtypeStruct(shape, dtype) for shape, dtype in outs],
        in_specs=[vmem] * len(operands),
        out_specs=[vmem] * len(outs),
        scratch_shapes=scratch,
        compiler_params=pltpu.CompilerParams(vmem_limit_bytes=mib * MIB, **extra),
    )(*operands)


def remote(source, target, send, receive, **where):
    return pltpu.make_async_remote_copy(
        src_ref=source,
        dst_ref=target,
        send_sem=send,
        recv_sem=receive,
        device_id=where,
        device_id_type=MESH,
    )


def ring(ring_size):
    here = lax.axis_index("tp")
    return here, lax.rem(here + 1, ring_size), lax.rem(here + ring_size - 1, ring_size)


def greet(ring_size, batch_size, opposite=False):
    barrier = pltpu.get_barrier_semaphore()
    here, right, left = ring(ring_size)
    for side in (right, left):
        pl.semaphore_signal(barrier, inc=1, device_id={"tp": side}, device_id_type=MESH)
    if opposite:
        side = lax.rem(here + 2, ring_size)
        pl.semaphore_signal(barrier, inc=1, device_id={"tp": side}, device_id_type=MESH)
    if batch_size:
        me = lax.axis_index("exp")

        def hello(step, carry):
            peer = lax.rem(me + step, batch_size)
            pl.semaphore_signal(barrier, inc=1, device_id={"exp": peer}, device_id_type=MESH)
            return carry

        lax.fori_loop(1, batch_size, hello, 0)
    return 2 + int(opposite) + max(batch_size - 1, 0)


def meet(signals):
    pl.semaphore_wait(pltpu.get_barrier_semaphore(), signals)


class Gather:
    def __init__(self, region, half, sems):
        self.region, self.half, self.sems = region, half, sems
        self.here, self.right, self.left = ring(4)
        self.far = lax.rem(self.here + 2, 4)

    def first(self, k):
        own = self.region(k, self.here)
        return (
            remote(own, own, self.sems.at[k, 0], self.sems.at[k, 1], tp=self.right),
            remote(own, own, self.sems.at[k, 2], self.sems.at[k, 3], tp=self.left),
        )

    def second(self, k):
        low, high = self.half(k, self.left, 0), self.half(k, self.right, 1)
        return (
            remote(low, low, self.sems.at[k, 4], self.sems.at[k, 5], tp=self.right),
            remote(high, high, self.sems.at[k, 6], self.sems.at[k, 7], tp=self.left),
        )

    def start(self, k):
        for copy in self.first(k):
            copy.start()

    def forward(self, k):
        for side, copy, arrived in zip(
            (self.left, self.right), self.second(k), (1, 3), strict=True
        ):
            whole = self.region(k, side)
            remote(whole, whole, self.sems.at[k, 0], self.sems.at[k, arrived], tp=self.right).wait_recv()
            copy.start()

    def finish(self, k):
        for half, sent, arrived in ((0, 4, 5), (1, 6, 7)):
            part = self.half(k, self.far, half)
            remote(part, part, self.sems.at[k, sent], self.sems.at[k, arrived], tp=self.right).wait_recv()

    def drain(self, k):
        for copy in self.first(k) + self.second(k):
            copy.wait_send()


class Reduce:
    def __init__(self, piece, in_left, in_right, out_right, out_left, mid_left, mid_right, sems):
        self.piece, self.sems = piece, sems
        self.in_left, self.in_right = in_left, in_right
        self.out_right, self.out_left = out_right, out_left
        self.mid_left, self.mid_right = mid_left, mid_right
        self.here, self.right, self.left = ring(4)
        self.far = lax.rem(self.here + 2, 4)

    def first(self, k):
        return (
            remote(self.piece(k, self.far, 0), self.in_left.at[k], self.sems.at[k, 0], self.sems.at[k, 1], tp=self.right),
            remote(self.piece(k, self.far, 1), self.in_right.at[k], self.sems.at[k, 2], self.sems.at[k, 3], tp=self.left),
        )

    def second(self, k):
        return (
            remote(self.out_right.at[k], self.mid_left.at[k], self.sems.at[k, 4], self.sems.at[k, 5], tp=self.right),
            remote(self.out_left.at[k], self.mid_right.at[k], self.sems.at[k, 6], self.sems.at[k, 7], tp=self.left),
        )

    def start(self, k):
        for copy in self.first(k):
            copy.start()

    def middle(self, k):
        by_left, by_right = self.first(k)
        to_right, to_left = self.second(k)
        by_left.wait_recv()
        summed = self.piece(k, self.right, 0)[...].astype(F32) + self.in_left[k].astype(F32)
        self.out_right[k, 0] = summed.astype(BF)
        self.out_right[k, 1] = self.piece(k, self.right, 1)[...]
        to_right.start()
        by_right.wait_recv()
        summed = self.piece(k, self.left, 1)[...].astype(F32) + self.in_right[k].astype(F32)
        self.out_left[k, 1] = summed.astype(BF)
        self.out_left[k, 0] = self.piece(k, self.left, 0)[...]
        to_left.start()

    def finish(self, k):
        for copy in self.second(k):
            copy.wait_recv()
        return [
            self.piece(k, self.here, half)[...].astype(F32)
            + self.mid_left[k, half].astype(F32)
            + self.mid_right[k, half].astype(F32)
            for half in (0, 1)
        ]

    def drain(self, k):
        for copy in self.first(k) + self.second(k):
            copy.wait_send()


def reduce_scratch(groups, rows, lanes):
    return [pltpu.VMEM((groups, rows, lanes), BF)] * 2 + [
        pltpu.VMEM((groups, 2, rows, lanes), BF)
    ] * 4


def sems(*dims):
    return pltpu.SemaphoreType.DMA(dims)


def dispatch_body(batch_size, lanes, source, out, send, arrive, ring_sems):
    signals = greet(4, batch_size)
    me = lax.axis_index("exp")
    here = lax.axis_index("tp")
    part = batch_size // GROUPS
    mine = pl.ds(pl.multiple_of(here * lanes, 128), lanes)
    tail = pl.ds(4 * lanes, lanes)
    own = pl.ds(pl.multiple_of(me * 16, 16), 16)
    out[:, own, mine] = source[:, own, mine]
    out[:, own, tail] = source[:, own, tail]
    meet(signals)

    def arriving(k):
        return lax.rem(me // part + GROUPS - k, GROUPS) * (part * 16)

    def span(k, who, begin, rows, array=slice(None)):
        spot = pl.ds(pl.multiple_of(arriving(k) + begin, 16), rows)
        return out.at[array, spot, pl.ds(pl.multiple_of(who * lanes, 128), lanes)]

    gather = Gather(
        lambda k, who: span(k, who, 0, part * 16),
        lambda k, who, half: span(k, who, 0, part * 16, pl.ds(half, 1)),
        ring_sems,
    )

    def scatter(columns, send_sem, sem_of):
        for k in range(GROUPS):

            def step(j, carry):
                peer = lax.rem(me // part + k, GROUPS) * part + lax.rem(me + j, part)
                rows = pl.ds(pl.multiple_of(peer * 16, 16), 16)
                remote(source.at[:, rows, columns], out.at[:, own, columns], send_sem, sem_of(k), exp=peer).start()
                return carry

            lax.fori_loop(1 if k == 0 else 0, part, step, 0)

    scatter(mine, send.at[0], lambda k: arrive.at[k])
    scatter(tail, send.at[1], lambda k: arrive.at[GROUPS])
    for k in range(GROUPS):
        rows = (part - 1 if k == 0 else part) * 16
        block = span(k, here, 0, rows)
        remote(block, block, send.at[0], arrive.at[k], exp=me).wait_recv()
        gather.start(k)
        if k:
            gather.forward(k - 1)
    gather.forward(GROUPS - 1)
    whole = out.at[:, pl.ds(0, (batch_size - 1) * 16), tail]
    remote(whole, whole, send.at[1], arrive.at[GROUPS], exp=me).wait_recv()
    for k in range(GROUPS):
        gather.finish(k)
    remote(whole, whole, send.at[0], arrive.at[0], exp=me).wait_send()
    remote(whole, whole, send.at[1], arrive.at[0], exp=me).wait_send()
    for k in range(GROUPS):
        gather.drain(k)


def return_parts(batch_size, lanes, source, out, stage, buffers, send, arrive, sum_sems, ring_sems):
    me = lax.axis_index("exp")
    here = lax.axis_index("tp")
    part = batch_size // GROUPS
    mine = pl.ds(pl.multiple_of(here * lanes, 128), lanes)
    own = pl.ds(pl.multiple_of(me * 16, 16), 16)

    def leaving(k):
        return lax.rem(me // part + k, GROUPS) * (part * 16)

    def arriving(k):
        return lax.rem(me // part + GROUPS - k, GROUPS) * (part * 16)

    def span(ref, base, who, begin, rows):
        spot = pl.ds(pl.multiple_of(base + begin, 16), rows)
        return ref.at[spot, pl.ds(pl.multiple_of(who * lanes, 128), lanes)]

    half_rows = part * 8
    reduce = Reduce(
        lambda k, who, half: span(source, leaving(k), who, half * half_rows, half_rows),
        *buffers,
        sum_sems,
    )
    gather = Gather(
        lambda k, who: span(out, arriving(k), who, 0, part * 16),
        lambda k, who, half: span(out, arriving(k), who, half * half_rows, half_rows),
        ring_sems,
    )

    def scatter(k):
        first, second = reduce.finish(k)
        spot = pl.multiple_of(leaving(k), 16)
        stage[pl.ds(spot, half_rows), :] = first.astype(BF)
        stage[pl.ds(pl.multiple_of(spot + half_rows, 16), half_rows), :] = second.astype(BF)
        if k == 0:
            out[own, mine] = stage[own, :]

        def step(j, carry):
            peer = lax.rem(me // part + k, GROUPS) * part + lax.rem(me + j, part)
            rows = pl.ds(pl.multiple_of(peer * 16, 16), 16)
            remote(stage.at[rows, :], out.at[own, mine], send.at[0], arrive.at[k], exp=peer).start()
            return carry

        lax.fori_loop(1 if k == 0 else 0, part, step, 0)

    def collect(k):
        rows = (part - 1 if k == 0 else part) * 16
        block = span(out, arriving(k), here, 0, rows)
        remote(block, block, send.at[0], arrive.at[k], exp=me).wait_recv()
        gather.start(k)

    def drain():
        whole = stage.at[pl.ds(0, (batch_size - 1) * 16), :]
        remote(whole, whole, send.at[0], arrive.at[0], exp=me).wait_send()
        for k in range(GROUPS):
            reduce.drain(k)
            gather.drain(k)

    return reduce, gather, scatter, collect, drain


def return_body(batch_size, lanes, source, out, stage, *rest):
    buffers, (send, arrive, sum_sems, ring_sems) = rest[:6], rest[6:]
    signals = greet(4, batch_size)
    reduce, gather, scatter, collect, drain = return_parts(
        batch_size, lanes, source, out, stage, buffers, send, arrive, sum_sems, ring_sems
    )
    meet(signals)
    for k in range(GROUPS):
        reduce.start(k)
    for k in range(GROUPS):
        reduce.middle(k)
        if k:
            scatter(k - 1)
    scatter(GROUPS - 1)
    for k in range(GROUPS):
        collect(k)
        if k:
            gather.forward(k - 1)
    gather.forward(GROUPS - 1)
    for k in range(GROUPS):
        gather.finish(k)
    drain()


def return_scratch(batch_size, lanes):
    return [
        pltpu.VMEM((batch_size * 16, lanes), BF),
        *reduce_scratch(GROUPS, batch_size * 8 // GROUPS, lanes),
        sems(1),
        sems(GROUPS),
        sems(GROUPS, 8),
        sems(GROUPS, 8),
    ]


def final_body(
    batch_size, part_in, large, small, residual_grad, rows, gain,
    input_grad, query_grad, key_grad, value_grad, proj_grad, router_grad, gain_grad, first_grad,
    table_grad,
    summed, large_in, small_in, large_out, small_out, lines, *rest,
):
    buffers, (send, arrive, line_sems, sum_sems, ring_sems) = rest[:6], rest[6:]
    signals = greet(4, batch_size, opposite=True)
    me = lax.axis_index("exp")
    here, right, left = ring(4)
    tokens, width = part_in.shape
    chunk = tokens // 4
    groups = buffers[0].shape[0]
    half_rows = chunk // groups // 2
    tall, wide = large_in.shape[1:]
    across = width // wide
    small_across = small.shape[1] // 128

    def spot(ref, who, k, begin, count):
        first = who * chunk + k * (2 * half_rows) + begin
        return ref.at[pl.ds(pl.multiple_of(first, 16), count), :]

    reduce = Reduce(
        lambda k, who, half: spot(part_in, who, k, half * half_rows, half_rows), *buffers, sum_sems
    )
    gather = Gather(
        lambda k, who: spot(summed, who, k, 0, 2 * half_rows),
        lambda k, who, half: spot(summed, who, k, half * half_rows, half_rows),
        ring_sems,
    )

    def large_part(ref, who):
        down = pl.ds(pl.multiple_of(who // across * tall, 16), tall)
        return ref.at[down, pl.ds(pl.multiple_of(lax.rem(who, across) * wide, 128), wide)]

    def small_part(ref, who):
        down = pl.ds(pl.multiple_of(who // small_across * 16, 16), 16)
        return ref.at[down, pl.ds(pl.multiple_of(lax.rem(who, small_across) * 128, 128), 128)]

    meet(signals)
    for k in range(groups):
        reduce.start(k)

    def scatter(step, carry):
        peer = lax.rem(me + step, batch_size)
        remote(large_part(large, peer), large_in.at[step], send.at[0], arrive.at[0], exp=peer).start()
        remote(small_part(small, peer), small_in.at[step], send.at[1], arrive.at[1], exp=peer).start()
        return carry

    lax.fori_loop(1, batch_size, scatter, 0)
    large_in[0] = large_part(large, me)[...]
    small_in[0] = small_part(small, me)[...]
    for k in range(groups):
        reduce.middle(k)
    for k in range(groups):
        pieces = reduce.finish(k)
        for half in (0, 1):
            target = spot(summed, here, k, half * half_rows, half_rows)
            target[...] = pieces[half].astype(BF)
        gather.start(k)
    large_rest = large_in.at[pl.ds(1, batch_size - 1)]
    small_rest = small_in.at[pl.ds(1, batch_size - 1)]
    remote(large_rest, large_rest, send.at[0], arrive.at[0], exp=me).wait_recv()
    remote(small_rest, small_rest, send.at[1], arrive.at[1], exp=me).wait_recv()

    def add(step, carry):
        return carry[0] + large_in[step].astype(F32), carry[1] + small_in[step].astype(F32)

    zero = (jnp.zeros((tall, wide), F32), jnp.zeros((16, 128), F32))
    large_sum, small_sum = lax.fori_loop(0, batch_size, add, zero)
    large_part(large_out, me)[...] = large_sum.astype(BF)
    small_part(small_out, me)[...] = small_sum.astype(BF)

    def spread(step, carry):
        peer = lax.rem(me + step, batch_size)
        own = large_part(large_out, me)
        remote(own, own, send.at[2], arrive.at[2], exp=peer).start()
        own = small_part(small_out, me)
        remote(own, own, send.at[3], arrive.at[3], exp=peer).start()
        return carry

    lax.fori_loop(1, batch_size, spread, 0)
    for k in range(groups):
        gather.forward(k)
    for k in range(groups):
        gather.finish(k)
    inputs = rows[...].astype(F32)
    scale = inverse_rms(inputs)
    scaled = summed[...].astype(F32) * gain[...]
    middle = jnp.mean(scaled * inputs, axis=-1, keepdims=True)
    input_grad[...] = (
        residual_grad[...] + scale * scaled - inputs * (scale * scale * scale * middle)
    )
    remote(large_rest, large_rest, send.at[2], arrive.at[2], exp=me).wait_recv()
    remote(small_rest, small_rest, send.at[3], arrive.at[3], exp=me).wait_recv()
    line = small_out.at[pl.ds(32, 16), pl.ds(0, width)]
    others = (right, left, lax.rem(here + 2, 4))
    copies = [
        remote(line, lines.at[i], line_sems.at[i, 0], line_sems.at[i, 1], tp=side)
        for i, side in enumerate(others)
    ]
    for copy in copies:
        copy.start()
    high = query_grad.shape[0]
    for i, ref in enumerate((query_grad, key_grad, value_grad, proj_grad)):
        ref[...] = large_out[i * high : (i + 1) * high, :].astype(F32)
    router_grad[...] = small_out[0 : router_grad.shape[0], 0:width].astype(F32)
    gain_grad[...] = small_out[32:48, 0:width].astype(F32)[0:1]
    table_grad[...] = small_out[48:64, 0:128].astype(F32)[0:3, 0:32]
    for copy in copies:
        copy.wait_recv()
    total = small_out[32:48, 0:width].astype(F32)
    for i in range(3):
        total = total + lines[i].astype(F32)
    first_grad[...] = total[8:9]
    for copy in copies:
        copy.wait_send()
    for i, ref in enumerate((large_rest, small_rest, large_rest, small_rest)):
        remote(ref, ref, send.at[i], arrive.at[0], exp=me).wait_send()
    for k in range(groups):
        reduce.drain(k)
        gather.drain(k)


def head_mask(head, head_width, width):
    lane = lax.broadcasted_iota(jnp.int32, (1, width), 1)
    return jnp.where(lane // head_width == head, 1.0, 0.0)


def fill_bias(bias, buckets, table):
    heads, block, width = bias.shape
    padded = buckets.shape[1]
    number = lax.broadcasted_iota(jnp.int32, (table.shape[1], padded), 0)
    hot = jnp.where(buckets[...] == number, 1.0, 0.0)
    offsets = jnp.dot(
        table[...], hot, precision=lax.Precision.HIGHEST, preferred_element_type=F32
    )
    for head in range(heads):
        spread = jnp.broadcast_to(offsets[head : head + 1, :], (block, padded))
        rolled = pltpu.roll(spread, padded - (block - 1), 1, stride=1, stride_axis=0)
        bias[head] = rolled[:, :width]


def attend_body(
    head_width, rows, gain, query_w, key_w, value_w, proj, buckets, table,
    mixed, mixed_all, proj_all, normed, query, query_t, key, key_t, value_t, logsum,
    bias, value, ring_sems, proj_sems,
):
    heads = bias.shape[0]
    tokens = rows.shape[0]
    width = query.shape[1]
    blocks = tokens // BLOCK
    pairs = blocks // 2
    signals = greet(4, 0)
    here = lax.axis_index("tp")
    inputs = rows[...].astype(F32)
    low = (inputs * inverse_rms(inputs) * gain[...]).astype(BF)
    normed[...] = low
    proj_all[here] = proj[...]
    meet(signals)
    gather = Gather(
        lambda k, who: mixed_all.at[who, pl.ds(pl.multiple_of(k * BLOCK, BLOCK), BLOCK), :],
        lambda k, who, half: mixed_all.at[
            who, pl.ds(pl.multiple_of(k * BLOCK + half * (BLOCK // 2), 16), BLOCK // 2), :
        ],
        ring_sems,
    )
    half_rows = proj.shape[0] // 2
    weights_gather = Gather(
        lambda k, who: proj_all.at[who],
        lambda k, who, half: proj_all.at[who, pl.ds(half * half_rows, half_rows), :],
        proj_sems,
    )
    weights_gather.start(0)
    query[...] = cols_product(low, query_w[...]).astype(BF)
    key[...] = cols_product(low, key_w[...]).astype(BF)
    value[...] = cols_product(low, value_w[...]).astype(BF)
    query_t[...] = cols_product(query_w[...], low).astype(BF)
    key_t[...] = cols_product(key_w[...], low).astype(BF)
    value_t[...] = cols_product(value_w[...], low).astype(BF)
    fill_bias(bias, buckets, table)
    weights_gather.forward(0)

    def step(pair, carry):
        for side in (0, 1):
            block = pair + side * pairs
            first = pl.multiple_of(block * BLOCK, BLOCK)
            shift = pl.multiple_of((blocks - 1 - block) * BLOCK, BLOCK)
            query_rows = query[pl.ds(first, BLOCK), :]
            total = jnp.zeros((BLOCK, width), F32)
            for head in range(heads):
                mask = head_mask(head, head_width, width)
                scores = product(query_rows * mask.astype(BF), key_t[...])
                scores = scores + bias[head, :, pl.ds(shift, tokens)]
                highest = jnp.max(scores, axis=-1, keepdims=True)
                weights = jnp.exp(scores - highest)
                summed = jnp.sum(weights, axis=-1, keepdims=True)
                part = product(weights.astype(BF), value[...]) / summed
                total = total + part * mask
                logsum[pl.ds(first, BLOCK), head : head + 1] = highest + jnp.log(summed)
            spot = pl.ds(pl.multiple_of(pair * BLOCK, BLOCK), BLOCK)
            mixed[pl.ds(first, BLOCK), :] = total.astype(BF)
            mixed_all[here, spot, side * width : (side + 1) * width] = total.astype(BF)
        gather.start(pair)

        @pl.when(pair > 0)
        def _():
            gather.forward(pair - 1)

        return carry

    lax.fori_loop(0, pairs, step, 0)
    weights_gather.finish(0)
    gather.forward(pairs - 1)
    for k in range(pairs):
        gather.finish(k)
    weights_gather.drain(0)
    for k in range(pairs):
        gather.drain(k)


def pack_third(third, experts):
    half = third.shape[1] // 2
    split = third.reshape(experts, 8, 2 * half)
    split = jnp.concatenate([split[:, :, :half], split[:, :, half:]], axis=1)
    return split.reshape(experts * 16, half)


def unpack_third(tail, runs):
    half = tail.shape[1]
    split = tail.astype(F32).reshape(runs, 16, half)
    return jnp.concatenate([split[:, :8], split[:, 8:]], axis=2).reshape(runs * 8, 2 * half)


def slot_of_row(row, experts, capacity):
    body = 16 * experts
    first = (row // 16) * capacity + row % 16
    second = ((row - body) // 16) * capacity + 16 + (row - body) % 16
    third = ((row - 2 * body) // 8) * capacity + 32 + (row - 2 * body) % 8
    return jnp.where(row < body, first, jnp.where(row < 2 * body, second, third))


def route_body(
    capacity, rows, mixed, proj, gain, router_w, ids_row, cotangent,
    residual, hidden, probs, send, slots, gates,
):
    tokens, width = rows.shape
    experts = router_w.shape[0]
    body = 16 * experts
    half, here = mixed.shape[1], mixed.shape[2] // 2
    for side in (0, 1):
        spot = slice(side * half, (side + 1) * half)
        total = rows[spot, :].astype(F32)
        for i in range(mixed.shape[0]):
            total = total + product(mixed[i, :, side * here : (side + 1) * here], proj[i])
        residual[spot, :] = total
    res = residual[...]
    low = (res * inverse_rms(res) * gain[...]).astype(BF)
    hidden[...] = low
    logits = cols_product(low, router_w[...])
    shifted = jnp.exp(logits - jnp.max(logits, axis=-1, keepdims=True))
    chances = shifted / jnp.sum(shifted, axis=-1, keepdims=True)
    probs[...] = chances
    number = lax.broadcasted_iota(jnp.int32, (experts, tokens), 0)
    hot_t = ids_row[...] == number
    ones_t = jnp.where(hot_t, 1.0, 0.0)
    hot = ones_t.T > 0.5
    gate = jnp.sum(jnp.where(hot, chances, 0.0), axis=1, keepdims=True)
    gates[...] = gate
    across = lax.broadcasted_iota(jnp.int32, (tokens, tokens), 0)
    along = lax.broadcasted_iota(jnp.int32, (tokens, tokens), 1)
    lower = jnp.where(across >= along, 1.0, 0.0).astype(BF)
    upper = jnp.where(across <= along, 1.0, 0.0).astype(BF)
    counts = product(lower, jnp.where(hot, 1.0, 0.0).astype(BF))
    counts_t = product(ones_t.astype(BF), upper)
    position = jnp.sum(jnp.where(hot, counts - 1.0, 0.0), axis=1, keepdims=True)
    position_t = jnp.sum(jnp.where(hot_t, counts_t - 1.0, 0.0), axis=0, keepdims=True)
    expert = lax.broadcasted_iota(jnp.int32, (tokens, experts), 1)
    chosen = jnp.sum(jnp.where(hot, expert.astype(F32), 0.0), axis=1, keepdims=True)
    slots[...] = chosen.astype(jnp.int32) * capacity + position.astype(jnp.int32)
    slots_t = ids_row[...] * capacity + position_t.astype(jnp.int32)
    grads = (gate * cotangent[...].astype(F32)).astype(BF)

    def group(begin, count):
        number = slot_of_row(
            lax.broadcasted_iota(jnp.int32, (count, 1), 0) + begin, experts, capacity
        )
        return jnp.where(number == slots_t, 1.0, 0.0).astype(BF)

    for begin, count, lane in ((0, body, 0), (body, body, width)):
        place = group(begin, count)
        send[0, :, lane : lane + width] = product(place, low).astype(BF)
        send[1, :, lane : lane + width] = product(place, grads).astype(BF)
    place = group(2 * body, body // 2)
    send[0, :, 2 * width :] = pack_third(product(place, low), experts).astype(BF)
    send[1, :, 2 * width :] = pack_third(product(place, grads), experts).astype(BF)


def expert_body(
    packed, weight_in, weight_out,
    value, back, in_grad, out_grad, tail_rows, tail_grads,
):
    width = weight_in.shape[0]
    rows, grads = packed.at[0], packed.at[1]
    body = packed.shape[1]
    runs = body // 16
    tail_rows[...] = unpack_third(rows[:, 2 * width :], runs).astype(BF)
    tail_grads[...] = unpack_third(grads[:, 2 * width :], runs).astype(BF)
    in_grad[...] = jnp.zeros(in_grad.shape, F32)
    out_grad[...] = jnp.zeros(out_grad.shape, F32)

    def chunk(x, g):
        pre = product(x, weight_in[...])
        inner = jnp.tanh(gelu_root * (pre + gelu_cube * pre * pre * pre))
        act = (0.5 * pre * (1.0 + inner)).astype(BF)
        slope = 0.5 * (1.0 + inner) + 0.5 * pre * (1.0 - inner * inner) * (
            gelu_root * (1.0 + 3.0 * gelu_cube * pre * pre)
        )
        out = product(act, weight_out[...])
        dots = jnp.sum(out * g.astype(F32), axis=1, keepdims=True)
        out_grad[...] += rows_product(act, g)
        act_grad = cols_product(g, weight_out[...])
        pre_grad = (act_grad * slope).astype(BF)
        in_grad[...] += rows_product(x, pre_grad)
        rows_back = cols_product(pre_grad, weight_in[...])
        return out, dots, rows_back

    lane = lax.broadcasted_iota(jnp.int32, (1, 128), 1)
    part = 256
    for begin in range(0, body, part):
        spot = pl.ds(begin, part)
        marks = jnp.zeros((part, 128), F32)
        for side in (0, 1):
            lanes = slice(side * width, (side + 1) * width)
            out, dots, rows_back = chunk(rows[spot, lanes], grads[spot, lanes])
            value[spot, lanes] = out.astype(BF)
            back[spot, lanes] = rows_back.astype(BF)
            marks = marks + jnp.where(lane == side, dots, 0.0)
        back[spot, 2 * width + width // 2 :] = marks.astype(BF)
    out, dots, rows_back = chunk(tail_rows[...], tail_grads[...])
    value[:, 2 * width + width // 2 :] = jnp.zeros((body, 128), BF)
    value[:, 2 * width : 2 * width + width // 2] = pack_third(out, runs).astype(BF)
    back[:, 2 * width : 2 * width + width // 2] = pack_third(rows_back, runs).astype(BF)
    spread = jnp.where(lane == 2, dots, 0.0).reshape(runs, 8, 128)
    spread = jnp.concatenate([spread, jnp.zeros_like(spread)], axis=1).reshape(body, 128)
    marks = back[:, 2 * width + width // 2 :].astype(F32) + spread
    back[:, 2 * width + width // 2 :] = marks.astype(BF)


def place_of(slots, experts, capacity, rows):
    number = slot_of_row(lax.broadcasted_iota(jnp.int32, (1, rows), 1), experts, capacity)
    return jnp.where(slots == number, 1.0, 0.0).astype(BF)


def token_body(
    capacity, returned, back, slots, gates, residual, hidden, probs, gain, router_w,
    cotangent, mixed, proj,
    output, router_grad, gain_grad, residual_grad, proj_grad, mixed_grad, mixed_grad_t,
):
    tokens, width = residual.shape
    experts = router_w.shape[0]
    body = 16 * experts
    place = place_of(slots[...], experts, capacity, 5 * body // 2)

    def fetch(ref):
        picked = product(place[:, :body], ref[:, :width])
        picked = picked + product(place[:, body : 2 * body], ref[:, width : 2 * width])
        tail = unpack_third(ref[:, 2 * width : 2 * width + width // 2], experts).astype(BF)
        return picked + product(place[:, 2 * body :], tail)

    token_rows = fetch(returned)
    upstream = cotangent[...].astype(F32)
    res = residual[...]
    output[...] = (res + gates[...] * token_rows).astype(BF)
    marks = back[:, 2 * width + width // 2 :]
    lane = lax.broadcasted_iota(jnp.int32, (1, 128), 1)
    tail = marks.astype(F32).reshape(experts, 16, 128)[:, :8].reshape(experts * 8, 128).astype(BF)
    dots = jnp.where(lane == 0, product(place[:, :body], marks), 0.0)
    dots = dots + jnp.where(lane == 1, product(place[:, body : 2 * body], marks), 0.0)
    dots = dots + jnp.where(lane == 2, product(place[:, 2 * body :], tail), 0.0)
    weighted = jnp.sum(dots, axis=1, keepdims=True)
    hot = slots[...] // capacity == lax.broadcasted_iota(jnp.int32, (tokens, experts), 1)
    logit_grad = (jnp.where(hot, weighted, 0.0) - probs[...] * weighted).astype(BF)
    router_grad[...] = rows_product(logit_grad, hidden[...]).astype(BF)
    hidden_grad = fetch(back) + product(logit_grad, router_w[...])
    scale = inverse_rms(res)
    gain_grad[...] = jnp.sum(hidden_grad * res * scale, axis=0, keepdims=True).astype(BF)
    scaled = gain[...] * hidden_grad
    middle = jnp.mean(scaled * res, axis=-1, keepdims=True)
    total = upstream + scale * scaled - res * (scale * scale * scale * middle)
    low = total.astype(BF)
    residual_grad[...] = total
    proj_grad[...] = rows_product(mixed[...], low).astype(BF)
    mixed_grad[...] = cols_product(low, proj[...]).astype(BF)
    mixed_grad_t[...] = cols_product(proj[...], low).astype(BF)


def attend_back_body(
    head_width, normed, query, query_t, key, key_t, value_t, logsum, grad, grad_t,
    query_w, key_w, value_w, buckets, table, rows, proj_grad, router_grad, gain_grad,
    normed_part, large, small,
    bias, sums, query_back, key_acc, value_acc,
):
    heads = bias.shape[0]
    tokens, width = query.shape
    blocks = tokens // BLOCK
    fill_bias(bias, buckets, table)
    sums[...] = jnp.zeros(sums.shape, F32)
    key_acc[...] = jnp.zeros(key_acc.shape, F32)
    value_acc[...] = jnp.zeros(value_acc.shape, F32)

    def step(block, carry):
        first = pl.multiple_of(block * BLOCK, BLOCK)
        shift = pl.multiple_of((blocks - 1 - block) * BLOCK, BLOCK)
        query_rows = query[pl.ds(first, BLOCK), :]
        grad_rows = grad[pl.ds(first, BLOCK), :]
        total = jnp.zeros((BLOCK, width), F32)
        for head in range(heads):
            mask = head_mask(head, head_width, width)
            span = slice(head * head_width, (head + 1) * head_width)
            scores = product(query_rows * mask.astype(BF), key_t[...])
            scores = scores + bias[head, :, pl.ds(shift, tokens)]
            probs = jnp.exp(scores - logsum[pl.ds(first, BLOCK), head : head + 1])
            prob_grad = product(grad_rows * mask.astype(BF), value_t[...])
            middle = jnp.sum(probs * prob_grad, axis=-1, keepdims=True)
            score_grad = probs * (prob_grad - middle)
            low = score_grad.astype(BF)
            sums[head, :, pl.ds(shift, tokens)] += score_grad
            total = total + product(low, key[...]) * mask
            key_acc[span, :] += product(query_t[span, pl.ds(first, BLOCK)], low)
            value_acc[span, :] += product(grad_t[span, pl.ds(first, BLOCK)], probs.astype(BF))
        query_back[pl.ds(first, BLOCK), :] = total.astype(BF)
        return carry

    lax.fori_loop(0, blocks, step, 0)
    backs = [query_back[...], key_acc[...].T.astype(BF), value_acc[...].T.astype(BF)]
    backs_t = [query_back[...].astype(F32).T.astype(BF)]
    backs_t += [key_acc[...].astype(BF), value_acc[...].astype(BF)]
    part = product(backs[0], query_w[...])
    part = part + product(backs[1], key_w[...]) + product(backs[2], value_w[...])
    normed_part[...] = part.astype(BF)
    for i in range(3):
        large[i * width : (i + 1) * width, :] = product(backs_t[i], normed[...]).astype(BF)
    large[3 * width :, :] = proj_grad[...]
    full = rows.shape[1]
    inputs = rows[...].astype(F32)
    line = jnp.sum(part * inputs * inverse_rms(inputs), axis=0, keepdims=True)
    small[...] = jnp.zeros(small.shape, BF)
    small[0 : router_grad.shape[0], 0:full] = router_grad[...]
    row = lax.broadcasted_iota(jnp.int32, (16, 1), 0)
    pair = jnp.where(row == 0, gain_grad[...].astype(F32), jnp.where(row == 8, line, 0.0))
    small[32:48, 0:full] = pair.astype(BF)

    padded = buckets.shape[1]
    lines = []
    for head in range(heads):
        wide = jnp.concatenate(
            [sums[head], jnp.zeros((BLOCK, padded - sums.shape[2]), F32)], axis=1
        )
        gathered = jnp.zeros((8, padded), F32)
        for part in range(BLOCK // 8):
            piece = wide[part * 8 : part * 8 + 8, :]
            gathered = gathered + pltpu.roll(piece, (BLOCK - 1 - part * 8) % padded, 1)
        line = jnp.zeros((1, padded), F32)
        for row in range(8):
            line = line + pltpu.roll(gathered, (padded - row) % padded, 1)[row : row + 1, :]
        lines.append(line)
    number = lax.broadcasted_iota(jnp.int32, (table.shape[1], padded), 0)
    hot = jnp.where(buckets[...] == number, 1.0, 0.0)
    stacked = jnp.concatenate(lines + [jnp.zeros((16 - heads, padded), F32)], axis=0)
    sums_of = lax.dot_general(
        stacked,
        hot,
        (((1,), (1,)), ((), ())),
        precision=lax.Precision.HIGHEST,
        preferred_element_type=F32,
    )
    blank = jnp.zeros((16, 128 - table.shape[1]), F32)
    small[48:64, 0:128] = jnp.concatenate([sums_of, blank], axis=1).astype(BF)


def per_device(
    layer_in, expert_ids, rel_buckets, first_gain, query_weight, key_weight, value_weight,
    proj_weight, rel_table, second_gain, router_weight, expert_in, expert_out, cotangent,
):
    tokens, width = layer_in.shape
    heads = rel_table.shape[1]
    here = query_weight.shape[1]
    head_width = here // heads
    experts = router_weight.shape[1]
    capacity = 5 * tokens // (4 * experts)
    body = 16 * experts
    packed = 2 * width + width // 2
    quarter = width // 2
    span = 2 * tokens - BLOCK
    ring_size = width // here
    gain_one = first_gain[None, :]
    gain_two = second_gain[None, :]
    buckets = jnp.pad(rel_buckets, (0, 1), constant_values=-1)[None, :]
    weights = (query_weight.T, key_weight.T, value_weight.T)
    table = rel_table.T
    router = router_weight.T

    mixed, mixed_all, proj_all, normed, query, query_t, key, key_t, value_t, logsum = call(
        functools.partial(attend_body, head_width),
        "attend",
        [
            ((tokens, here), BF),
            ((ring_size, tokens // 2, 2 * here), BF),
            ((ring_size, here, width), BF),
            ((tokens, width), BF),
            ((tokens, here), BF),
            ((here, tokens), BF),
            ((tokens, here), BF),
            ((here, tokens), BF),
            ((here, tokens), BF),
            ((tokens, 128), F32),
        ],
        [
            pltpu.VMEM((heads, BLOCK, span), F32),
            pltpu.VMEM((tokens, here), BF),
            sems(tokens // BLOCK // 2, 8),
            sems(1, 8),
        ],
        layer_in, gain_one, *weights, proj_weight, buckets, table,
        number=1,
    )
    residual, hidden, probs, leaving, slots, gates = call(
        functools.partial(route_body, capacity),
        "route",
        [
            ((tokens, width), F32),
            ((tokens, width), BF),
            ((tokens, experts), F32),
            ((2, body, packed), BF),
            ((tokens, 1), jnp.int32),
            ((tokens, 1), F32),
        ],
        [],
        layer_in, mixed_all, proj_all, gain_two, router, expert_ids.reshape(1, tokens), cotangent,
    )
    (arrived,) = call(
        functools.partial(dispatch_body, experts, quarter),
        "dispatch",
        [((2, body, packed), BF)],
        [sems(2), sems(GROUPS + 1), sems(GROUPS, 8)],
        leaving,
        number=2,
    )
    value, back, in_grad, out_grad = call(
        expert_body,
        "expert",
        [
            ((body, packed + 128), BF),
            ((body, packed + 128), BF),
            ((width, expert_in.shape[2]), F32),
            ((expert_out.shape[1], width), F32),
        ],
        [pltpu.VMEM((body // 2, width), BF)] * 2,
        arrived, expert_in[0], expert_out[0],
    )

    def give_back(array, number):
        return call(
            functools.partial(return_body, experts, (packed + 128) // 4),
            "give_back",
            [((body, packed + 128), BF)],
            return_scratch(experts, (packed + 128) // 4),
            array,
            number=number,
        )[0]

    (
        output, router_grad, second_gain_grad, residual_grad, proj_grad, mixed_grad, mixed_grad_t
    ) = call(
        functools.partial(token_body, capacity),
        "token",
        [
            ((tokens, width), BF),
            ((experts, width), BF),
            ((1, width), BF),
            ((tokens, width), F32),
            ((here, width), BF),
            ((tokens, here), BF),
            ((here, tokens), BF),
        ],
        [],
        give_back(value, 3), give_back(back, 3), slots, gates, residual, hidden, probs, gain_two,
        router, cotangent, mixed, proj_weight,
    )
    normed_part, large, small = call(
        functools.partial(attend_back_body, head_width),
        "attend_back",
        [((tokens, width), BF), ((4 * here, width), BF), ((64, 1024), BF)],
        [
            pltpu.VMEM((heads, BLOCK, span), F32),
            pltpu.VMEM((heads, BLOCK, span), F32),
            pltpu.VMEM((tokens, here), BF),
            pltpu.VMEM((here, tokens), F32),
            pltpu.VMEM((here, tokens), F32),
        ],
        normed, query, query_t, key, key_t, value_t, logsum, mixed_grad, mixed_grad_t,
        *weights, buckets, table, layer_in, proj_grad, router_grad, second_gain_grad,
    )
    tall, wide = 2 * 4 * here // experts, width // 2
    (
        input_grad, query_grad, key_grad, value_grad, proj_total, router_total, gain_total,
        first_total, table_total,
    ) = call(
        functools.partial(final_body, experts),
        "final",
        [
            ((tokens, width), F32),
            ((here, width), F32),
            ((here, width), F32),
            ((here, width), F32),
            ((here, width), F32),
            ((experts, width), F32),
            ((1, width), F32),
            ((1, width), F32),
            (table.shape, F32),
        ],
        [
            pltpu.VMEM((tokens, width), BF),
            pltpu.VMEM((experts, tall, wide), BF),
            pltpu.VMEM((experts, 16, 128), BF),
            pltpu.VMEM((4 * here, width), BF),
            pltpu.VMEM((64, 1024), BF),
            pltpu.VMEM((3, 16, width), BF),
            *reduce_scratch(4, tokens // 32, width),
            sems(4),
            sems(4),
            sems(3, 2),
            sems(4, 8),
            sems(4, 8),
        ],
        normed_part, large, small, residual_grad, layer_in, gain_one,
        number=4,
    )
    return (
        output,
        input_grad,
        first_total[0],
        query_grad.T,
        key_grad.T,
        value_grad.T,
        proj_total,
        table_total.T,
        gain_total[0],
        router_total.T,
        in_grad[None],
        out_grad[None],
    )


def solution(mesh):
    return jax.shard_map(
        per_device,
        mesh=mesh,
        in_specs=(
            P("exp", None),
            P("exp", None),
            P(),
            P(),
            P(None, "tp"),
            P(None, "tp"),
            P(None, "tp"),
            P("tp", None),
            P(None, "tp"),
            P(),
            P(),
            P("exp", None, "tp"),
            P("exp", "tp", None),
            P("exp", None),
        ),
        out_specs=(
            P("exp", None),
            P("exp", None),
            P(),
            P(None, "tp"),
            P(None, "tp"),
            P(None, "tp"),
            P("tp", None),
            P(None, "tp"),
            P(),
            P(),
            P("exp", None, "tp"),
            P("exp", "tp", None),
        ),
        check_vma=False,
    )
```

```python
import functools

import jax
import jax.numpy as jnp
from jax import lax
from jax.experimental import pallas as pl
from jax.experimental.pallas import tpu as pltpu
from jax.sharding import PartitionSpec as P

epsilon = 1e-06
gelu_root = 0.7978845608028654
gelu_cube = 0.044715
BF = jnp.bfloat16
F32 = jnp.float32
BLOCK = 128
MIB = 1024 * 1024
GROUPS = 4
MESH = pl.DeviceIdType.MESH


def product(left, right):
    return jnp.dot(left, right, preferred_element_type=F32)


def rows_product(left, right):
    return lax.dot_general(left, right, (((0,), (0,)), ((), ())), preferred_element_type=F32)


def cols_product(left, right):
    return lax.dot_general(left, right, (((1,), (1,)), ((), ())), preferred_element_type=F32)


def inverse_rms(values):
    return lax.rsqrt(jnp.mean(values * values, axis=-1, keepdims=True) + epsilon)


def call(body, name, outs, scratch, *operands, mib=48, number=None):
    vmem = pl.BlockSpec(memory_space=pltpu.VMEM)
    extra = {} if number is None else {"collective_id": number, "has_side_effects": True}
    return pl.pallas_call(
        body,
        name=name,
        out_shape=[jax.ShapeDtypeStruct(shape, dtype) for shape, dtype in outs],
        in_specs=[vmem] * len(operands),
        out_specs=[vmem] * len(outs),
        scratch_shapes=scratch,
        compiler_params=pltpu.CompilerParams(vmem_limit_bytes=mib * MIB, **extra),
    )(*operands)


def remote(source, target, send, receive, **where):
    return pltpu.make_async_remote_copy(
        src_ref=source,
        dst_ref=target,
        send_sem=send,
        recv_sem=receive,
        device_id=where,
        device_id_type=MESH,
    )


def ring(ring_size):
    here = lax.axis_index("tp")
    return here, lax.rem(here + 1, ring_size), lax.rem(here + ring_size - 1, ring_size)


def greet(ring_size, batch_size, opposite=False, same_core=False):
    barrier = pltpu.get_barrier_semaphore()
    here, right, left = ring(ring_size)
    for side in (right, left):
        pl.semaphore_signal(barrier, inc=1, device_id={"tp": side}, device_id_type=MESH)
    if opposite:
        side = lax.rem(here + 2, ring_size)
        pl.semaphore_signal(barrier, inc=1, device_id={"tp": side}, device_id_type=MESH)
    if not batch_size:
        return 2 + int(opposite)
    me = lax.axis_index("exp")
    stride = 2 if same_core else 1
    peers = batch_size // stride

    def hello(step, carry):
        peer = lax.rem(me + step * stride, batch_size)
        pl.semaphore_signal(barrier, inc=1, device_id={"exp": peer}, device_id_type=MESH)
        return carry

    lax.fori_loop(1, peers, hello, 0)
    if same_core:
        sibling = me + 1 - 2 * lax.rem(me, 2)
        pl.semaphore_signal(barrier, inc=1, device_id={"exp": sibling}, device_id_type=MESH)
    return 2 + int(opposite) + peers - 1 + int(same_core)


def meet(signals):
    pl.semaphore_wait(pltpu.get_barrier_semaphore(), signals)


class Gather:
    def __init__(self, region, half, sems):
        self.region, self.half, self.sems = region, half, sems
        self.here, self.right, self.left = ring(4)
        self.far = lax.rem(self.here + 2, 4)

    def first(self, k):
        own = self.region(k, self.here)
        return (
            remote(own, own, self.sems.at[k, 0], self.sems.at[k, 1], tp=self.right),
            remote(own, own, self.sems.at[k, 2], self.sems.at[k, 3], tp=self.left),
        )

    def second(self, k):
        low, high = self.half(k, self.left, 0), self.half(k, self.right, 1)
        return (
            remote(low, low, self.sems.at[k, 4], self.sems.at[k, 5], tp=self.right),
            remote(high, high, self.sems.at[k, 6], self.sems.at[k, 7], tp=self.left),
        )

    def start(self, k):
        for copy in self.first(k):
            copy.start()

    def forward(self, k):
        for side, copy, arrived in zip(
            (self.left, self.right), self.second(k), (1, 3), strict=True
        ):
            whole = self.region(k, side)
            remote(whole, whole, self.sems.at[k, 0], self.sems.at[k, arrived], tp=self.right).wait_recv()
            copy.start()

    def finish(self, k):
        for half, sent, arrived in ((0, 4, 5), (1, 6, 7)):
            part = self.half(k, self.far, half)
            remote(part, part, self.sems.at[k, sent], self.sems.at[k, arrived], tp=self.right).wait_recv()

    def drain(self, k):
        for copy in self.first(k) + self.second(k):
            copy.wait_send()


class Reduce:
    def __init__(self, piece, in_left, in_right, out_right, out_left, mid_left, mid_right, sems):
        self.piece, self.sems = piece, sems
        self.in_left, self.in_right = in_left, in_right
        self.out_right, self.out_left = out_right, out_left
        self.mid_left, self.mid_right = mid_left, mid_right
        self.here, self.right, self.left = ring(4)
        self.far = lax.rem(self.here + 2, 4)

    def first(self, k):
        return (
            remote(self.piece(k, self.far, 0), self.in_left.at[k], self.sems.at[k, 0], self.sems.at[k, 1], tp=self.right),
            remote(self.piece(k, self.far, 1), self.in_right.at[k], self.sems.at[k, 2], self.sems.at[k, 3], tp=self.left),
        )

    def second(self, k):
        return (
            remote(self.out_right.at[k], self.mid_left.at[k], self.sems.at[k, 4], self.sems.at[k, 5], tp=self.right),
            remote(self.out_left.at[k], self.mid_right.at[k], self.sems.at[k, 6], self.sems.at[k, 7], tp=self.left),
        )

    def start(self, k):
        for copy in self.first(k):
            copy.start()

    def middle(self, k):
        by_left, by_right = self.first(k)
        to_right, to_left = self.second(k)
        by_left.wait_recv()
        summed = self.piece(k, self.right, 0)[...].astype(F32) + self.in_left[k].astype(F32)
        self.out_right[k, 0] = summed.astype(BF)
        self.out_right[k, 1] = self.piece(k, self.right, 1)[...]
        to_right.start()
        by_right.wait_recv()
        summed = self.piece(k, self.left, 1)[...].astype(F32) + self.in_right[k].astype(F32)
        self.out_left[k, 1] = summed.astype(BF)
        self.out_left[k, 0] = self.piece(k, self.left, 0)[...]
        to_left.start()

    def finish(self, k):
        for copy in self.second(k):
            copy.wait_recv()
        return [
            self.piece(k, self.here, half)[...].astype(F32)
            + self.mid_left[k, half].astype(F32)
            + self.mid_right[k, half].astype(F32)
            for half in (0, 1)
        ]

    def drain(self, k):
        for copy in self.first(k) + self.second(k):
            copy.wait_send()


def reduce_scratch(groups, rows, lanes):
    return [pltpu.VMEM((groups, rows, lanes), BF)] * 2 + [
        pltpu.VMEM((groups, 2, rows, lanes), BF)
    ] * 4


def sems(*dims):
    return pltpu.SemaphoreType.DMA(dims)


def dispatch_body(batch_size, lanes, source, out, send, arrive, ring_sems):
    signals = greet(4, batch_size)
    me = lax.axis_index("exp")
    here = lax.axis_index("tp")
    part = batch_size // GROUPS
    mine = pl.ds(pl.multiple_of(here * lanes, 128), lanes)
    tail = pl.ds(4 * lanes, lanes)
    own = pl.ds(pl.multiple_of(me * 16, 16), 16)
    out[:, own, mine] = source[:, own, mine]
    out[:, own, tail] = source[:, own, tail]
    meet(signals)

    def arriving(k):
        return lax.rem(me // part + GROUPS - k, GROUPS) * (part * 16)

    def span(k, who, begin, rows, array=slice(None)):
        spot = pl.ds(pl.multiple_of(arriving(k) + begin, 16), rows)
        return out.at[array, spot, pl.ds(pl.multiple_of(who * lanes, 128), lanes)]

    gather = Gather(
        lambda k, who: span(k, who, 0, part * 16),
        lambda k, who, half: span(k, who, 0, part * 16, pl.ds(half, 1)),
        ring_sems,
    )

    def scatter(columns, send_sem, sem_of):
        for k in range(GROUPS):

            def step(j, carry):
                peer = lax.rem(me // part + k, GROUPS) * part + lax.rem(me + j, part)
                rows = pl.ds(pl.multiple_of(peer * 16, 16), 16)
                remote(source.at[:, rows, columns], out.at[:, own, columns], send_sem, sem_of(k), exp=peer).start()
                return carry

            lax.fori_loop(1 if k == 0 else 0, part, step, 0)

    scatter(mine, send.at[0], lambda k: arrive.at[k])
    scatter(tail, send.at[1], lambda k: arrive.at[GROUPS])
    for k in range(GROUPS):
        rows = (part - 1 if k == 0 else part) * 16
        block = span(k, here, 0, rows)
        remote(block, block, send.at[0], arrive.at[k], exp=me).wait_recv()
        gather.start(k)
        if k:
            gather.forward(k - 1)
    gather.forward(GROUPS - 1)
    whole = out.at[:, pl.ds(0, (batch_size - 1) * 16), tail]
    remote(whole, whole, send.at[1], arrive.at[GROUPS], exp=me).wait_recv()
    for k in range(GROUPS):
        gather.finish(k)
    remote(whole, whole, send.at[0], arrive.at[0], exp=me).wait_send()
    remote(whole, whole, send.at[1], arrive.at[0], exp=me).wait_send()
    for k in range(GROUPS):
        gather.drain(k)


def return_parts(batch_size, lanes, source, out, stage, buffers, send, arrive, sum_sems, ring_sems):
    me = lax.axis_index("exp")
    here = lax.axis_index("tp")
    part = batch_size // GROUPS
    mine = pl.ds(pl.multiple_of(here * lanes, 128), lanes)
    own = pl.ds(pl.multiple_of(me * 16, 16), 16)

    def leaving(k):
        return lax.rem(me // part + k, GROUPS) * (part * 16)

    def arriving(k):
        return lax.rem(me // part + GROUPS - k, GROUPS) * (part * 16)

    def span(ref, base, who, begin, rows):
        spot = pl.ds(pl.multiple_of(base + begin, 16), rows)
        return ref.at[spot, pl.ds(pl.multiple_of(who * lanes, 128), lanes)]

    half_rows = part * 8
    reduce = Reduce(
        lambda k, who, half: span(source, leaving(k), who, half * half_rows, half_rows),
        *buffers,
        sum_sems,
    )
    gather = Gather(
        lambda k, who: span(out, arriving(k), who, 0, part * 16),
        lambda k, who, half: span(out, arriving(k), who, half * half_rows, half_rows),
        ring_sems,
    )

    def scatter(k):
        first, second = reduce.finish(k)
        spot = pl.multiple_of(leaving(k), 16)
        stage[pl.ds(spot, half_rows), :] = first.astype(BF)
        stage[pl.ds(pl.multiple_of(spot + half_rows, 16), half_rows), :] = second.astype(BF)
        if k == 0:
            out[own, mine] = stage[own, :]

        def step(j, carry):
            peer = lax.rem(me // part + k, GROUPS) * part + lax.rem(me + j, part)
            rows = pl.ds(pl.multiple_of(peer * 16, 16), 16)
            remote(stage.at[rows, :], out.at[own, mine], send.at[0], arrive.at[k], exp=peer).start()
            return carry

        lax.fori_loop(1 if k == 0 else 0, part, step, 0)

    def collect(k):
        rows = (part - 1 if k == 0 else part) * 16
        block = span(out, arriving(k), here, 0, rows)
        remote(block, block, send.at[0], arrive.at[k], exp=me).wait_recv()
        gather.start(k)

    def drain():
        whole = stage.at[pl.ds(0, (batch_size - 1) * 16), :]
        remote(whole, whole, send.at[0], arrive.at[0], exp=me).wait_send()
        for k in range(GROUPS):
            reduce.drain(k)
            gather.drain(k)

    return reduce, gather, scatter, collect, drain


def return_body(batch_size, lanes, source, out, stage, *rest):
    buffers, (send, arrive, sum_sems, ring_sems) = rest[:6], rest[6:]
    signals = greet(4, batch_size)
    reduce, gather, scatter, collect, drain = return_parts(
        batch_size, lanes, source, out, stage, buffers, send, arrive, sum_sems, ring_sems
    )
    meet(signals)
    for k in range(GROUPS):
        reduce.start(k)
    for k in range(GROUPS):
        reduce.middle(k)
        if k:
            scatter(k - 1)
    scatter(GROUPS - 1)
    for k in range(GROUPS):
        collect(k)
        if k:
            gather.forward(k - 1)
    gather.forward(GROUPS - 1)
    for k in range(GROUPS):
        gather.finish(k)
    drain()


def return_scratch(batch_size, lanes):
    return [
        pltpu.VMEM((batch_size * 16, lanes), BF),
        *reduce_scratch(GROUPS, batch_size * 8 // GROUPS, lanes),
        sems(1),
        sems(GROUPS),
        sems(GROUPS, 8),
        sems(GROUPS, 8),
    ]


def final_body(
    batch_size, capacity, part_in, large, small, returned, slots, gates, residual,
    summed, large_out, small_out, lines, output,
    large_side, small_side, large_in, small_in, *rest,
):
    buffers, (send, arrive, line_sems, sum_sems, ring_sems) = rest[:6], rest[6:]
    signals = greet(4, batch_size, opposite=True, same_core=True)
    me = lax.axis_index("exp")
    core = lax.rem(me, 2)
    sibling = me + 1 - 2 * core
    here, right, left = ring(4)
    tokens, width = part_in.shape
    chunk = tokens // 4
    groups = buffers[0].shape[0]
    half_rows = chunk // groups // 2
    peers, tall, wide = large_in.shape
    half_lanes = small.shape[1] // 2
    small_across = half_lanes // 128

    def spot(ref, who, k, begin, count):
        first = who * chunk + k * (2 * half_rows) + begin
        return ref.at[pl.ds(pl.multiple_of(first, 16), count), :]

    reduce = Reduce(
        lambda k, who, half: spot(part_in, who, k, half * half_rows, half_rows), *buffers, sum_sems
    )
    gather = Gather(
        lambda k, who: spot(summed, who, k, 0, 2 * half_rows),
        lambda k, who, half: spot(summed, who, k, half * half_rows, half_rows),
        ring_sems,
    )

    def large_half(ref, side):
        return ref.at[:, pl.ds(pl.multiple_of(side * wide, 128), wide)]

    def small_half(ref, side):
        return ref.at[:, pl.ds(pl.multiple_of(side * half_lanes, 128), half_lanes)]

    def large_rows(ref, who):
        return ref.at[pl.ds(pl.multiple_of(who * tall, 16), tall), :]

    def small_rows(ref, who):
        down = pl.ds(pl.multiple_of(who // small_across * 16, 16), 16)
        return ref.at[down, pl.ds(pl.multiple_of(lax.rem(who, small_across) * 128, 128), 128)]

    def large_final(who):
        down = pl.ds(pl.multiple_of(who * tall, 16), tall)
        return large_out.at[down, pl.ds(pl.multiple_of(core * wide, 128), wide)]

    def small_final(who):
        down = pl.ds(pl.multiple_of(who // small_across * 16, 16), 16)
        lane = core * half_lanes + lax.rem(who, small_across) * 128
        return small_out.at[down, pl.ds(pl.multiple_of(lane, 128), 128)]

    meet(signals)
    pair = [
        remote(large_half(large, 1 - core), large_side, send.at[0], arrive.at[0], exp=sibling),
        remote(small_half(small, 1 - core), small_side, send.at[1], arrive.at[1], exp=sibling),
    ]
    for copy in pair:
        copy.start()
    for k in range(groups):
        reduce.start(k)
    for copy in pair:
        copy.wait_recv()
    both = large_side[...].astype(F32) + large_half(large, core)[...].astype(F32)
    large_side[...] = both.astype(BF)
    both = small_side[...].astype(F32) + small_half(small, core)[...].astype(F32)
    small_side[...] = both.astype(BF)
    mine = me // 2

    def scatter(step, carry):
        peer = lax.rem(mine + step, peers)
        to = peer * 2 + core
        remote(large_rows(large_side, peer), large_in.at[step], send.at[2], arrive.at[2], exp=to).start()
        remote(small_rows(small_side, peer), small_in.at[step], send.at[3], arrive.at[3], exp=to).start()
        return carry

    lax.fori_loop(1, peers, scatter, 0)
    large_in[0] = large_rows(large_side, mine)[...]
    small_in[0] = small_rows(small_side, mine)[...]
    for k in range(groups):
        reduce.middle(k)

    experts = batch_size
    body = 16 * experts
    place = place_of(slots[...], experts, capacity, 5 * body // 2)
    token_rows = fetch(place, returned, width, experts)
    output[...] = (residual[...] + gates[...] * token_rows).astype(BF)

    large_rest = large_in.at[pl.ds(1, peers - 1)]
    small_rest = small_in.at[pl.ds(1, peers - 1)]
    remote(large_rest, large_rest, send.at[2], arrive.at[2], exp=me).wait_recv()
    remote(small_rest, small_rest, send.at[3], arrive.at[3], exp=me).wait_recv()

    def add(step, carry):
        return carry[0] + large_in[step].astype(F32), carry[1] + small_in[step].astype(F32)

    zero = (jnp.zeros((tall, wide), F32), jnp.zeros((16, 128), F32))
    large_sum, small_sum = lax.fori_loop(0, peers, add, zero)
    large_final(mine)[...] = large_sum.astype(BF)
    small_final(mine)[...] = small_sum.astype(BF)

    def spread(step, carry):
        to = lax.rem(mine + step, peers) * 2 + core
        own = large_final(mine)
        remote(own, own, send.at[4], arrive.at[4], exp=to).start()
        own = small_final(mine)
        remote(own, own, send.at[5], arrive.at[5], exp=to).start()
        return carry

    lax.fori_loop(1, peers, spread, 0)
    for k in range(groups):
        pieces = reduce.finish(k)
        for half in (0, 1):
            target = spot(summed, here, k, half * half_rows, half_rows)
            target[...] = pieces[half].astype(BF)
        gather.start(k)
    remote(large_rest, large_rest, send.at[4], arrive.at[4], exp=me).wait_recv()
    remote(small_rest, small_rest, send.at[5], arrive.at[5], exp=me).wait_recv()
    back = []
    for i, half in ((6, large_half(large_out, core)), (7, small_half(small_out, core))):
        back.append(remote(half, half, send.at[i], arrive.at[i], exp=sibling))
    for copy in back:
        copy.start()
    for k in range(groups):
        gather.forward(k)
    for i, half in ((6, large_half(large_out, 1 - core)), (7, small_half(small_out, 1 - core))):
        remote(half, half, send.at[i], arrive.at[i], exp=sibling).wait_recv()
    line = small_out.at[pl.ds(32, 16), :]
    others = (right, left, lax.rem(here + 2, 4))
    copies = [
        remote(line, lines.at[i], line_sems.at[i, 0], line_sems.at[i, 1], tp=side)
        for i, side in enumerate(others)
    ]
    for copy in copies:
        copy.start()
    for k in range(groups):
        gather.finish(k)
    for copy in copies:
        copy.wait_recv()
    for copy in copies + pair + back:
        copy.wait_send()
    for i, ref in ((2, large_rest), (3, small_rest), (4, large_rest), (5, small_rest)):
        remote(ref, ref, send.at[i], arrive.at[0], exp=me).wait_send()
    for k in range(groups):
        reduce.drain(k)
        gather.drain(k)


def finish_body(
    summed, rows, residual_grad, gain, large, small, lines,
    input_grad, query_grad, key_grad, value_grad, proj_grad, router_grad, gain_grad, first_grad,
    table_grad,
):
    inputs = rows[...].astype(F32)
    scale = inverse_rms(inputs)
    scaled = summed[...].astype(F32) * gain[...]
    middle = jnp.mean(scaled * inputs, axis=-1, keepdims=True)
    input_grad[...] = (
        residual_grad[...] + scale * scaled - inputs * (scale * scale * scale * middle)
    )

    @pl.when(pl.program_id(0) == 0)
    def _():
        high, width = query_grad.shape
        for i, ref in enumerate((query_grad, key_grad, value_grad, proj_grad)):
            ref[...] = large[i * high : (i + 1) * high, :].astype(F32)
        router_grad[...] = small[0 : router_grad.shape[0], 0:width].astype(F32)
        total = small[32:48, 0:width].astype(F32)
        gain_grad[...] = total[0:1]
        table_grad[...] = small[48:64, 0:128].astype(F32)[0:3, 0:32]
        for i in range(3):
            total = total + lines[i][:, 0:width].astype(F32)
        first_grad[...] = total[8:9]


def head_mask(head, head_width, width):
    lane = lax.broadcasted_iota(jnp.int32, (1, width), 1)
    return jnp.where(lane // head_width == head, 1.0, 0.0)


def fill_bias(bias, buckets, table):
    heads, block, width = bias.shape
    padded = buckets.shape[1]
    number = lax.broadcasted_iota(jnp.int32, (table.shape[1], padded), 0)
    hot = jnp.where(buckets[...] == number, 1.0, 0.0)
    offsets = jnp.dot(
        table[...], hot, precision=lax.Precision.HIGHEST, preferred_element_type=F32
    )
    for head in range(heads):
        spread = jnp.broadcast_to(offsets[head : head + 1, :], (block, padded))
        rolled = pltpu.roll(spread, padded - (block - 1), 1, stride=1, stride_axis=0)
        bias[head] = rolled[:, :width]


def attend_body(
    head_width, rows, gain, query_w, key_w, value_w, proj, buckets, table,
    mixed, mixed_all, proj_all, normed, query, query_t, key, key_t, value_t, logsum,
    bias, value, ring_sems, proj_sems,
):
    heads = bias.shape[0]
    tokens = rows.shape[0]
    width = query.shape[1]
    blocks = tokens // BLOCK
    pairs = blocks // 2
    signals = greet(4, 0)
    here = lax.axis_index("tp")
    inputs = rows[...].astype(F32)
    low = (inputs * inverse_rms(inputs) * gain[...]).astype(BF)
    normed[...] = low
    proj_all[here] = proj[...]
    meet(signals)
    gather = Gather(
        lambda k, who: mixed_all.at[who, pl.ds(pl.multiple_of(k * BLOCK, BLOCK), BLOCK), :],
        lambda k, who, half: mixed_all.at[
            who, pl.ds(pl.multiple_of(k * BLOCK + half * (BLOCK // 2), 16), BLOCK // 2), :
        ],
        ring_sems,
    )
    half_rows = proj.shape[0] // 2
    weights_gather = Gather(
        lambda k, who: proj_all.at[who],
        lambda k, who, half: proj_all.at[who, pl.ds(half * half_rows, half_rows), :],
        proj_sems,
    )
    weights_gather.start(0)
    query[...] = cols_product(low, query_w[...]).astype(BF)
    key[...] = cols_product(low, key_w[...]).astype(BF)
    value[...] = cols_product(low, value_w[...]).astype(BF)
    query_t[...] = cols_product(query_w[...], low).astype(BF)
    key_t[...] = cols_product(key_w[...], low).astype(BF)
    value_t[...] = cols_product(value_w[...], low).astype(BF)
    fill_bias(bias, buckets, table)
    weights_gather.forward(0)

    def step(pair, carry):
        for side in (0, 1):
            block = pair + side * pairs
            first = pl.multiple_of(block * BLOCK, BLOCK)
            shift = pl.multiple_of((blocks - 1 - block) * BLOCK, BLOCK)
            query_rows = query[pl.ds(first, BLOCK), :]
            total = jnp.zeros((BLOCK, width), F32)
            for head in range(heads):
                mask = head_mask(head, head_width, width)
                scores = product(query_rows * mask.astype(BF), key_t[...])
                scores = scores + bias[head, :, pl.ds(shift, tokens)]
                highest = jnp.max(scores, axis=-1, keepdims=True)
                weights = jnp.exp(scores - highest)
                summed = jnp.sum(weights, axis=-1, keepdims=True)
                part = product(weights.astype(BF), value[...]) / summed
                total = total + part * mask
                logsum[pl.ds(first, BLOCK), head : head + 1] = highest + jnp.log(summed)
            spot = pl.ds(pl.multiple_of(pair * BLOCK, BLOCK), BLOCK)
            mixed[pl.ds(first, BLOCK), :] = total.astype(BF)
            mixed_all[here, spot, side * width : (side + 1) * width] = total.astype(BF)
        gather.start(pair)

        @pl.when(pair > 0)
        def _():
            gather.forward(pair - 1)

        return carry

    lax.fori_loop(0, pairs, step, 0)
    weights_gather.finish(0)
    gather.forward(pairs - 1)
    for k in range(pairs):
        gather.finish(k)
    weights_gather.drain(0)
    for k in range(pairs):
        gather.drain(k)


def pack_third(third, experts):
    half = third.shape[1] // 2
    split = third.reshape(experts, 8, 2 * half)
    split = jnp.concatenate([split[:, :, :half], split[:, :, half:]], axis=1)
    return split.reshape(experts * 16, half)


def unpack_third(tail, runs):
    half = tail.shape[1]
    split = tail.astype(F32).reshape(runs, 16, half)
    return jnp.concatenate([split[:, :8], split[:, 8:]], axis=2).reshape(runs * 8, 2 * half)


def slot_of_row(row, experts, capacity):
    body = 16 * experts
    first = (row // 16) * capacity + row % 16
    second = ((row - body) // 16) * capacity + 16 + (row - body) % 16
    third = ((row - 2 * body) // 8) * capacity + 32 + (row - 2 * body) % 8
    return jnp.where(row < body, first, jnp.where(row < 2 * body, second, third))


def route_body(
    capacity, rows, mixed, proj, gain, router_w, ids_row, cotangent,
    residual, hidden, probs, send, slots, gates,
):
    tokens, width = rows.shape
    experts = router_w.shape[0]
    body = 16 * experts
    half, here = mixed.shape[1], mixed.shape[2] // 2
    for side in (0, 1):
        spot = slice(side * half, (side + 1) * half)
        total = rows[spot, :].astype(F32)
        for i in range(mixed.shape[0]):
            total = total + product(mixed[i, :, side * here : (side + 1) * here], proj[i])
        residual[spot, :] = total
    res = residual[...]
    low = (res * inverse_rms(res) * gain[...]).astype(BF)
    hidden[...] = low
    logits = cols_product(low, router_w[...])
    shifted = jnp.exp(logits - jnp.max(logits, axis=-1, keepdims=True))
    chances = shifted / jnp.sum(shifted, axis=-1, keepdims=True)
    probs[...] = chances
    number = lax.broadcasted_iota(jnp.int32, (experts, tokens), 0)
    hot_t = ids_row[...] == number
    ones_t = jnp.where(hot_t, 1.0, 0.0)
    hot = ones_t.T > 0.5
    gate = jnp.sum(jnp.where(hot, chances, 0.0), axis=1, keepdims=True)
    gates[...] = gate
    across = lax.broadcasted_iota(jnp.int32, (tokens, tokens), 0)
    along = lax.broadcasted_iota(jnp.int32, (tokens, tokens), 1)
    lower = jnp.where(across >= along, 1.0, 0.0).astype(BF)
    upper = jnp.where(across <= along, 1.0, 0.0).astype(BF)
    counts = product(lower, jnp.where(hot, 1.0, 0.0).astype(BF))
    counts_t = product(ones_t.astype(BF), upper)
    position = jnp.sum(jnp.where(hot, counts - 1.0, 0.0), axis=1, keepdims=True)
    position_t = jnp.sum(jnp.where(hot_t, counts_t - 1.0, 0.0), axis=0, keepdims=True)
    expert = lax.broadcasted_iota(jnp.int32, (tokens, experts), 1)
    chosen = jnp.sum(jnp.where(hot, expert.astype(F32), 0.0), axis=1, keepdims=True)
    slots[...] = chosen.astype(jnp.int32) * capacity + position.astype(jnp.int32)
    slots_t = ids_row[...] * capacity + position_t.astype(jnp.int32)
    grads = (gate * cotangent[...].astype(F32)).astype(BF)

    def group(begin, count):
        number = slot_of_row(
            lax.broadcasted_iota(jnp.int32, (count, 1), 0) + begin, experts, capacity
        )
        return jnp.where(number == slots_t, 1.0, 0.0).astype(BF)

    for begin, count, lane in ((0, body, 0), (body, body, width)):
        place = group(begin, count)
        send[0, :, lane : lane + width] = product(place, low).astype(BF)
        send[1, :, lane : lane + width] = product(place, grads).astype(BF)
    place = group(2 * body, body // 2)
    send[0, :, 2 * width :] = pack_third(product(place, low), experts).astype(BF)
    send[1, :, 2 * width :] = pack_third(product(place, grads), experts).astype(BF)


def expert_body(
    packed, weight_in, weight_out,
    value, back, in_grad, out_grad, tail_rows, tail_grads,
):
    width = weight_in.shape[0]
    rows, grads = packed.at[0], packed.at[1]
    body = packed.shape[1]
    runs = body // 16
    tail_rows[...] = unpack_third(rows[:, 2 * width :], runs).astype(BF)
    tail_grads[...] = unpack_third(grads[:, 2 * width :], runs).astype(BF)
    in_grad[...] = jnp.zeros(in_grad.shape, F32)
    out_grad[...] = jnp.zeros(out_grad.shape, F32)

    def chunk(x, g):
        pre = product(x, weight_in[...])
        inner = jnp.tanh(gelu_root * (pre + gelu_cube * pre * pre * pre))
        act = (0.5 * pre * (1.0 + inner)).astype(BF)
        slope = 0.5 * (1.0 + inner) + 0.5 * pre * (1.0 - inner * inner) * (
            gelu_root * (1.0 + 3.0 * gelu_cube * pre * pre)
        )
        out = product(act, weight_out[...])
        dots = jnp.sum(out * g.astype(F32), axis=1, keepdims=True)
        out_grad[...] += rows_product(act, g)
        act_grad = cols_product(g, weight_out[...])
        pre_grad = (act_grad * slope).astype(BF)
        in_grad[...] += rows_product(x, pre_grad)
        rows_back = cols_product(pre_grad, weight_in[...])
        return out, dots, rows_back

    lane = lax.broadcasted_iota(jnp.int32, (1, 128), 1)
    part = 256
    for begin in range(0, body, part):
        spot = pl.ds(begin, part)
        marks = jnp.zeros((part, 128), F32)
        for side in (0, 1):
            lanes = slice(side * width, (side + 1) * width)
            out, dots, rows_back = chunk(rows[spot, lanes], grads[spot, lanes])
            value[spot, lanes] = out.astype(BF)
            back[spot, lanes] = rows_back.astype(BF)
            marks = marks + jnp.where(lane == side, dots, 0.0)
        back[spot, 2 * width + width // 2 :] = marks.astype(BF)
    out, dots, rows_back = chunk(tail_rows[...], tail_grads[...])
    value[:, 2 * width + width // 2 :] = jnp.zeros((body, 128), BF)
    value[:, 2 * width : 2 * width + width // 2] = pack_third(out, runs).astype(BF)
    back[:, 2 * width : 2 * width + width // 2] = pack_third(rows_back, runs).astype(BF)
    spread = jnp.where(lane == 2, dots, 0.0).reshape(runs, 8, 128)
    spread = jnp.concatenate([spread, jnp.zeros_like(spread)], axis=1).reshape(body, 128)
    marks = back[:, 2 * width + width // 2 :].astype(F32) + spread
    back[:, 2 * width + width // 2 :] = marks.astype(BF)


def place_of(slots, experts, capacity, rows):
    number = slot_of_row(lax.broadcasted_iota(jnp.int32, (1, rows), 1), experts, capacity)
    return jnp.where(slots == number, 1.0, 0.0).astype(BF)


def fetch(place, ref, width, experts):
    body = 16 * experts
    picked = product(place[:, :body], ref[:, :width])
    picked = picked + product(place[:, body : 2 * body], ref[:, width : 2 * width])
    tail = unpack_third(ref[:, 2 * width : 2 * width + width // 2], experts).astype(BF)
    return picked + product(place[:, 2 * body :], tail)


def backward_body(
    batch_size, capacity, head_width, lanes,
    value_in, back, slots, residual, hidden, probs, gain, router_w, cotangent, mixed, proj,
    normed, query, query_t, key, key_t, value_t, logsum,
    query_w, key_w, value_w, buckets, table, rows,
    returned, residual_grad, normed_part, large, small,
    grad, grad_t, bias, sums, query_back, key_acc, value_acc, stage, *rest,
):
    buffers, (send, arrive, sum_sems, ring_sems) = rest[:6], rest[6:]
    signals = greet(4, batch_size)
    reduce, gather, scatter, collect, drain = return_parts(
        batch_size, lanes, value_in, returned, stage, buffers, send, arrive, sum_sems, ring_sems
    )
    tokens, full = residual.shape
    experts = router_w.shape[0]
    body = 16 * experts
    heads = bias.shape[0]
    width = query.shape[1]
    blocks = tokens // BLOCK
    place = place_of(slots[...], experts, capacity, 5 * body // 2)
    meet(signals)
    for k in range(GROUPS):
        reduce.start(k)

    marks = back[:, 2 * full + full // 2 :]
    lane = lax.broadcasted_iota(jnp.int32, (1, 128), 1)
    tail = marks.astype(F32).reshape(experts, 16, 128)[:, :8].reshape(experts * 8, 128).astype(BF)
    dots = jnp.where(lane == 0, product(place[:, :body], marks), 0.0)
    dots = dots + jnp.where(lane == 1, product(place[:, body : 2 * body], marks), 0.0)
    dots = dots + jnp.where(lane == 2, product(place[:, 2 * body :], tail), 0.0)
    weighted = jnp.sum(dots, axis=1, keepdims=True)
    hot = slots[...] // capacity == lax.broadcasted_iota(jnp.int32, (tokens, experts), 1)
    logit_grad = (jnp.where(hot, weighted, 0.0) - probs[...] * weighted).astype(BF)
    router_grad = rows_product(logit_grad, hidden[...])
    hidden_grad = fetch(place, back, full, experts) + product(logit_grad, router_w[...])
    for k in range(GROUPS // 2):
        reduce.middle(k)
    res = residual[...]
    scale = inverse_rms(res)
    gain_grad = jnp.sum(hidden_grad * res * scale, axis=0, keepdims=True)
    scaled = gain[...] * hidden_grad
    middle = jnp.mean(scaled * res, axis=-1, keepdims=True)
    total = cotangent[...].astype(F32) + scale * scaled - res * (scale * scale * scale * middle)
    low = total.astype(BF)
    residual_grad[...] = total
    for k in range(GROUPS // 2, GROUPS):
        reduce.middle(k)
    large[3 * width :, :] = rows_product(mixed[...], low).astype(BF)
    grad[...] = cols_product(low, proj[...]).astype(BF)
    grad_t[...] = cols_product(proj[...], low).astype(BF)

    fill_bias(bias, buckets, table)
    sums[...] = jnp.zeros(sums.shape, F32)
    key_acc[...] = jnp.zeros(key_acc.shape, F32)
    value_acc[...] = jnp.zeros(value_acc.shape, F32)

    def step(block, carry):
        first = pl.multiple_of(block * BLOCK, BLOCK)
        shift = pl.multiple_of((blocks - 1 - block) * BLOCK, BLOCK)
        query_rows = query[pl.ds(first, BLOCK), :]
        grad_rows = grad[pl.ds(first, BLOCK), :]
        acc = jnp.zeros((BLOCK, width), F32)
        for head in range(heads):
            mask = head_mask(head, head_width, width)
            span = slice(head * head_width, (head + 1) * head_width)
            scores = product(query_rows * mask.astype(BF), key_t[...])
            scores = scores + bias[head, :, pl.ds(shift, tokens)]
            chances = jnp.exp(scores - logsum[pl.ds(first, BLOCK), head : head + 1])
            prob_grad = product(grad_rows * mask.astype(BF), value_t[...])
            centre = jnp.sum(chances * prob_grad, axis=-1, keepdims=True)
            score_grad = chances * (prob_grad - centre)
            score_low = score_grad.astype(BF)
            sums[head, :, pl.ds(shift, tokens)] += score_grad
            acc = acc + product(score_low, key[...]) * mask
            key_acc[span, :] += product(query_t[span, pl.ds(first, BLOCK)], score_low)
            value_acc[span, :] += product(grad_t[span, pl.ds(first, BLOCK)], chances.astype(BF))
        query_back[pl.ds(first, BLOCK), :] = acc.astype(BF)
        return carry

    def run(begin, end):
        lax.fori_loop(begin, end, step, 0)

    run(0, 2)
    scatter(0)
    scatter(1)
    run(2, 3)
    scatter(2)
    scatter(3)
    run(3, 5)
    collect(0)
    collect(1)
    run(5, 6)
    collect(2)
    collect(3)
    run(6, 7)
    gather.forward(0)
    gather.forward(1)
    run(7, blocks)
    gather.forward(2)
    gather.forward(3)
    backs = [query_back[...], key_acc[...].T.astype(BF), value_acc[...].T.astype(BF)]
    backs_t = [query_back[...].astype(F32).T.astype(BF)]
    backs_t += [key_acc[...].astype(BF), value_acc[...].astype(BF)]
    part = product(backs[0], query_w[...])
    part = part + product(backs[1], key_w[...]) + product(backs[2], value_w[...])
    normed_part[...] = part.astype(BF)
    for i in range(3):
        large[i * width : (i + 1) * width, :] = product(backs_t[i], normed[...]).astype(BF)
    inputs = rows[...].astype(F32)
    line = jnp.sum(part * inputs * inverse_rms(inputs), axis=0, keepdims=True)
    small[...] = jnp.zeros(small.shape, BF)
    small[0:experts, 0:full] = router_grad.astype(BF)
    row = lax.broadcasted_iota(jnp.int32, (16, 1), 0)
    pair = jnp.where(row == 0, gain_grad, jnp.where(row == 8, line, 0.0))
    small[32:48, 0:full] = pair.astype(BF)

    padded = buckets.shape[1]
    lines = []
    for head in range(heads):
        wide = jnp.concatenate(
            [sums[head], jnp.zeros((BLOCK, padded - sums.shape[2]), F32)], axis=1
        )
        gathered = jnp.zeros((8, padded), F32)
        for piece_at in range(0, BLOCK, 8):
            piece = wide[piece_at : piece_at + 8, :]
            gathered = gathered + pltpu.roll(piece, (BLOCK - 1 - piece_at) % padded, 1)
        line = jnp.zeros((1, padded), F32)
        for i in range(8):
            line = line + pltpu.roll(gathered, (padded - i) % padded, 1)[i : i + 1, :]
        lines.append(line)
    number = lax.broadcasted_iota(jnp.int32, (table.shape[1], padded), 0)
    matches = jnp.where(buckets[...] == number, 1.0, 0.0)
    stacked = jnp.concatenate(lines + [jnp.zeros((16 - heads, padded), F32)], axis=0)
    sums_of = lax.dot_general(
        stacked,
        matches,
        (((1,), (1,)), ((), ())),
        precision=lax.Precision.HIGHEST,
        preferred_element_type=F32,
    )
    blank = jnp.zeros((16, 128 - table.shape[1]), F32)
    small[48:64, 0:128] = jnp.concatenate([sums_of, blank], axis=1).astype(BF)
    for k in range(GROUPS):
        gather.finish(k)
    drain()


def per_device(
    layer_in, expert_ids, rel_buckets, first_gain, query_weight, key_weight, value_weight,
    proj_weight, rel_table, second_gain, router_weight, expert_in, expert_out, cotangent,
):
    tokens, width = layer_in.shape
    heads = rel_table.shape[1]
    here = query_weight.shape[1]
    head_width = here // heads
    experts = router_weight.shape[1]
    capacity = 5 * tokens // (4 * experts)
    body = 16 * experts
    packed = 2 * width + width // 2
    quarter = width // 2
    span = 2 * tokens - BLOCK
    ring_size = width // here
    gain_one = first_gain[None, :]
    gain_two = second_gain[None, :]
    buckets = jnp.pad(rel_buckets, (0, 1), constant_values=-1)[None, :]
    weights = (query_weight.T, key_weight.T, value_weight.T)
    table = rel_table.T
    router = router_weight.T

    mixed, mixed_all, proj_all, normed, query, query_t, key, key_t, value_t, logsum = call(
        functools.partial(attend_body, head_width),
        "attend",
        [
            ((tokens, here), BF),
            ((ring_size, tokens // 2, 2 * here), BF),
            ((ring_size, here, width), BF),
            ((tokens, width), BF),
            ((tokens, here), BF),
            ((here, tokens), BF),
            ((tokens, here), BF),
            ((here, tokens), BF),
            ((here, tokens), BF),
            ((tokens, 128), F32),
        ],
        [
            pltpu.VMEM((heads, BLOCK, span), F32),
            pltpu.VMEM((tokens, here), BF),
            sems(tokens // BLOCK // 2, 8),
            sems(1, 8),
        ],
        layer_in, gain_one, *weights, proj_weight, buckets, table,
        number=1,
    )
    residual, hidden, probs, leaving, slots, gates = call(
        functools.partial(route_body, capacity),
        "route",
        [
            ((tokens, width), F32),
            ((tokens, width), BF),
            ((tokens, experts), F32),
            ((2, body, packed), BF),
            ((tokens, 1), jnp.int32),
            ((tokens, 1), F32),
        ],
        [],
        layer_in, mixed_all, proj_all, gain_two, router, expert_ids.reshape(1, tokens), cotangent,
    )
    (arrived,) = call(
        functools.partial(dispatch_body, experts, quarter),
        "dispatch",
        [((2, body, packed), BF)],
        [sems(2), sems(GROUPS + 1), sems(GROUPS, 8)],
        leaving,
        number=2,
    )
    value, back, in_grad, out_grad = call(
        expert_body,
        "expert",
        [
            ((body, packed + 128), BF),
            ((body, packed + 128), BF),
            ((width, expert_in.shape[2]), F32),
            ((expert_out.shape[1], width), F32),
        ],
        [pltpu.VMEM((body // 2, width), BF)] * 2,
        arrived, expert_in[0], expert_out[0],
    )

    (back_sum,) = call(
        functools.partial(return_body, experts, (packed + 128) // 4),
        "give_back",
        [((body, packed + 128), BF)],
        return_scratch(experts, (packed + 128) // 4),
        back,
        number=3,
    )
    returned, residual_grad, normed_part, large, small = call(
        functools.partial(backward_body, experts, capacity, head_width, (packed + 128) // 4),
        "backward",
        [
            ((body, packed + 128), BF),
            ((tokens, width), F32),
            ((tokens, width), BF),
            ((4 * here, width), BF),
            ((64, 1024), BF),
        ],
        [
            pltpu.VMEM((tokens, here), BF),
            pltpu.VMEM((here, tokens), BF),
            pltpu.VMEM((heads, BLOCK, span), F32),
            pltpu.VMEM((heads, BLOCK, span), F32),
            pltpu.VMEM((tokens, here), BF),
            pltpu.VMEM((here, tokens), F32),
            pltpu.VMEM((here, tokens), F32),
            *return_scratch(experts, (packed + 128) // 4),
        ],
        value, back_sum, slots, residual, hidden, probs, gain_two, router, cotangent, mixed,
        proj_weight, normed, query, query_t, key, key_t, value_t, logsum, *weights, buckets, table,
        layer_in,
        number=5,
        mib=58,
    )
    peers = experts // 2
    tall, wide = 4 * here // peers, width // 2
    summed, large_sum, small_sum, lines, output = call(
        functools.partial(final_body, experts, capacity),
        "final",
        [
            ((tokens, width), BF),
            ((4 * here, width), BF),
            ((64, 1024), BF),
            ((3, 16, 1024), BF),
            ((tokens, width), BF),
        ],
        [
            pltpu.VMEM((4 * here, wide), BF),
            pltpu.VMEM((64, 512), BF),
            pltpu.VMEM((peers, tall, wide), BF),
            pltpu.VMEM((peers, 16, 128), BF),
            *reduce_scratch(4, tokens // 32, width),
            sems(8),
            sems(8),
            sems(3, 2),
            sems(4, 8),
            sems(4, 8),
        ],
        normed_part, large, small, returned, slots, gates, residual,
        number=4,
    )

    def whole(array):
        return pl.BlockSpec(array.shape, lambda i: (0,) * len(array.shape))

    def strip(array):
        return pl.BlockSpec((128, array.shape[1]), lambda i: (i, 0))

    results = [
        jax.ShapeDtypeStruct(shape, F32)
        for shape in [(tokens, width)] + [(here, width)] * 4
        + [(experts, width), (1, width), (1, width), table.shape]
    ]
    (
        input_grad, query_grad, key_grad, value_grad, proj_total, router_total, gain_total,
        first_total, table_total,
    ) = pl.pallas_call(
        finish_body,
        name="finish",
        grid=(tokens // 128,),
        out_shape=results,
        in_specs=[
            strip(summed), strip(layer_in), strip(residual_grad), whole(gain_one),
            whole(large_sum), whole(small_sum), whole(lines),
        ],
        out_specs=[strip(results[0])] + [whole(result) for result in results[1:]],
        compiler_params=pltpu.CompilerParams(vmem_limit_bytes=32 * MIB),
    )(summed, layer_in, residual_grad, gain_one, large_sum, small_sum, lines)
    return (
        output,
        input_grad,
        first_total[0],
        query_grad.T,
        key_grad.T,
        value_grad.T,
        proj_total,
        table_total.T,
        gain_total[0],
        router_total.T,
        in_grad[None],
        out_grad[None],
    )


def solution(mesh):
    return jax.shard_map(
        per_device,
        mesh=mesh,
        in_specs=(
            P("exp", None),
            P("exp", None),
            P(),
            P(),
            P(None, "tp"),
            P(None, "tp"),
            P(None, "tp"),
            P("tp", None),
            P(None, "tp"),
            P(),
            P(),
            P("exp", None, "tp"),
            P("exp", "tp", None),
            P("exp", None),
        ),
        out_specs=(
            P("exp", None),
            P("exp", None),
            P(),
            P(None, "tp"),
            P(None, "tp"),
            P(None, "tp"),
            P("tp", None),
            P(None, "tp"),
            P(),
            P(),
            P("exp", None, "tp"),
            P("exp", "tp", None),
        ),
        check_vma=False,
    )
```

```python
import functools

import jax
import jax.numpy as jnp
from jax import lax
from jax.experimental import pallas as pl
from jax.experimental.pallas import tpu as pltpu
from jax.sharding import PartitionSpec as P

epsilon = 1e-06
gelu_root = 0.7978845608028654
gelu_cube = 0.044715
BF = jnp.bfloat16
F32 = jnp.float32
BLOCK = 128
MIB = 1024 * 1024
GROUPS = 4
MESH = pl.DeviceIdType.MESH


def product(left, right):
    return jnp.dot(left, right, preferred_element_type=F32)


def rows_product(left, right):
    return lax.dot_general(left, right, (((0,), (0,)), ((), ())), preferred_element_type=F32)


def cols_product(left, right):
    return lax.dot_general(left, right, (((1,), (1,)), ((), ())), preferred_element_type=F32)


def inverse_rms(values):
    return lax.rsqrt(jnp.mean(values * values, axis=-1, keepdims=True) + epsilon)


def call(body, name, outs, scratch, *operands, mib=48, number=None):
    vmem = pl.BlockSpec(memory_space=pltpu.VMEM)
    extra = {} if number is None else {"collective_id": number, "has_side_effects": True}
    return pl.pallas_call(
        body,
        name=name,
        out_shape=[jax.ShapeDtypeStruct(shape, dtype) for shape, dtype in outs],
        in_specs=[vmem] * len(operands),
        out_specs=[vmem] * len(outs),
        scratch_shapes=scratch,
        compiler_params=pltpu.CompilerParams(vmem_limit_bytes=mib * MIB, **extra),
    )(*operands)


def remote(source, target, send, receive, **where):
    return pltpu.make_async_remote_copy(
        src_ref=source,
        dst_ref=target,
        send_sem=send,
        recv_sem=receive,
        device_id=where,
        device_id_type=MESH,
    )


def ring(ring_size):
    here = lax.axis_index("tp")
    return here, lax.rem(here + 1, ring_size), lax.rem(here + ring_size - 1, ring_size)


def greet(ring_size, batch_size, opposite=False, same_core=False):
    barrier = pltpu.get_barrier_semaphore()
    here, right, left = ring(ring_size)
    for side in (right, left):
        pl.semaphore_signal(barrier, inc=1, device_id={"tp": side}, device_id_type=MESH)
    if opposite:
        side = lax.rem(here + 2, ring_size)
        pl.semaphore_signal(barrier, inc=1, device_id={"tp": side}, device_id_type=MESH)
    me = lax.axis_index("exp")
    if same_core:
        sibling = me + 1 - 2 * lax.rem(me, 2)
        pl.semaphore_signal(barrier, inc=1, device_id={"exp": sibling}, device_id_type=MESH)
    if not batch_size:
        return 2 + int(opposite) + int(same_core)
    stride = 2 if same_core else 1
    peers = batch_size // stride

    def hello(step, carry):
        peer = lax.rem(me + step * stride, batch_size)
        pl.semaphore_signal(barrier, inc=1, device_id={"exp": peer}, device_id_type=MESH)
        return carry

    lax.fori_loop(1, peers, hello, 0)
    return 2 + int(opposite) + peers - 1 + int(same_core)


def meet(signals):
    pl.semaphore_wait(pltpu.get_barrier_semaphore(), signals)


class Gather:
    def __init__(self, region, half, sems):
        self.region, self.half, self.sems = region, half, sems
        self.here, self.right, self.left = ring(4)
        self.far = lax.rem(self.here + 2, 4)

    def first(self, k):
        own = self.region(k, self.here)
        return (
            remote(own, own, self.sems.at[k, 0], self.sems.at[k, 1], tp=self.right),
            remote(own, own, self.sems.at[k, 2], self.sems.at[k, 3], tp=self.left),
        )

    def second(self, k):
        low, high = self.half(k, self.left, 0), self.half(k, self.right, 1)
        return (
            remote(low, low, self.sems.at[k, 4], self.sems.at[k, 5], tp=self.right),
            remote(high, high, self.sems.at[k, 6], self.sems.at[k, 7], tp=self.left),
        )

    def start(self, k):
        for copy in self.first(k):
            copy.start()

    def forward(self, k):
        for side, copy, arrived in zip(
            (self.left, self.right), self.second(k), (1, 3), strict=True
        ):
            whole = self.region(k, side)
            remote(whole, whole, self.sems.at[k, 0], self.sems.at[k, arrived], tp=self.right).wait_recv()
            copy.start()

    def finish(self, k):
        for half, sent, arrived in ((0, 4, 5), (1, 6, 7)):
            part = self.half(k, self.far, half)
            remote(part, part, self.sems.at[k, sent], self.sems.at[k, arrived], tp=self.right).wait_recv()

    def drain(self, k):
        for copy in self.first(k) + self.second(k):
            copy.wait_send()


class Reduce:
    def __init__(self, piece, in_left, in_right, out_right, out_left, mid_left, mid_right, sems):
        self.piece, self.sems = piece, sems
        self.in_left, self.in_right = in_left, in_right
        self.out_right, self.out_left = out_right, out_left
        self.mid_left, self.mid_right = mid_left, mid_right
        self.here, self.right, self.left = ring(4)
        self.far = lax.rem(self.here + 2, 4)

    def first(self, k):
        return (
            remote(self.piece(k, self.far, 0), self.in_left.at[k], self.sems.at[k, 0], self.sems.at[k, 1], tp=self.right),
            remote(self.piece(k, self.far, 1), self.in_right.at[k], self.sems.at[k, 2], self.sems.at[k, 3], tp=self.left),
        )

    def second(self, k):
        return (
            remote(self.out_right.at[k], self.mid_left.at[k], self.sems.at[k, 4], self.sems.at[k, 5], tp=self.right),
            remote(self.out_left.at[k], self.mid_right.at[k], self.sems.at[k, 6], self.sems.at[k, 7], tp=self.left),
        )

    def start(self, k):
        for copy in self.first(k):
            copy.start()

    def middle(self, k):
        by_left, by_right = self.first(k)
        to_right, to_left = self.second(k)
        by_left.wait_recv()
        summed = self.piece(k, self.right, 0)[...].astype(F32) + self.in_left[k].astype(F32)
        self.out_right[k, 0] = summed.astype(BF)
        self.out_right[k, 1] = self.piece(k, self.right, 1)[...]
        to_right.start()
        by_right.wait_recv()
        summed = self.piece(k, self.left, 1)[...].astype(F32) + self.in_right[k].astype(F32)
        self.out_left[k, 1] = summed.astype(BF)
        self.out_left[k, 0] = self.piece(k, self.left, 0)[...]
        to_left.start()

    def finish(self, k):
        for copy in self.second(k):
            copy.wait_recv()
        return [
            self.piece(k, self.here, half)[...].astype(F32)
            + self.mid_left[k, half].astype(F32)
            + self.mid_right[k, half].astype(F32)
            for half in (0, 1)
        ]

    def drain(self, k):
        for copy in self.first(k) + self.second(k):
            copy.wait_send()


def reduce_scratch(groups, rows, lanes):
    return [pltpu.VMEM((groups, rows, lanes), BF)] * 2 + [
        pltpu.VMEM((groups, 2, rows, lanes), BF)
    ] * 4


def sems(*dims):
    return pltpu.SemaphoreType.DMA(dims)


def return_parts(batch_size, lanes, source, out, stage, buffers, send, arrive, sum_sems, ring_sems):
    me = lax.axis_index("exp")
    here = lax.axis_index("tp")
    part = batch_size // GROUPS
    mine = pl.ds(pl.multiple_of(here * lanes, 128), lanes)
    own = pl.ds(pl.multiple_of(me * 16, 16), 16)

    def leaving(k):
        return lax.rem(me // part + GROUPS - k, GROUPS) * (part * 16)

    def arriving(k):
        return lax.rem(me // part + k, GROUPS) * (part * 16)

    def span(ref, base, who, begin, rows):
        spot = pl.ds(pl.multiple_of(base + begin, 16), rows)
        return ref.at[spot, pl.ds(pl.multiple_of(who * lanes, 128), lanes)]

    half_rows = part * 8
    reduce = Reduce(
        lambda k, who, half: span(source, leaving(k), who, half * half_rows, half_rows),
        *buffers,
        sum_sems,
    )
    gather = Gather(
        lambda k, who: span(out, arriving(k), who, 0, part * 16),
        lambda k, who, half: span(out, arriving(k), who, half * half_rows, half_rows),
        ring_sems,
    )

    def scatter(k):
        first, second = reduce.finish(k)
        spot = pl.multiple_of(leaving(k), 16)
        stage[pl.ds(spot, half_rows), :] = first.astype(BF)
        stage[pl.ds(pl.multiple_of(spot + half_rows, 16), half_rows), :] = second.astype(BF)
        if k == 0:
            out[own, mine] = stage[own, :]

        def step(j, carry):
            peer = lax.rem(me // part + GROUPS - k, GROUPS) * part + lax.rem(me + j, part)
            rows = pl.ds(pl.multiple_of(peer * 16, 16), 16)
            remote(stage.at[rows, :], out.at[own, mine], send.at[0], arrive.at[k], exp=peer).start()
            return carry

        lax.fori_loop(1 if k == 0 else 0, part, step, 0)

    def collect(k):
        rows = (part - 1 if k == 0 else part) * 16
        block = span(out, arriving(k), here, 0, rows)
        remote(block, block, send.at[0], arrive.at[k], exp=me).wait_recv()
        gather.start(k)

    def drain():
        whole = stage.at[pl.ds(0, (batch_size - 1) * 16), :]
        remote(whole, whole, send.at[0], arrive.at[0], exp=me).wait_send()
        for k in range(GROUPS):
            reduce.drain(k)
            gather.drain(k)

    return reduce, gather, scatter, collect, drain


def return_scratch(batch_size, lanes):
    return [
        pltpu.VMEM((batch_size * 16, lanes), BF),
        *reduce_scratch(GROUPS, batch_size * 8 // GROUPS, lanes),
        sems(1),
        sems(GROUPS),
        sems(GROUPS, 8),
        sems(GROUPS, 8),
    ]


def final_body(
    batch_size, capacity, part_in, large, small, returned, slots, gates, residual,
    summed, large_out, small_out, lines, output,
    large_side, small_side, large_in, small_in, *rest,
):
    buffers, (send, arrive, line_sems, sum_sems, ring_sems) = rest[:6], rest[6:]
    signals = greet(4, batch_size, opposite=True, same_core=True)
    me = lax.axis_index("exp")
    core = lax.rem(me, 2)
    sibling = me + 1 - 2 * core
    here, right, left = ring(4)
    tokens, width = part_in.shape
    chunk = tokens // 4
    groups = buffers[0].shape[0]
    half_rows = chunk // groups // 2
    peers, tall, wide = large_in.shape
    half_lanes = small.shape[1] // 2
    small_across = half_lanes // 128

    def spot(ref, who, k, begin, count):
        first = who * chunk + k * (2 * half_rows) + begin
        return ref.at[pl.ds(pl.multiple_of(first, 16), count), :]

    reduce = Reduce(
        lambda k, who, half: spot(part_in, who, k, half * half_rows, half_rows), *buffers, sum_sems
    )
    gather = Gather(
        lambda k, who: spot(summed, who, k, 0, 2 * half_rows),
        lambda k, who, half: spot(summed, who, k, half * half_rows, half_rows),
        ring_sems,
    )

    def large_half(ref, side):
        return ref.at[:, pl.ds(pl.multiple_of(side * wide, 128), wide)]

    def small_half(ref, side):
        return ref.at[:, pl.ds(pl.multiple_of(side * half_lanes, 128), half_lanes)]

    def large_rows(ref, who):
        return ref.at[pl.ds(pl.multiple_of(who * tall, 16), tall), :]

    def small_rows(ref, who):
        down = pl.ds(pl.multiple_of(who // small_across * 16, 16), 16)
        return ref.at[down, pl.ds(pl.multiple_of(lax.rem(who, small_across) * 128, 128), 128)]

    def large_final(who):
        down = pl.ds(pl.multiple_of(who * tall, 16), tall)
        return large_out.at[down, pl.ds(pl.multiple_of(core * wide, 128), wide)]

    def small_final(who):
        down = pl.ds(pl.multiple_of(who // small_across * 16, 16), 16)
        lane = core * half_lanes + lax.rem(who, small_across) * 128
        return small_out.at[down, pl.ds(pl.multiple_of(lane, 128), 128)]

    meet(signals)
    pair = [
        remote(large_half(large, 1 - core), large_side, send.at[0], arrive.at[0], exp=sibling),
        remote(small_half(small, 1 - core), small_side, send.at[1], arrive.at[1], exp=sibling),
    ]
    for copy in pair:
        copy.start()
    for k in range(groups):
        reduce.start(k)
    for copy in pair:
        copy.wait_recv()
    both = large_side[...].astype(F32) + large_half(large, core)[...].astype(F32)
    large_side[...] = both.astype(BF)
    both = small_side[...].astype(F32) + small_half(small, core)[...].astype(F32)
    small_side[...] = both.astype(BF)
    mine = me // 2

    def scatter(step, carry):
        peer = lax.rem(mine + step, peers)
        to = peer * 2 + core
        remote(large_rows(large_side, peer), large_in.at[step], send.at[2], arrive.at[2], exp=to).start()
        remote(small_rows(small_side, peer), small_in.at[step], send.at[3], arrive.at[3], exp=to).start()
        return carry

    lax.fori_loop(1, peers, scatter, 0)
    large_in[0] = large_rows(large_side, mine)[...]
    small_in[0] = small_rows(small_side, mine)[...]
    for k in range(groups):
        reduce.middle(k)

    experts = batch_size
    body = 16 * experts
    place = place_of(slots[...], experts, capacity, 5 * body // 2)
    token_rows = fetch(place, returned, width, experts)
    output[...] = (residual[...] + gates[...] * token_rows).astype(BF)

    large_rest = large_in.at[pl.ds(1, peers - 1)]
    small_rest = small_in.at[pl.ds(1, peers - 1)]
    remote(large_rest, large_rest, send.at[2], arrive.at[2], exp=me).wait_recv()
    remote(small_rest, small_rest, send.at[3], arrive.at[3], exp=me).wait_recv()

    def add(step, carry):
        return carry[0] + large_in[step].astype(F32), carry[1] + small_in[step].astype(F32)

    zero = (jnp.zeros((tall, wide), F32), jnp.zeros((16, 128), F32))
    large_sum, small_sum = lax.fori_loop(0, peers, add, zero)
    large_final(mine)[...] = large_sum.astype(BF)
    small_final(mine)[...] = small_sum.astype(BF)

    def spread(step, carry):
        to = lax.rem(mine + step, peers) * 2 + core
        own = large_final(mine)
        remote(own, own, send.at[4], arrive.at[4], exp=to).start()
        own = small_final(mine)
        remote(own, own, send.at[5], arrive.at[5], exp=to).start()
        return carry

    lax.fori_loop(1, peers, spread, 0)
    for k in range(groups):
        pieces = reduce.finish(k)
        for half in (0, 1):
            target = spot(summed, here, k, half * half_rows, half_rows)
            target[...] = pieces[half].astype(BF)
        gather.start(k)
    remote(large_rest, large_rest, send.at[4], arrive.at[4], exp=me).wait_recv()
    remote(small_rest, small_rest, send.at[5], arrive.at[5], exp=me).wait_recv()
    back = []
    for i, half in ((6, large_half(large_out, core)), (7, small_half(small_out, core))):
        back.append(remote(half, half, send.at[i], arrive.at[i], exp=sibling))
    for copy in back:
        copy.start()
    for k in range(groups):
        gather.forward(k)
    for i, half in ((6, large_half(large_out, 1 - core)), (7, small_half(small_out, 1 - core))):
        remote(half, half, send.at[i], arrive.at[i], exp=sibling).wait_recv()
    line = small_out.at[pl.ds(32, 16), :]
    others = (right, left, lax.rem(here + 2, 4))
    copies = [
        remote(line, lines.at[i], line_sems.at[i, 0], line_sems.at[i, 1], tp=side)
        for i, side in enumerate(others)
    ]
    for copy in copies:
        copy.start()
    for k in range(groups):
        gather.finish(k)
    for copy in copies:
        copy.wait_recv()
    for copy in copies + pair + back:
        copy.wait_send()
    for i, ref in ((2, large_rest), (3, small_rest), (4, large_rest), (5, small_rest)):
        remote(ref, ref, send.at[i], arrive.at[0], exp=me).wait_send()
    for k in range(groups):
        reduce.drain(k)
        gather.drain(k)


def finish_body(
    summed, rows, residual_grad, gain, large, small, lines,
    input_grad, query_grad, key_grad, value_grad, proj_grad, router_grad, gain_grad, first_grad,
    table_grad,
):
    inputs = rows[...].astype(F32)
    scale = inverse_rms(inputs)
    scaled = summed[...].astype(F32) * gain[...]
    middle = jnp.mean(scaled * inputs, axis=-1, keepdims=True)
    input_grad[...] = (
        residual_grad[...] + scale * scaled - inputs * (scale * scale * scale * middle)
    )

    @pl.when(pl.program_id(0) == 0)
    def _():
        high, width = query_grad.shape
        for i, ref in enumerate((query_grad, key_grad, value_grad, proj_grad)):
            ref[...] = large[i * high : (i + 1) * high, :].astype(F32)
        router_grad[...] = small[0 : router_grad.shape[0], 0:width].astype(F32)
        total = small[32:48, 0:width].astype(F32)
        gain_grad[...] = total[0:1]
        table_grad[...] = small[48:64, 0:128].astype(F32)[0:3, 0:32]
        for i in range(3):
            total = total + lines[i][:, 0:width].astype(F32)
        first_grad[...] = total[8:9]


def head_mask(head, head_width, width):
    lane = lax.broadcasted_iota(jnp.int32, (1, width), 1)
    return jnp.where(lane // head_width == head, 1.0, 0.0)


def fill_bias(bias, buckets, table):
    heads, block, width = bias.shape
    padded = buckets.shape[1]
    number = lax.broadcasted_iota(jnp.int32, (table.shape[1], padded), 0)
    hot = jnp.where(buckets[...] == number, 1.0, 0.0)
    offsets = jnp.dot(
        table[...], hot, precision=lax.Precision.HIGHEST, preferred_element_type=F32
    )
    for head in range(heads):
        spread = jnp.broadcast_to(offsets[head : head + 1, :], (block, padded))
        rolled = pltpu.roll(spread, padded - (block - 1), 1, stride=1, stride_axis=0)
        bias[head] = rolled[:, :width]


def attend_body(
    head_width, rows, gain, query_w, key_w, value_w, proj, buckets, table,
    mixed, mixed_all, proj_all, normed, query, query_t, key, key_t, value_t, logsum,
    bias, value, ring_sems, proj_sems, pair_sems,
):
    heads = bias.shape[0]
    tokens = rows.shape[0]
    width = query.shape[1]
    blocks = tokens // BLOCK
    pairs = blocks // 2
    signals = greet(4, 0, same_core=True)
    here = lax.axis_index("tp")
    me = lax.axis_index("exp")
    core = lax.rem(me, 2)
    sibling = me + 1 - 2 * core
    inputs = rows[...].astype(F32)
    low = (inputs * inverse_rms(inputs) * gain[...]).astype(BF)
    normed[...] = low
    proj_all[here] = proj[...]
    meet(signals)
    gather = Gather(
        lambda k, who: mixed_all.at[who, pl.ds(pl.multiple_of(k * BLOCK, BLOCK), BLOCK), :],
        lambda k, who, half: mixed_all.at[
            who, pl.ds(pl.multiple_of(k * BLOCK + half * (BLOCK // 2), 16), BLOCK // 2), :
        ],
        ring_sems,
    )
    half_rows = proj.shape[0] // 2

    def proj_part(who, side, begin, count):
        spot = pl.multiple_of(side * half_rows + begin, 16)
        return proj_all.at[who, pl.ds(spot, count), :]

    weights_gather = Gather(
        lambda k, who: proj_part(who, core, 0, half_rows),
        lambda k, who, half: proj_part(who, core, half * (half_rows // 2), half_rows // 2),
        proj_sems,
    )

    def to_sibling(i, who, side):
        part = proj_part(who, side, 0, half_rows)
        return remote(part, part, pair_sems.at[i, 0], pair_sems.at[i, 1], exp=sibling)

    foreign = (weights_gather.left, weights_gather.right, weights_gather.far)
    weights_gather.start(0)
    query[...] = cols_product(low, query_w[...]).astype(BF)
    key[...] = cols_product(low, key_w[...]).astype(BF)
    value[...] = cols_product(low, value_w[...]).astype(BF)
    query_t[...] = cols_product(query_w[...], low).astype(BF)
    key_t[...] = cols_product(key_w[...], low).astype(BF)
    value_t[...] = cols_product(value_w[...], low).astype(BF)
    fill_bias(bias, buckets, table)
    weights_gather.forward(0)
    for i in (0, 1):
        to_sibling(i, foreign[i], core).start()

    def step(pair, carry):
        for side in (0, 1):
            block = pair + side * pairs
            first = pl.multiple_of(block * BLOCK, BLOCK)
            shift = pl.multiple_of((blocks - 1 - block) * BLOCK, BLOCK)
            query_rows = query[pl.ds(first, BLOCK), :]
            total = jnp.zeros((BLOCK, width), F32)
            for head in range(heads):
                mask = head_mask(head, head_width, width)
                scores = product(query_rows * mask.astype(BF), key_t[...])
                scores = scores + bias[head, :, pl.ds(shift, tokens)]
                highest = jnp.max(scores, axis=-1, keepdims=True)
                weights = jnp.exp(scores - highest)
                summed = jnp.sum(weights, axis=-1, keepdims=True)
                part = product(weights.astype(BF), value[...]) / summed
                total = total + part * mask
                logsum[pl.ds(first, BLOCK), head : head + 1] = highest + jnp.log(summed)
            spot = pl.ds(pl.multiple_of(pair * BLOCK, BLOCK), BLOCK)
            mixed[pl.ds(first, BLOCK), :] = total.astype(BF)
            mixed_all[here, spot, side * width : (side + 1) * width] = total.astype(BF)
        gather.start(pair)

        @pl.when(pair > 0)
        def _():
            gather.forward(pair - 1)

        return carry

    lax.fori_loop(0, pairs // 2, step, 0)
    weights_gather.finish(0)
    to_sibling(2, foreign[2], core).start()
    lax.fori_loop(pairs // 2, pairs, step, 0)
    gather.forward(pairs - 1)
    for k in range(pairs):
        gather.finish(k)
    for i in range(3):
        to_sibling(i, foreign[i], 1 - core).wait_recv()
        to_sibling(i, foreign[i], core).wait_send()
    weights_gather.drain(0)
    for k in range(pairs):
        gather.drain(k)


def pack_third(third, experts):
    half = third.shape[1] // 2
    split = third.reshape(experts, 8, 2 * half)
    split = jnp.concatenate([split[:, :, :half], split[:, :, half:]], axis=1)
    return split.reshape(experts * 16, half)


def unpack_third(tail, runs):
    half = tail.shape[1]
    split = tail.astype(F32).reshape(runs, 16, half)
    return jnp.concatenate([split[:, :8], split[:, 8:]], axis=2).reshape(runs * 8, 2 * half)


def slot_of_row(row, experts, capacity):
    body = 16 * experts
    first = (row // 16) * capacity + row % 16
    second = ((row - body) // 16) * capacity + 16 + (row - body) % 16
    third = ((row - 2 * body) // 8) * capacity + 32 + (row - 2 * body) % 8
    return jnp.where(row < body, first, jnp.where(row < 2 * body, second, third))


def moe_body(
    batch_size, capacity, lanes, back_lanes,
    rows, mixed, proj, gain, router_w, ids_row, cotangent, weight_in, weight_out,
    residual, hidden, probs, slots, gates, value, back_sum, in_grad, out_grad,
    leave, arrived, back, stage, *rest,
):
    buffers, (send_back, arrive_back, sum_sems, back_sems) = rest[:6], rest[6:10]
    send, arrive, arrive_tail, ring_sems = rest[10:]
    signals = greet(4, batch_size)
    me = lax.axis_index("exp")
    here = lax.axis_index("tp")
    part = batch_size // GROUPS
    zone_rows = part * 16
    tokens, width = rows.shape
    experts = router_w.shape[0]
    half, heads_here = mixed.shape[1], mixed.shape[2] // 2
    for side in (0, 1):
        spot = slice(side * half, (side + 1) * half)
        total = rows[spot, :].astype(F32)
        for i in range(mixed.shape[0]):
            lane = side * heads_here
            total = total + product(mixed[i, :, lane : lane + heads_here], proj[i])
        residual[spot, :] = total
    res = residual[...]
    low = (res * inverse_rms(res) * gain[...]).astype(BF)
    hidden[...] = low
    logits = cols_product(low, router_w[...])
    shifted = jnp.exp(logits - jnp.max(logits, axis=-1, keepdims=True))
    chances = shifted / jnp.sum(shifted, axis=-1, keepdims=True)
    probs[...] = chances
    number = lax.broadcasted_iota(jnp.int32, (experts, tokens), 0)
    hot_t = ids_row[...] == number
    ones_t = jnp.where(hot_t, 1.0, 0.0)
    hot = ones_t.T > 0.5
    gate = jnp.sum(jnp.where(hot, chances, 0.0), axis=1, keepdims=True)
    gates[...] = gate
    across = lax.broadcasted_iota(jnp.int32, (tokens, tokens), 0)
    along = lax.broadcasted_iota(jnp.int32, (tokens, tokens), 1)
    upper = jnp.where(across <= along, 1.0, 0.0).astype(BF)
    counts_t = product(ones_t.astype(BF), upper)
    position_t = jnp.sum(jnp.where(hot_t, counts_t - 1.0, 0.0), axis=0, keepdims=True)
    slots_t = ids_row[...] * capacity + position_t.astype(jnp.int32)
    spread = jnp.broadcast_to(slots_t.astype(F32), (128, tokens))
    slots[...] = spread.T[:, 0:1].astype(jnp.int32)
    grads = (gate * cotangent[...].astype(F32)).astype(BF)
    meet(signals)

    mine = pl.ds(pl.multiple_of(here * lanes, 128), lanes)
    tail = pl.ds(4 * lanes, leave.shape[2] - 4 * lanes)
    own = pl.ds(pl.multiple_of(me * 16, 16), 16)
    place_row = lax.broadcasted_iota(jnp.int32, (zone_rows * 5 // 2, 1), 0)
    third = place_row - 2 * zone_rows
    inside = jnp.where(
        place_row < zone_rows,
        place_row // 16 * capacity + place_row % 16,
        jnp.where(
            place_row < 2 * zone_rows,
            (place_row - zone_rows) // 16 * capacity + 16 + place_row % 16,
            third // 8 * capacity + 32 + third % 8,
        ),
    )
    for k in range(GROUPS):
        zone = lax.rem(me // part + k, GROUPS)
        place = jnp.where(inside + zone * (part * capacity) == slots_t, 1.0, 0.0).astype(BF)
        spot = pl.ds(pl.multiple_of(zone * zone_rows, 16), zone_rows)
        for array, source in ((0, low), (1, grads)):
            picked = product(place, source)
            leave[array, spot, 0:width] = picked[:zone_rows].astype(BF)
            leave[array, spot, width : 2 * width] = picked[zone_rows : 2 * zone_rows].astype(BF)
            packed = pack_third(picked[2 * zone_rows :], part)
            leave[array, spot, 2 * width :] = packed.astype(BF)
        if k == 0:
            arrived[:, own, mine] = leave[:, own, mine]
            arrived[:, own, tail] = leave[:, own, tail]
        for columns, sent, landed in ((mine, 0, arrive), (tail, 1, arrive_tail)):

            def step(j, carry):
                peer = zone * part + lax.rem(me + j, part)
                block = pl.ds(pl.multiple_of(peer * 16, 16), 16)
                remote(
                    leave.at[:, block, columns], arrived.at[:, own, columns],
                    send.at[sent], landed.at[k], exp=peer,
                ).start()
                return carry

            lax.fori_loop(1 if k == 0 else 0, part, step, 0)

    def arriving(k):
        return lax.rem(me // part + GROUPS - k, GROUPS) * zone_rows

    def span(k, who, count, array=slice(None)):
        spot = pl.ds(pl.multiple_of(arriving(k), 16), count)
        return arrived.at[array, spot, pl.ds(pl.multiple_of(who * lanes, 128), lanes)]

    gather = Gather(
        lambda k, who: span(k, who, zone_rows),
        lambda k, who, side: span(k, who, zone_rows, pl.ds(side, 1)),
        ring_sems,
    )

    def quarter(k):
        block = span(k, here, zone_rows - 16 if k == 0 else zone_rows)
        remote(block, block, send.at[0], arrive.at[k], exp=me).wait_recv()
        gather.start(k)

    def whole(k):
        gather.finish(k)
        count = zone_rows - 16 if k == 0 else zone_rows
        block = arrived.at[:, pl.ds(pl.multiple_of(arriving(k), 16), count), tail]
        remote(block, block, send.at[1], arrive_tail.at[k], exp=me).wait_recv()

    def experts_on(k):
        spot = pl.ds(pl.multiple_of(arriving(k), 16), zone_rows)

        def rows_of(array):
            last = unpack_third(arrived[array, spot, 2 * width :], part).astype(BF)
            first = [arrived[array, spot, 0:width], arrived[array, spot, width : 2 * width]]
            return jnp.concatenate(first + [last], axis=0)

        x, g = rows_of(0), rows_of(1)
        pre = product(x, weight_in[...])
        inner = jnp.tanh(gelu_root * (pre + gelu_cube * pre * pre * pre))
        act = (0.5 * pre * (1.0 + inner)).astype(BF)
        slope = 0.5 * (1.0 + inner) + 0.5 * pre * (1.0 - inner * inner) * (
            gelu_root * (1.0 + 3.0 * gelu_cube * pre * pre)
        )
        act_grad = cols_product(g, weight_out[...])
        pre_grad = (act_grad * slope).astype(BF)
        rows_back = cols_product(pre_grad, weight_in[...])
        out = product(act, weight_out[...])
        dots = jnp.sum(out * g.astype(F32), axis=1, keepdims=True)
        lane = lax.broadcasted_iota(jnp.int32, (1, 128), 1)
        marks = jnp.where(lane == 0, dots[:zone_rows], 0.0)
        marks = marks + jnp.where(lane == 1, dots[zone_rows : 2 * zone_rows], 0.0)
        last = jnp.where(lane == 2, dots[2 * zone_rows :], 0.0).reshape(part, 8, 128)
        last = jnp.concatenate([last, jnp.zeros_like(last)], axis=1).reshape(zone_rows, 128)
        for ref, result, extra in (
            (back, rows_back, marks + last),
            (value, out, jnp.zeros((zone_rows, 128), F32)),
        ):
            ref[spot, 0:width] = result[:zone_rows].astype(BF)
            ref[spot, width : 2 * width] = result[zone_rows : 2 * zone_rows].astype(BF)
            packed = pack_third(result[2 * zone_rows :], part)
            ref[spot, 2 * width : 2 * width + width // 2] = packed.astype(BF)
            ref[spot, 2 * width + width // 2 :] = extra.astype(BF)
        return x, g, act, pre_grad

    def weights_on(k, held):
        x, g, act, pre_grad = held
        if k == 0:
            out_grad[...] = rows_product(act, g)
            in_grad[...] = rows_product(x, pre_grad)
        else:
            out_grad[...] += rows_product(act, g)
            in_grad[...] += rows_product(x, pre_grad)

    reduce, gather_back, scatter, collect, drain = return_parts(
        batch_size, back_lanes, back, back_sum, stage, buffers,
        send_back, arrive_back, sum_sems, back_sems,
    )

    def work(k):
        whole(k)
        held = experts_on(k)
        reduce.start(k)
        weights_on(k, held)

    quarter(0)
    quarter(1)
    gather.forward(0)
    quarter(2)
    gather.forward(1)
    work(0)
    quarter(3)
    gather.forward(2)
    reduce.middle(0)
    work(1)
    gather.forward(3)
    reduce.middle(1)
    scatter(0)
    work(2)
    reduce.middle(2)
    scatter(1)
    collect(0)
    work(3)
    reduce.middle(3)
    scatter(2)
    collect(1)
    gather_back.forward(0)
    scatter(3)
    collect(2)
    gather_back.forward(1)
    collect(3)
    gather_back.forward(2)
    gather_back.forward(3)
    for k in range(GROUPS):
        gather_back.finish(k)
    drain()
    for k in range(GROUPS):
        gather.drain(k)
    for columns, sent in ((mine, 0), (tail, 1)):
        block = leave.at[:, pl.ds(0, (batch_size - 1) * 16), columns]
        remote(block, block, send.at[sent], arrive.at[0], exp=me).wait_send()


def place_of(slots, experts, capacity, rows):
    number = slot_of_row(lax.broadcasted_iota(jnp.int32, (1, rows), 1), experts, capacity)
    return jnp.where(slots == number, 1.0, 0.0).astype(BF)


def fetch(place, ref, width, experts):
    body = 16 * experts
    picked = product(place[:, :body], ref[:, :width])
    picked = picked + product(place[:, body : 2 * body], ref[:, width : 2 * width])
    tail = unpack_third(ref[:, 2 * width : 2 * width + width // 2], experts).astype(BF)
    return picked + product(place[:, 2 * body :], tail)


def backward_body(
    batch_size, capacity, head_width, lanes,
    value_in, back, slots, residual, hidden, probs, gain, router_w, cotangent, mixed, proj,
    normed, query, query_t, key, key_t, value_t, logsum,
    query_w, key_w, value_w, buckets, table, rows,
    returned, residual_grad, normed_part, large, small,
    grad, grad_t, bias, sums, query_back, key_acc, value_acc, stage, *rest,
):
    buffers, (send, arrive, sum_sems, ring_sems) = rest[:6], rest[6:]
    signals = greet(4, batch_size)
    reduce, gather, scatter, collect, drain = return_parts(
        batch_size, lanes, value_in, returned, stage, buffers, send, arrive, sum_sems, ring_sems
    )
    tokens, full = residual.shape
    experts = router_w.shape[0]
    body = 16 * experts
    heads = bias.shape[0]
    width = query.shape[1]
    blocks = tokens // BLOCK
    place = place_of(slots[...], experts, capacity, 5 * body // 2)
    meet(signals)
    for k in range(GROUPS):
        reduce.start(k)

    marks = back[:, 2 * full + full // 2 :]
    lane = lax.broadcasted_iota(jnp.int32, (1, 128), 1)
    tail = marks.astype(F32).reshape(experts, 16, 128)[:, :8].reshape(experts * 8, 128).astype(BF)
    dots = jnp.where(lane == 0, product(place[:, :body], marks), 0.0)
    dots = dots + jnp.where(lane == 1, product(place[:, body : 2 * body], marks), 0.0)
    dots = dots + jnp.where(lane == 2, product(place[:, 2 * body :], tail), 0.0)
    weighted = jnp.sum(dots, axis=1, keepdims=True)
    hot = slots[...] // capacity == lax.broadcasted_iota(jnp.int32, (tokens, experts), 1)
    logit_grad = (jnp.where(hot, weighted, 0.0) - probs[...] * weighted).astype(BF)
    router_grad = rows_product(logit_grad, hidden[...])
    hidden_grad = fetch(place, back, full, experts) + product(logit_grad, router_w[...])
    for k in range(GROUPS // 2):
        reduce.middle(k)
    res = residual[...]
    scale = inverse_rms(res)
    gain_grad = jnp.sum(hidden_grad * res * scale, axis=0, keepdims=True)
    scaled = gain[...] * hidden_grad
    middle = jnp.mean(scaled * res, axis=-1, keepdims=True)
    total = cotangent[...].astype(F32) + scale * scaled - res * (scale * scale * scale * middle)
    low = total.astype(BF)
    residual_grad[...] = total
    for k in range(GROUPS // 2, GROUPS):
        reduce.middle(k)
    large[3 * width :, :] = rows_product(mixed[...], low).astype(BF)
    grad[...] = cols_product(low, proj[...]).astype(BF)
    grad_t[...] = cols_product(proj[...], low).astype(BF)

    fill_bias(bias, buckets, table)
    sums[...] = jnp.zeros(sums.shape, F32)
    key_acc[...] = jnp.zeros(key_acc.shape, F32)
    value_acc[...] = jnp.zeros(value_acc.shape, F32)

    def step(block, carry):
        first = pl.multiple_of(block * BLOCK, BLOCK)
        shift = pl.multiple_of((blocks - 1 - block) * BLOCK, BLOCK)
        query_rows = query[pl.ds(first, BLOCK), :]
        grad_rows = grad[pl.ds(first, BLOCK), :]
        acc = jnp.zeros((BLOCK, width), F32)
        for head in range(heads):
            mask = head_mask(head, head_width, width)
            span = slice(head * head_width, (head + 1) * head_width)
            scores = product(query_rows * mask.astype(BF), key_t[...])
            scores = scores + bias[head, :, pl.ds(shift, tokens)]
            chances = jnp.exp(scores - logsum[pl.ds(first, BLOCK), head : head + 1])
            prob_grad = product(grad_rows * mask.astype(BF), value_t[...])
            centre = jnp.sum(chances * prob_grad, axis=-1, keepdims=True)
            score_grad = chances * (prob_grad - centre)
            score_low = score_grad.astype(BF)
            sums[head, :, pl.ds(shift, tokens)] += score_grad
            acc = acc + product(score_low, key[...]) * mask
            key_acc[span, :] += product(query_t[span, pl.ds(first, BLOCK)], score_low)
            value_acc[span, :] += product(grad_t[span, pl.ds(first, BLOCK)], chances.astype(BF))
        query_back[pl.ds(first, BLOCK), :] = acc.astype(BF)
        return carry

    def run(begin, end):
        lax.fori_loop(begin, end, step, 0)

    run(0, 1)
    scatter(0)
    run(1, 2)
    scatter(1)
    run(2, 3)
    scatter(2)
    collect(0)
    run(3, 4)
    scatter(3)
    collect(1)
    gather.forward(0)
    run(4, 5)
    collect(2)
    gather.forward(1)
    run(5, 6)
    collect(3)
    gather.forward(2)
    run(6, 7)
    gather.forward(3)
    run(7, blocks)
    backs = [query_back[...], key_acc[...].T.astype(BF), value_acc[...].T.astype(BF)]
    backs_t = [query_back[...].astype(F32).T.astype(BF)]
    backs_t += [key_acc[...].astype(BF), value_acc[...].astype(BF)]
    part = product(backs[0], query_w[...])
    part = part + product(backs[1], key_w[...]) + product(backs[2], value_w[...])
    normed_part[...] = part.astype(BF)
    for i in range(3):
        large[i * width : (i + 1) * width, :] = product(backs_t[i], normed[...]).astype(BF)
    inputs = rows[...].astype(F32)
    line = jnp.sum(part * inputs * inverse_rms(inputs), axis=0, keepdims=True)
    small[...] = jnp.zeros(small.shape, BF)
    small[0:experts, 0:full] = router_grad.astype(BF)
    row = lax.broadcasted_iota(jnp.int32, (16, 1), 0)
    pair = jnp.where(row == 0, gain_grad, jnp.where(row == 8, line, 0.0))
    small[32:48, 0:full] = pair.astype(BF)

    padded = buckets.shape[1]
    lines = []
    for head in range(heads):
        wide = jnp.concatenate(
            [sums[head], jnp.zeros((BLOCK, padded - sums.shape[2]), F32)], axis=1
        )
        gathered = jnp.zeros((8, padded), F32)
        for piece_at in range(0, BLOCK, 8):
            piece = wide[piece_at : piece_at + 8, :]
            gathered = gathered + pltpu.roll(piece, (BLOCK - 1 - piece_at) % padded, 1)
        line = jnp.zeros((1, padded), F32)
        for i in range(8):
            line = line + pltpu.roll(gathered, (padded - i) % padded, 1)[i : i + 1, :]
        lines.append(line)
    number = lax.broadcasted_iota(jnp.int32, (table.shape[1], padded), 0)
    matches = jnp.where(buckets[...] == number, 1.0, 0.0)
    stacked = jnp.concatenate(lines + [jnp.zeros((16 - heads, padded), F32)], axis=0)
    sums_of = lax.dot_general(
        stacked,
        matches,
        (((1,), (1,)), ((), ())),
        precision=lax.Precision.HIGHEST,
        preferred_element_type=F32,
    )
    blank = jnp.zeros((16, 128 - table.shape[1]), F32)
    small[48:64, 0:128] = jnp.concatenate([sums_of, blank], axis=1).astype(BF)
    for k in range(GROUPS):
        gather.finish(k)
    drain()


def per_device(
    layer_in, expert_ids, rel_buckets, first_gain, query_weight, key_weight, value_weight,
    proj_weight, rel_table, second_gain, router_weight, expert_in, expert_out, cotangent,
):
    tokens, width = layer_in.shape
    heads = rel_table.shape[1]
    here = query_weight.shape[1]
    head_width = here // heads
    experts = router_weight.shape[1]
    capacity = 5 * tokens // (4 * experts)
    body = 16 * experts
    packed = 2 * width + width // 2
    span = 2 * tokens - BLOCK
    ring_size = width // here
    gain_one = first_gain[None, :]
    gain_two = second_gain[None, :]
    buckets = jnp.pad(rel_buckets, (0, 1), constant_values=-1)[None, :]
    weights = (query_weight.T, key_weight.T, value_weight.T)
    table = rel_table.T
    router = router_weight.T

    mixed, mixed_all, proj_all, normed, query, query_t, key, key_t, value_t, logsum = call(
        functools.partial(attend_body, head_width),
        "attend",
        [
            ((tokens, here), BF),
            ((ring_size, tokens // 2, 2 * here), BF),
            ((ring_size, here, width), BF),
            ((tokens, width), BF),
            ((tokens, here), BF),
            ((here, tokens), BF),
            ((tokens, here), BF),
            ((here, tokens), BF),
            ((here, tokens), BF),
            ((tokens, 128), F32),
        ],
        [
            pltpu.VMEM((heads, BLOCK, span), F32),
            pltpu.VMEM((tokens, here), BF),
            sems(tokens // BLOCK // 2, 8),
            sems(1, 8),
            sems(3, 2),
        ],
        layer_in, gain_one, *weights, proj_weight, buckets, table,
        number=1,
    )
    wide_lanes = (packed + 128) // 4
    residual, hidden, probs, slots, gates, value, back_sum, in_grad, out_grad = call(
        functools.partial(moe_body, experts, capacity, 256, wide_lanes),
        "experts",
        [
            ((tokens, width), F32),
            ((tokens, width), BF),
            ((tokens, experts), F32),
            ((tokens, 1), jnp.int32),
            ((tokens, 1), F32),
            ((body, packed + 128), BF),
            ((body, packed + 128), BF),
            ((width, expert_in.shape[2]), F32),
            ((expert_out.shape[1], width), F32),
        ],
        [
            pltpu.VMEM((2, body, packed), BF),
            pltpu.VMEM((2, body, packed), BF),
            pltpu.VMEM((body, packed + 128), BF),
            *return_scratch(experts, wide_lanes),
            sems(2),
            sems(GROUPS),
            sems(GROUPS),
            sems(GROUPS, 8),
        ],
        layer_in, mixed_all, proj_all, gain_two, router, expert_ids.reshape(1, tokens), cotangent,
        expert_in[0], expert_out[0],
        number=2,
        mib=60,
    )
    returned, residual_grad, normed_part, large, small = call(
        functools.partial(backward_body, experts, capacity, head_width, wide_lanes),
        "backward",
        [
            ((body, packed + 128), BF),
            ((tokens, width), F32),
            ((tokens, width), BF),
            ((4 * here, width), BF),
            ((64, 1024), BF),
        ],
        [
            pltpu.VMEM((tokens, here), BF),
            pltpu.VMEM((here, tokens), BF),
            pltpu.VMEM((heads, BLOCK, span), F32),
            pltpu.VMEM((heads, BLOCK, span), F32),
            pltpu.VMEM((tokens, here), BF),
            pltpu.VMEM((here, tokens), F32),
            pltpu.VMEM((here, tokens), F32),
            *return_scratch(experts, wide_lanes),
        ],
        value, back_sum, slots, residual, hidden, probs, gain_two, router, cotangent, mixed,
        proj_weight, normed, query, query_t, key, key_t, value_t, logsum, *weights, buckets, table,
        layer_in,
        number=5,
        mib=58,
    )
    peers = experts // 2
    tall, wide = 4 * here // peers, width // 2
    summed, large_sum, small_sum, lines, output = call(
        functools.partial(final_body, experts, capacity),
        "final",
        [
            ((tokens, width), BF),
            ((4 * here, width), BF),
            ((64, 1024), BF),
            ((3, 16, 1024), BF),
            ((tokens, width), BF),
        ],
        [
            pltpu.VMEM((4 * here, wide), BF),
            pltpu.VMEM((64, 512), BF),
            pltpu.VMEM((peers, tall, wide), BF),
            pltpu.VMEM((peers, 16, 128), BF),
            *reduce_scratch(4, tokens // 32, width),
            sems(8),
            sems(8),
            sems(3, 2),
            sems(4, 8),
            sems(4, 8),
        ],
        normed_part, large, small, returned, slots, gates, residual,
        number=4,
    )

    def whole(array):
        return pl.BlockSpec(array.shape, lambda i: (0,) * len(array.shape))

    def strip(array):
        return pl.BlockSpec((128, array.shape[1]), lambda i: (i, 0))

    results = [
        jax.ShapeDtypeStruct(shape, F32)
        for shape in [(tokens, width)] + [(here, width)] * 4
        + [(experts, width), (1, width), (1, width), table.shape]
    ]
    (
        input_grad, query_grad, key_grad, value_grad, proj_total, router_total, gain_total,
        first_total, table_total,
    ) = pl.pallas_call(
        finish_body,
        name="finish",
        grid=(tokens // 128,),
        out_shape=results,
        in_specs=[
            strip(summed), strip(layer_in), strip(residual_grad), whole(gain_one),
            whole(large_sum), whole(small_sum), whole(lines),
        ],
        out_specs=[strip(results[0])] + [whole(result) for result in results[1:]],
        compiler_params=pltpu.CompilerParams(vmem_limit_bytes=32 * MIB),
    )(summed, layer_in, residual_grad, gain_one, large_sum, small_sum, lines)
    return (
        output,
        input_grad,
        first_total[0],
        query_grad.T,
        key_grad.T,
        value_grad.T,
        proj_total,
        table_total.T,
        gain_total[0],
        router_total.T,
        in_grad[None],
        out_grad[None],
    )


def solution(mesh):
    return jax.shard_map(
        per_device,
        mesh=mesh,
        in_specs=(
            P("exp", None),
            P("exp", None),
            P(),
            P(),
            P(None, "tp"),
            P(None, "tp"),
            P(None, "tp"),
            P("tp", None),
            P(None, "tp"),
            P(),
            P(),
            P("exp", None, "tp"),
            P("exp", "tp", None),
            P("exp", None),
        ),
        out_specs=(
            P("exp", None),
            P("exp", None),
            P(),
            P(None, "tp"),
            P(None, "tp"),
            P(None, "tp"),
            P("tp", None),
            P(None, "tp"),
            P(),
            P(),
            P("exp", None, "tp"),
            P("exp", "tp", None),
        ),
        check_vma=False,
    )
```

```python
import functools

import jax
import jax.numpy as jnp
from jax import lax
from jax.experimental import pallas as pl
from jax.experimental.pallas import tpu as pltpu
from jax.sharding import PartitionSpec as P

epsilon = 1e-06
gelu_root = 0.7978845608028654
gelu_cube = 0.044715
BF = jnp.bfloat16
F32 = jnp.float32
BLOCK = 128
MIB = 1024 * 1024
GROUPS = 4
MESH = pl.DeviceIdType.MESH


def product(left, right):
    return jnp.dot(left, right, preferred_element_type=F32)


def rows_product(left, right):
    return lax.dot_general(left, right, (((0,), (0,)), ((), ())), preferred_element_type=F32)


def cols_product(left, right):
    return lax.dot_general(left, right, (((1,), (1,)), ((), ())), preferred_element_type=F32)


def inverse_rms(values):
    return lax.rsqrt(jnp.mean(values * values, axis=-1, keepdims=True) + epsilon)


def call(body, name, outs, scratch, *operands, mib=48, number=None, far_in=(), far_out=()):
    vmem = pl.BlockSpec(memory_space=pltpu.VMEM)
    far = pl.BlockSpec(memory_space=pltpu.HBM)
    extra = {} if number is None else {"collective_id": number, "has_side_effects": True}
    return pl.pallas_call(
        body,
        name=name,
        out_shape=[jax.ShapeDtypeStruct(shape, dtype) for shape, dtype in outs],
        in_specs=[far if i in far_in else vmem for i in range(len(operands))],
        out_specs=[far if i in far_out else vmem for i in range(len(outs))],
        scratch_shapes=scratch,
        compiler_params=pltpu.CompilerParams(vmem_limit_bytes=mib * MIB, **extra),
    )(*operands)


def remote(source, target, send, receive, **where):
    return pltpu.make_async_remote_copy(
        src_ref=source,
        dst_ref=target,
        send_sem=send,
        recv_sem=receive,
        device_id=where,
        device_id_type=MESH,
    )


def ring(ring_size):
    here = lax.axis_index("tp")
    return here, lax.rem(here + 1, ring_size), lax.rem(here + ring_size - 1, ring_size)


def greet(ring_size, batch_size, opposite=False, same_core=False):
    barrier = pltpu.get_barrier_semaphore()
    here, right, left = ring(ring_size)
    for side in (right, left):
        pl.semaphore_signal(barrier, inc=1, device_id={"tp": side}, device_id_type=MESH)
    if opposite:
        side = lax.rem(here + 2, ring_size)
        pl.semaphore_signal(barrier, inc=1, device_id={"tp": side}, device_id_type=MESH)
    me = lax.axis_index("exp")
    if same_core:
        sibling = me + 1 - 2 * lax.rem(me, 2)
        pl.semaphore_signal(barrier, inc=1, device_id={"exp": sibling}, device_id_type=MESH)
    if not batch_size:
        return 2 + int(opposite) + int(same_core)
    stride = 2 if same_core else 1
    peers = batch_size // stride

    def hello(step, carry):
        peer = lax.rem(me + step * stride, batch_size)
        pl.semaphore_signal(barrier, inc=1, device_id={"exp": peer}, device_id_type=MESH)
        return carry

    lax.fori_loop(1, peers, hello, 0)
    return 2 + int(opposite) + peers - 1 + int(same_core)


def meet(signals):
    pl.semaphore_wait(pltpu.get_barrier_semaphore(), signals)


def place_index(device):
    z, y, core = device // 8, device // 2 % 4, device % 2
    return (z + y) % 4 * 8 + z * 2 + core


def device_at(place):
    group, z, core = place // 8, place % 8 // 2, place % 2
    return z * 8 + (group + 4 - z) % 4 * 2 + core


class Gather:
    def __init__(self, region, half, sems):
        self.region, self.half, self.sems = region, half, sems
        self.here, self.right, self.left = ring(4)
        self.far = lax.rem(self.here + 2, 4)

    def first(self, k):
        own = self.region(k, self.here)
        return (
            remote(own, own, self.sems.at[k, 0], self.sems.at[k, 1], tp=self.right),
            remote(own, own, self.sems.at[k, 2], self.sems.at[k, 3], tp=self.left),
        )

    def second(self, k):
        low, high = self.half(k, self.left, 0), self.half(k, self.right, 1)
        return (
            remote(low, low, self.sems.at[k, 4], self.sems.at[k, 5], tp=self.right),
            remote(high, high, self.sems.at[k, 6], self.sems.at[k, 7], tp=self.left),
        )

    def start(self, k):
        for copy in self.first(k):
            copy.start()

    def forward(self, k):
        for side, copy, arrived in zip(
            (self.left, self.right), self.second(k), (1, 3), strict=True
        ):
            whole = self.region(k, side)
            remote(whole, whole, self.sems.at[k, 0], self.sems.at[k, arrived], tp=self.right).wait_recv()
            copy.start()

    def finish(self, k):
        for half, sent, arrived in ((0, 4, 5), (1, 6, 7)):
            part = self.half(k, self.far, half)
            remote(part, part, self.sems.at[k, sent], self.sems.at[k, arrived], tp=self.right).wait_recv()

    def drain(self, k):
        for copy in self.first(k) + self.second(k):
            copy.wait_send()


class Reduce:
    def __init__(self, piece, in_left, in_right, out_right, out_left, mid_left, mid_right, sems):
        self.piece, self.sems = piece, sems
        self.in_left, self.in_right = in_left, in_right
        self.out_right, self.out_left = out_right, out_left
        self.mid_left, self.mid_right = mid_left, mid_right
        self.here, self.right, self.left = ring(4)
        self.far = lax.rem(self.here + 2, 4)

    def first(self, k):
        return (
            remote(self.piece(k, self.far, 0), self.in_left.at[k], self.sems.at[k, 0], self.sems.at[k, 1], tp=self.right),
            remote(self.piece(k, self.far, 1), self.in_right.at[k], self.sems.at[k, 2], self.sems.at[k, 3], tp=self.left),
        )

    def second(self, k):
        return (
            remote(self.out_right.at[k], self.mid_left.at[k], self.sems.at[k, 4], self.sems.at[k, 5], tp=self.right),
            remote(self.out_left.at[k], self.mid_right.at[k], self.sems.at[k, 6], self.sems.at[k, 7], tp=self.left),
        )

    def start(self, k):
        for copy in self.first(k):
            copy.start()

    def middle(self, k):
        by_left, by_right = self.first(k)
        to_right, to_left = self.second(k)
        by_left.wait_recv()
        summed = self.piece(k, self.right, 0)[...].astype(F32) + self.in_left[k].astype(F32)
        self.out_right[k, 0] = summed.astype(BF)
        self.out_right[k, 1] = self.piece(k, self.right, 1)[...]
        to_right.start()
        by_right.wait_recv()
        summed = self.piece(k, self.left, 1)[...].astype(F32) + self.in_right[k].astype(F32)
        self.out_left[k, 1] = summed.astype(BF)
        self.out_left[k, 0] = self.piece(k, self.left, 0)[...]
        to_left.start()

    def finish(self, k):
        for copy in self.second(k):
            copy.wait_recv()
        return [
            self.piece(k, self.here, half)[...].astype(F32)
            + self.mid_left[k, half].astype(F32)
            + self.mid_right[k, half].astype(F32)
            for half in (0, 1)
        ]

    def drain(self, k):
        for copy in self.first(k) + self.second(k):
            copy.wait_send()


def reduce_scratch(groups, rows, lanes):
    return [pltpu.VMEM((groups, rows, lanes), BF)] * 2 + [
        pltpu.VMEM((groups, 2, rows, lanes), BF)
    ] * 4


def sems(*dims):
    return pltpu.SemaphoreType.DMA(dims)


def return_parts(batch_size, lanes, source, out, stage, buffers, send, arrive, sum_sems, ring_sems):
    me = lax.axis_index("exp")
    position = place_index(me)
    here = lax.axis_index("tp")
    part = batch_size // GROUPS
    mine = pl.ds(pl.multiple_of(here * lanes, 128), lanes)
    own = pl.ds(pl.multiple_of(position * 16, 16), 16)

    def leaving(k):
        return lax.rem(position // part + GROUPS - k, GROUPS) * (part * 16)

    def arriving(k):
        return lax.rem(position // part + k, GROUPS) * (part * 16)

    def span(ref, base, who, begin, rows):
        spot = pl.ds(pl.multiple_of(base + begin, 16), rows)
        return ref.at[spot, pl.ds(pl.multiple_of(who * lanes, 128), lanes)]

    half_rows = part * 8
    reduce = Reduce(
        lambda k, who, half: span(source, leaving(k), who, half * half_rows, half_rows),
        *buffers,
        sum_sems,
    )
    gather = Gather(
        lambda k, who: span(out, arriving(k), who, 0, part * 16),
        lambda k, who, half: span(out, arriving(k), who, half * half_rows, half_rows),
        ring_sems,
    )

    def scatter(k):
        first, second = reduce.finish(k)
        spot = pl.multiple_of(leaving(k), 16)
        stage[pl.ds(spot, half_rows), :] = first.astype(BF)
        stage[pl.ds(pl.multiple_of(spot + half_rows, 16), half_rows), :] = second.astype(BF)
        if k == 0:
            out[own, mine] = stage[own, :]

        def step(j, carry):
            group = lax.rem(position // part + GROUPS - k, GROUPS)
            peer = group * part + lax.rem(position + j, part)
            rows = pl.ds(pl.multiple_of(peer * 16, 16), 16)
            remote(
                stage.at[rows, :], out.at[own, mine], send.at[0], arrive.at[k], exp=device_at(peer)
            ).start()
            return carry

        lax.fori_loop(1 if k == 0 else 0, part, step, 0)

    def collect(k):
        rows = (part - 1 if k == 0 else part) * 16
        block = span(out, arriving(k), here, 0, rows)
        remote(block, block, send.at[0], arrive.at[k], exp=me).wait_recv()
        gather.start(k)

    def drain():
        whole = stage.at[pl.ds(0, (batch_size - 1) * 16), :]
        remote(whole, whole, send.at[0], arrive.at[0], exp=me).wait_send()
        for k in range(GROUPS):
            reduce.drain(k)
            gather.drain(k)

    return reduce, gather, scatter, collect, drain


def return_scratch(batch_size, lanes):
    return [
        pltpu.VMEM((batch_size * 16, lanes), BF),
        *reduce_scratch(GROUPS, batch_size * 8 // GROUPS, lanes),
        sems(1),
        sems(GROUPS),
        sems(GROUPS, 8),
        sems(GROUPS, 8),
    ]


def final_body(
    batch_size, capacity, part_in, large, small, returned_far, slots, gates, residual_far,
    summed, large_out, small_out, lines, output_far,
    large_side, small_side, large_in, small_in, returned, residual, output, far_sems, *rest,
):
    buffers, (send, arrive, line_sems, sum_sems, ring_sems) = rest[:6], rest[6:]
    signals = greet(4, batch_size, opposite=True, same_core=True)
    me = lax.axis_index("exp")
    core = lax.rem(me, 2)
    sibling = me + 1 - 2 * core
    here, right, left = ring(4)
    tokens, width = part_in.shape
    chunk = tokens // 4
    groups = buffers[0].shape[0]
    half_rows = chunk // groups // 2
    peers, tall, wide = large_in.shape
    half_lanes = small.shape[1] // 2
    small_across = half_lanes // 128

    def spot(ref, who, k, begin, count):
        first = who * chunk + k * (2 * half_rows) + begin
        return ref.at[pl.ds(pl.multiple_of(first, 16), count), :]

    reduce = Reduce(
        lambda k, who, half: spot(part_in, who, k, half * half_rows, half_rows), *buffers, sum_sems
    )
    gather = Gather(
        lambda k, who: spot(summed, who, k, 0, 2 * half_rows),
        lambda k, who, half: spot(summed, who, k, half * half_rows, half_rows),
        ring_sems,
    )

    def large_half(ref, side):
        return ref.at[:, pl.ds(pl.multiple_of(side * wide, 128), wide)]

    def small_half(ref, side):
        return ref.at[:, pl.ds(pl.multiple_of(side * half_lanes, 128), half_lanes)]

    def large_rows(ref, who):
        return ref.at[pl.ds(pl.multiple_of(who * tall, 16), tall), :]

    def small_rows(ref, who):
        down = pl.ds(pl.multiple_of(who // small_across * 16, 16), 16)
        return ref.at[down, pl.ds(pl.multiple_of(lax.rem(who, small_across) * 128, 128), 128)]

    def large_final(who):
        down = pl.ds(pl.multiple_of(who * tall, 16), tall)
        return large_out.at[down, pl.ds(pl.multiple_of(core * wide, 128), wide)]

    def small_final(who):
        down = pl.ds(pl.multiple_of(who // small_across * 16, 16), 16)
        lane = core * half_lanes + lax.rem(who, small_across) * 128
        return small_out.at[down, pl.ds(pl.multiple_of(lane, 128), 128)]

    late = [
        pltpu.make_async_copy(returned_far, returned, far_sems.at[0]),
        pltpu.make_async_copy(residual_far, residual, far_sems.at[1]),
    ]
    for copy in late:
        copy.start()
    meet(signals)
    pair = [
        remote(large_half(large, 1 - core), large_side, send.at[0], arrive.at[0], exp=sibling),
        remote(small_half(small, 1 - core), small_side, send.at[1], arrive.at[1], exp=sibling),
    ]
    for copy in pair:
        copy.start()
    for k in range(groups):
        reduce.start(k)
    for copy in pair:
        copy.wait_recv()
    both = large_side[...].astype(F32) + large_half(large, core)[...].astype(F32)
    large_side[...] = both.astype(BF)
    both = small_side[...].astype(F32) + small_half(small, core)[...].astype(F32)
    small_side[...] = both.astype(BF)
    mine = me // 2

    def scatter(step, carry):
        peer = lax.rem(mine + step, peers)
        to = peer * 2 + core
        remote(large_rows(large_side, peer), large_in.at[step], send.at[2], arrive.at[2], exp=to).start()
        remote(small_rows(small_side, peer), small_in.at[step], send.at[3], arrive.at[3], exp=to).start()
        return carry

    lax.fori_loop(1, peers, scatter, 0)
    large_in[0] = large_rows(large_side, mine)[...]
    small_in[0] = small_rows(small_side, mine)[...]
    for k in range(groups):
        reduce.middle(k)

    experts = batch_size
    body = 16 * experts
    place = place_of(slots[...], experts, capacity, 5 * body // 2)
    for copy in late:
        copy.wait()
    token_rows = fetch(place, returned, width, experts)
    output[...] = (residual[...] + gates[...] * token_rows).astype(BF)
    kept = pltpu.make_async_copy(output, output_far, far_sems.at[2])
    kept.start()

    large_rest = large_in.at[pl.ds(1, peers - 1)]
    small_rest = small_in.at[pl.ds(1, peers - 1)]
    remote(large_rest, large_rest, send.at[2], arrive.at[2], exp=me).wait_recv()
    remote(small_rest, small_rest, send.at[3], arrive.at[3], exp=me).wait_recv()

    def add(step, carry):
        return carry[0] + large_in[step].astype(F32), carry[1] + small_in[step].astype(F32)

    zero = (jnp.zeros((tall, wide), F32), jnp.zeros((16, 128), F32))
    large_sum, small_sum = lax.fori_loop(0, peers, add, zero)
    large_final(mine)[...] = large_sum.astype(BF)
    small_final(mine)[...] = small_sum.astype(BF)

    def spread(step, carry):
        to = lax.rem(mine + step, peers) * 2 + core
        own = large_final(mine)
        remote(own, own, send.at[4], arrive.at[4], exp=to).start()
        own = small_final(mine)
        remote(own, own, send.at[5], arrive.at[5], exp=to).start()
        return carry

    lax.fori_loop(1, peers, spread, 0)
    for k in range(groups):
        pieces = reduce.finish(k)
        for half in (0, 1):
            target = spot(summed, here, k, half * half_rows, half_rows)
            target[...] = pieces[half].astype(BF)
        gather.start(k)
    remote(large_rest, large_rest, send.at[4], arrive.at[4], exp=me).wait_recv()
    remote(small_rest, small_rest, send.at[5], arrive.at[5], exp=me).wait_recv()
    back = []
    for i, half in ((6, large_half(large_out, core)), (7, small_half(small_out, core))):
        back.append(remote(half, half, send.at[i], arrive.at[i], exp=sibling))
    for copy in back:
        copy.start()
    for k in range(groups):
        gather.forward(k)
    for i, half in ((6, large_half(large_out, 1 - core)), (7, small_half(small_out, 1 - core))):
        remote(half, half, send.at[i], arrive.at[i], exp=sibling).wait_recv()
    line = small_out.at[pl.ds(32, 16), :]
    others = (right, left, lax.rem(here + 2, 4))
    copies = [
        remote(line, lines.at[i], line_sems.at[i, 0], line_sems.at[i, 1], tp=side)
        for i, side in enumerate(others)
    ]
    for copy in copies:
        copy.start()
    for k in range(groups):
        gather.finish(k)
    for copy in copies:
        copy.wait_recv()
    kept.wait()
    for copy in copies + pair + back:
        copy.wait_send()
    for i, ref in ((2, large_rest), (3, small_rest), (4, large_rest), (5, small_rest)):
        remote(ref, ref, send.at[i], arrive.at[0], exp=me).wait_send()
    for k in range(groups):
        reduce.drain(k)
        gather.drain(k)


def finish_body(
    summed, rows, residual_grad, gain, large, small, lines, output, in_grad, out_grad,
    input_grad, query_grad, key_grad, value_grad, proj_grad, router_grad, gain_grad, first_grad,
    table_grad, output_last, in_grad_last, out_grad_last, far_sems,
):
    passed = [
        pltpu.make_async_copy(source, target, far_sems.at[i])
        for i, (source, target) in enumerate(
            ((output, output_last), (in_grad, in_grad_last), (out_grad, out_grad_last))
        )
    ]

    @pl.when(pl.program_id(0) == 0)
    def _():
        for copy in passed:
            copy.start()

    inputs = rows[...].astype(F32)
    scale = inverse_rms(inputs)
    scaled = summed[...].astype(F32) * gain[...]
    middle = jnp.mean(scaled * inputs, axis=-1, keepdims=True)
    input_grad[...] = (
        residual_grad[...] + scale * scaled - inputs * (scale * scale * scale * middle)
    )

    @pl.when(pl.program_id(0) == 0)
    def _():
        high, width = query_grad.shape
        for i, ref in enumerate((query_grad, key_grad, value_grad, proj_grad)):
            ref[...] = large[i * high : (i + 1) * high, :].astype(F32)
        router_grad[...] = small[0 : router_grad.shape[0], 0:width].astype(F32)
        total = small[32:48, 0:width].astype(F32)
        gain_grad[...] = total[0:1]
        table_grad[...] = small[48:64, 0:128].astype(F32)[0:3, 0:32]
        for i in range(3):
            total = total + lines[i][:, 0:width].astype(F32)
        first_grad[...] = total[8:9]

    @pl.when(pl.program_id(0) == pl.num_programs(0) - 1)
    def _():
        for copy in passed:
            copy.wait()


def head_mask(head, head_width, width):
    lane = lax.broadcasted_iota(jnp.int32, (1, width), 1)
    return jnp.where(lane // head_width == head, 1.0, 0.0)


def fill_bias(bias, buckets, table):
    heads, block, width = bias.shape
    padded = buckets.shape[1]
    number = lax.broadcasted_iota(jnp.int32, (table.shape[1], padded), 0)
    hot = jnp.where(buckets[...] == number, 1.0, 0.0)
    offsets = jnp.dot(
        table[...], hot, precision=lax.Precision.HIGHEST, preferred_element_type=F32
    )
    for head in range(heads):
        spread = jnp.broadcast_to(offsets[head : head + 1, :], (block, padded))
        rolled = pltpu.roll(spread, padded - (block - 1), 1, stride=1, stride_axis=0)
        bias[head] = rolled[:, :width]


def attend_body(
    head_width, capacity,
    rows, gain, query_w, key_w, value_w, proj, buckets, table, second_gain, router_w, ids_row,
    mixed_far, normed_far, query_far, query_t_far, key_far, key_t_far, value_t_far, logsum_far,
    residual, hidden, probs, slots, slots_row, gates,
    mixed, normed, query, query_t, key, key_t, value_t, logsum,
    mixed_all, proj_all, bias, value, ring_sems, proj_sems, pair_sems, far_sems,
):
    heads = bias.shape[0]
    tokens = rows.shape[0]
    width = query.shape[1]
    blocks = tokens // BLOCK
    pairs = blocks // 2
    signals = greet(4, 0, same_core=True)
    here = lax.axis_index("tp")
    me = lax.axis_index("exp")
    core = lax.rem(me, 2)
    sibling = me + 1 - 2 * core
    inputs = rows[...].astype(F32)
    low = (inputs * inverse_rms(inputs) * gain[...]).astype(BF)
    normed[...] = low
    proj_all[here] = proj[...]
    meet(signals)
    gather = Gather(
        lambda k, who: mixed_all.at[who, pl.ds(pl.multiple_of(k * BLOCK, BLOCK), BLOCK), :],
        lambda k, who, half: mixed_all.at[
            who, pl.ds(pl.multiple_of(k * BLOCK + half * (BLOCK // 2), 16), BLOCK // 2), :
        ],
        ring_sems,
    )
    half_rows = proj.shape[0] // 2

    def proj_part(who, side, begin, count):
        spot = pl.multiple_of(side * half_rows + begin, 16)
        return proj_all.at[who, pl.ds(spot, count), :]

    weights_gather = Gather(
        lambda k, who: proj_part(who, core, 0, half_rows),
        lambda k, who, half: proj_part(who, core, half * (half_rows // 2), half_rows // 2),
        proj_sems,
    )

    def to_sibling(i, who, side):
        part = proj_part(who, side, 0, half_rows)
        return remote(part, part, pair_sems.at[i, 0], pair_sems.at[i, 1], exp=sibling)

    foreign = (weights_gather.left, weights_gather.right, weights_gather.far)
    weights_gather.start(0)
    query[...] = cols_product(low, query_w[...]).astype(BF)
    key[...] = cols_product(low, key_w[...]).astype(BF)
    value[...] = cols_product(low, value_w[...]).astype(BF)
    query_t[...] = cols_product(query_w[...], low).astype(BF)
    key_t[...] = cols_product(key_w[...], low).astype(BF)
    value_t[...] = cols_product(value_w[...], low).astype(BF)
    def keep(ref, far, i):
        copy = pltpu.make_async_copy(ref, far, far_sems.at[i])
        copy.start()
        return [copy]

    early_copies = []
    for i, (ref, far) in enumerate(
        (
            (normed, normed_far), (query, query_far), (query_t, query_t_far), (key, key_far),
            (key_t, key_t_far), (value_t, value_t_far),
        )
    ):
        early_copies += keep(ref, far, i)
    fill_bias(bias, buckets, table)
    weights_gather.forward(0)
    for i in (0, 1):
        to_sibling(i, foreign[i], core).start()

    def step(pair, carry):
        for side in (0, 1):
            block = pair + side * pairs
            first = pl.multiple_of(block * BLOCK, BLOCK)
            shift = pl.multiple_of((blocks - 1 - block) * BLOCK, BLOCK)
            query_rows = query[pl.ds(first, BLOCK), :]
            total = jnp.zeros((BLOCK, width), F32)
            for head in range(heads):
                mask = head_mask(head, head_width, width)
                scores = product(query_rows * mask.astype(BF), key_t[...])
                scores = scores + bias[head, :, pl.ds(shift, tokens)]
                highest = jnp.max(scores, axis=-1, keepdims=True)
                weights = jnp.exp(scores - highest)
                summed = jnp.sum(weights, axis=-1, keepdims=True)
                part = product(weights.astype(BF), value[...]) / summed
                total = total + part * mask
                logsum[pl.ds(first, BLOCK), head : head + 1] = highest + jnp.log(summed)
            spot = pl.ds(pl.multiple_of(pair * BLOCK, BLOCK), BLOCK)
            mixed[pl.ds(first, BLOCK), :] = total.astype(BF)
            mixed_all[here, spot, side * width : (side + 1) * width] = total.astype(BF)
        gather.start(pair)

        @pl.when(pair > 0)
        def _():
            gather.forward(pair - 1)

        return carry

    lax.fori_loop(0, pairs // 2, step, 0)
    weights_gather.finish(0)
    to_sibling(2, foreign[2], core).start()
    lax.fori_loop(pairs // 2, pairs, step, 0)
    gather.forward(pairs - 1)
    out_copies = keep(mixed, mixed_far, 6) + keep(logsum, logsum_far, 7)
    experts = router_w.shape[0]
    number = lax.broadcasted_iota(jnp.int32, (experts, tokens), 0)
    hot_t = ids_row[...] == number
    ones_t = jnp.where(hot_t, 1.0, 0.0)
    across = lax.broadcasted_iota(jnp.int32, (tokens, tokens), 0)
    along = lax.broadcasted_iota(jnp.int32, (tokens, tokens), 1)
    upper = jnp.where(across <= along, 1.0, 0.0).astype(BF)
    counts_t = product(ones_t.astype(BF), upper)
    position_t = jnp.sum(jnp.where(hot_t, counts_t - 1.0, 0.0), axis=0, keepdims=True)
    line = ids_row[...] * capacity + position_t.astype(jnp.int32)
    slots_row[...] = line
    slots[...] = jnp.broadcast_to(line.astype(F32), (128, tokens)).T[:, 0:1].astype(jnp.int32)
    for i in range(3):
        to_sibling(i, foreign[i], 1 - core).wait_recv()
    for k in range(pairs):
        gather.finish(k)
        halves = [pl.ds(side * (tokens // 2) + k * BLOCK, BLOCK) for side in (0, 1)]
        res = jnp.concatenate([rows[spot, :] for spot in halves], axis=0).astype(F32)
        for i in range(mixed_all.shape[0]):
            both = mixed_all[i, k * BLOCK : (k + 1) * BLOCK, :]
            both = jnp.concatenate([both[:, :width], both[:, width:]], axis=0)
            res = res + product(both, proj_all[i])
        low = (res * inverse_rms(res) * second_gain[...]).astype(BF)
        logits = cols_product(low, router_w[...])
        shifted = jnp.exp(logits - jnp.max(logits, axis=-1, keepdims=True))
        chances = shifted / jnp.sum(shifted, axis=-1, keepdims=True)
        for side in (0, 1):
            spot, part = halves[side], slice(side * BLOCK, (side + 1) * BLOCK)
            residual[spot, :] = res[part]
            hidden[spot, :] = low[part]
            probs[spot, :] = chances[part]
            expert = lax.broadcasted_iota(jnp.int32, (BLOCK, experts), 1)
            hot = slots[spot, :] // capacity == expert
            chosen = jnp.sum(jnp.where(hot, chances[part], 0.0), axis=1, keepdims=True)
            gates[spot, :] = chosen
    for i in range(3):
        to_sibling(i, foreign[i], core).wait_send()
    for copy in early_copies + out_copies:
        copy.wait()
    weights_gather.drain(0)
    for k in range(pairs):
        gather.drain(k)


def pack_third(third, experts):
    half = third.shape[1] // 2
    split = third.reshape(experts, 8, 2 * half)
    split = jnp.concatenate([split[:, :, :half], split[:, :, half:]], axis=1)
    return split.reshape(experts * 16, half)


def unpack_third(tail, runs):
    half = tail.shape[1]
    split = tail.astype(F32).reshape(runs, 16, half)
    return jnp.concatenate([split[:, :8], split[:, 8:]], axis=2).reshape(runs * 8, 2 * half)


def slot_of_row(row, experts, capacity):
    body = 16 * experts
    first = device_at(row // 16) * capacity + row % 16
    second = device_at((row - body) // 16) * capacity + 16 + (row - body) % 16
    third = device_at((row - 2 * body) // 8) * capacity + 32 + (row - 2 * body) % 8
    return jnp.where(row < body, first, jnp.where(row < 2 * body, second, third))


def moe_body(
    batch_size, capacity, lanes, back_lanes,
    hidden, gates, slots_row, cotangent, weight_in, weight_out,
    value, back_sum, in_grad_far, out_grad_far,
    leave, arrived, back, in_grad, out_grad, far_sems, stage, *rest,
):
    buffers, (send_back, arrive_back, sum_sems, back_sems) = rest[:6], rest[6:10]
    send, arrive, arrive_tail, ring_sems = rest[10:]
    signals = greet(4, batch_size)
    me = lax.axis_index("exp")
    here = lax.axis_index("tp")
    position = place_index(me)
    part = batch_size // GROUPS
    zone_rows = part * 16
    width = hidden.shape[1]
    slots_t = slots_row[...]
    low = hidden[...]
    gate = gates[...]
    grads = (gate * cotangent[...].astype(F32)).astype(BF)
    meet(signals)

    mine = pl.ds(pl.multiple_of(here * lanes, 128), lanes)
    tail = pl.ds(4 * lanes, leave.shape[2] - 4 * lanes)
    own = pl.ds(pl.multiple_of(position * 16, 16), 16)
    place_row = lax.broadcasted_iota(jnp.int32, (zone_rows * 5 // 2, 1), 0)
    third = place_row - 2 * zone_rows
    member = jnp.where(third < 0, place_row % zone_rows // 16, third // 8)
    inside = jnp.where(
        place_row < zone_rows,
        place_row % 16,
        jnp.where(third < 0, 16 + place_row % 16, 32 + third % 8),
    )
    for k in range(GROUPS):
        zone = lax.rem(position // part + k, GROUPS)
        wanted = device_at(zone * part + member) * capacity + inside
        place = jnp.where(wanted == slots_t, 1.0, 0.0).astype(BF)
        spot = pl.ds(pl.multiple_of(zone * zone_rows, 16), zone_rows)
        for array, source in ((0, low), (1, grads)):
            picked = product(place, source)
            leave[array, spot, 0:width] = picked[:zone_rows].astype(BF)
            leave[array, spot, width : 2 * width] = picked[zone_rows : 2 * zone_rows].astype(BF)
            packed = pack_third(picked[2 * zone_rows :], part)
            leave[array, spot, 2 * width :] = packed.astype(BF)
        if k == 0:
            arrived[:, own, mine] = leave[:, own, mine]
            arrived[:, own, tail] = leave[:, own, tail]
        for columns, sent, landed in ((mine, 0, arrive), (tail, 1, arrive_tail)):

            def step(j, carry):
                peer = zone * part + lax.rem(position + j, part)
                block = pl.ds(pl.multiple_of(peer * 16, 16), 16)
                remote(
                    leave.at[:, block, columns], arrived.at[:, own, columns],
                    send.at[sent], landed.at[k], exp=device_at(peer),
                ).start()
                return carry

            lax.fori_loop(1 if k == 0 else 0, part, step, 0)

    def arriving(k):
        return lax.rem(position // part + GROUPS - k, GROUPS) * zone_rows

    def span(k, who, count, array=slice(None)):
        spot = pl.ds(pl.multiple_of(arriving(k), 16), count)
        return arrived.at[array, spot, pl.ds(pl.multiple_of(who * lanes, 128), lanes)]

    gather = Gather(
        lambda k, who: span(k, who, zone_rows),
        lambda k, who, side: span(k, who, zone_rows, pl.ds(side, 1)),
        ring_sems,
    )

    def quarter(k):
        block = span(k, here, zone_rows - 16 if k == 0 else zone_rows)
        remote(block, block, send.at[0], arrive.at[k], exp=me).wait_recv()
        gather.start(k)

    def whole(k):
        gather.finish(k)
        count = zone_rows - 16 if k == 0 else zone_rows
        block = arrived.at[:, pl.ds(pl.multiple_of(arriving(k), 16), count), tail]
        remote(block, block, send.at[1], arrive_tail.at[k], exp=me).wait_recv()

    def experts_on(k):
        spot = pl.ds(pl.multiple_of(arriving(k), 16), zone_rows)

        def rows_of(array):
            last = unpack_third(arrived[array, spot, 2 * width :], part).astype(BF)
            first = [arrived[array, spot, 0:width], arrived[array, spot, width : 2 * width]]
            return jnp.concatenate(first + [last], axis=0)

        x, g = rows_of(0), rows_of(1)
        pre = product(x, weight_in[...])
        inner = jnp.tanh(gelu_root * (pre + gelu_cube * pre * pre * pre))
        act = (0.5 * pre * (1.0 + inner)).astype(BF)
        slope = 0.5 * (1.0 + inner) + 0.5 * pre * (1.0 - inner * inner) * (
            gelu_root * (1.0 + 3.0 * gelu_cube * pre * pre)
        )
        act_grad = cols_product(g, weight_out[...])
        pre_grad = (act_grad * slope).astype(BF)
        rows_back = cols_product(pre_grad, weight_in[...])
        out = product(act, weight_out[...])
        dots = jnp.sum(out * g.astype(F32), axis=1, keepdims=True)
        lane = lax.broadcasted_iota(jnp.int32, (1, 128), 1)
        marks = jnp.where(lane == 0, dots[:zone_rows], 0.0)
        marks = marks + jnp.where(lane == 1, dots[zone_rows : 2 * zone_rows], 0.0)
        last = jnp.where(lane == 2, dots[2 * zone_rows :], 0.0).reshape(part, 8, 128)
        last = jnp.concatenate([last, jnp.zeros_like(last)], axis=1).reshape(zone_rows, 128)
        for ref, result, extra in (
            (back, rows_back, marks + last),
            (value, out, jnp.zeros((zone_rows, 128), F32)),
        ):
            ref[spot, 0:width] = result[:zone_rows].astype(BF)
            ref[spot, width : 2 * width] = result[zone_rows : 2 * zone_rows].astype(BF)
            packed = pack_third(result[2 * zone_rows :], part)
            ref[spot, 2 * width : 2 * width + width // 2] = packed.astype(BF)
            ref[spot, 2 * width + width // 2 :] = extra.astype(BF)
        return x, g, act, pre_grad

    def weights_on(k, held):
        x, g, act, pre_grad = held
        if k == 0:
            out_grad[...] = rows_product(act, g)
            in_grad[...] = rows_product(x, pre_grad)
        else:
            out_grad[...] += rows_product(act, g)
            in_grad[...] += rows_product(x, pre_grad)

    reduce, gather_back, scatter, collect, drain = return_parts(
        batch_size, back_lanes, back, back_sum, stage, buffers,
        send_back, arrive_back, sum_sems, back_sems,
    )

    def work(k):
        whole(k)
        held = experts_on(k)
        reduce.start(k)
        weights_on(k, held)

    quarter(0)
    quarter(1)
    gather.forward(0)
    quarter(2)
    gather.forward(1)
    work(0)
    quarter(3)
    gather.forward(2)
    reduce.middle(0)
    work(1)
    gather.forward(3)
    reduce.middle(1)
    scatter(0)
    work(2)
    reduce.middle(2)
    scatter(1)
    collect(0)
    work(3)
    far_copies = [
        pltpu.make_async_copy(in_grad, in_grad_far, far_sems.at[0]),
        pltpu.make_async_copy(out_grad, out_grad_far, far_sems.at[1]),
    ]
    for copy in far_copies:
        copy.start()
    reduce.middle(3)
    scatter(2)
    collect(1)
    gather_back.forward(0)
    scatter(3)
    collect(2)
    gather_back.forward(1)
    collect(3)
    gather_back.forward(2)
    gather_back.forward(3)
    for k in range(GROUPS):
        gather_back.finish(k)
    for copy in far_copies:
        copy.wait()
    drain()
    for k in range(GROUPS):
        gather.drain(k)
    for columns, sent in ((mine, 0), (tail, 1)):
        block = leave.at[:, pl.ds(0, (batch_size - 1) * 16), columns]
        remote(block, block, send.at[sent], arrive.at[0], exp=me).wait_send()


def place_of(slots, experts, capacity, rows):
    number = slot_of_row(lax.broadcasted_iota(jnp.int32, (1, rows), 1), experts, capacity)
    return jnp.where(slots == number, 1.0, 0.0).astype(BF)


def fetch(place, ref, width, experts):
    body = 16 * experts
    picked = product(place[:, :body], ref[:, :width])
    picked = picked + product(place[:, body : 2 * body], ref[:, width : 2 * width])
    tail = unpack_third(ref[:, 2 * width : 2 * width + width // 2], experts).astype(BF)
    return picked + product(place[:, 2 * body :], tail)


def backward_body(
    batch_size, capacity, head_width, lanes,
    value_in, back, slots, residual, hidden, probs, gain, router_w, cotangent, mixed, proj,
    normed_far, query_far, query_t_far, key_far, key_t_far, value_t_far, logsum_far,
    query_w, key_w, value_w, buckets, table, rows_far,
    returned, residual_grad_far, normed_part, large, small,
    normed, query, query_t, key, key_t, value_t, logsum, rows, residual_grad, far_sems,
    grad, grad_t, bias, sums, query_back, key_acc, value_acc, stage, *rest,
):
    buffers, (send, arrive, sum_sems, ring_sems) = rest[:6], rest[6:]
    signals = greet(4, batch_size)
    reduce, gather, scatter, collect, drain = return_parts(
        batch_size, lanes, value_in, returned, stage, buffers, send, arrive, sum_sems, ring_sems
    )
    tokens, full = residual.shape
    experts = router_w.shape[0]
    body = 16 * experts
    heads = bias.shape[0]
    width = query.shape[1]
    blocks = tokens // BLOCK
    late = [
        pltpu.make_async_copy(far, ref, far_sems.at[i])
        for i, (far, ref) in enumerate(
            (
                (query_far, query), (query_t_far, query_t), (key_far, key), (key_t_far, key_t),
                (value_t_far, value_t), (logsum_far, logsum), (normed_far, normed),
                (rows_far, rows),
            )
        )
    ]
    for copy in late:
        copy.start()
    place = place_of(slots[...], experts, capacity, 5 * body // 2)
    meet(signals)
    for k in range(GROUPS):
        reduce.start(k)

    marks = back[:, 2 * full + full // 2 :]
    lane = lax.broadcasted_iota(jnp.int32, (1, 128), 1)
    tail = marks.astype(F32).reshape(experts, 16, 128)[:, :8].reshape(experts * 8, 128).astype(BF)
    dots = jnp.where(lane == 0, product(place[:, :body], marks), 0.0)
    dots = dots + jnp.where(lane == 1, product(place[:, body : 2 * body], marks), 0.0)
    dots = dots + jnp.where(lane == 2, product(place[:, 2 * body :], tail), 0.0)
    weighted = jnp.sum(dots, axis=1, keepdims=True)
    hot = slots[...] // capacity == lax.broadcasted_iota(jnp.int32, (tokens, experts), 1)
    logit_grad = (jnp.where(hot, weighted, 0.0) - probs[...] * weighted).astype(BF)
    router_grad = rows_product(logit_grad, hidden[...])
    hidden_grad = fetch(place, back, full, experts) + product(logit_grad, router_w[...])
    for k in range(GROUPS // 2):
        reduce.middle(k)
    res = residual[...]
    scale = inverse_rms(res)
    gain_grad = jnp.sum(hidden_grad * res * scale, axis=0, keepdims=True)
    scaled = gain[...] * hidden_grad
    middle = jnp.mean(scaled * res, axis=-1, keepdims=True)
    total = cotangent[...].astype(F32) + scale * scaled - res * (scale * scale * scale * middle)
    low = total.astype(BF)
    residual_grad[...] = total
    kept = pltpu.make_async_copy(residual_grad, residual_grad_far, far_sems.at[len(late)])
    kept.start()
    for k in range(GROUPS // 2, GROUPS):
        reduce.middle(k)
    large[3 * width :, :] = rows_product(mixed[...], low).astype(BF)
    grad[...] = cols_product(low, proj[...]).astype(BF)
    grad_t[...] = cols_product(proj[...], low).astype(BF)

    for copy in late:
        copy.wait()
    fill_bias(bias, buckets, table)
    sums[...] = jnp.zeros(sums.shape, F32)
    key_acc[...] = jnp.zeros(key_acc.shape, F32)
    value_acc[...] = jnp.zeros(value_acc.shape, F32)

    def step(block, carry):
        first = pl.multiple_of(block * BLOCK, BLOCK)
        shift = pl.multiple_of((blocks - 1 - block) * BLOCK, BLOCK)
        query_rows = query[pl.ds(first, BLOCK), :]
        grad_rows = grad[pl.ds(first, BLOCK), :]
        acc = jnp.zeros((BLOCK, width), F32)
        for head in range(heads):
            mask = head_mask(head, head_width, width)
            span = slice(head * head_width, (head + 1) * head_width)
            scores = product(query_rows * mask.astype(BF), key_t[...])
            scores = scores + bias[head, :, pl.ds(shift, tokens)]
            chances = jnp.exp(scores - logsum[pl.ds(first, BLOCK), head : head + 1])
            prob_grad = product(grad_rows * mask.astype(BF), value_t[...])
            centre = jnp.sum(chances * prob_grad, axis=-1, keepdims=True)
            score_grad = chances * (prob_grad - centre)
            score_low = score_grad.astype(BF)
            sums[head, :, pl.ds(shift, tokens)] += score_grad
            acc = acc + product(score_low, key[...]) * mask
            key_acc[span, :] += product(query_t[span, pl.ds(first, BLOCK)], score_low)
            value_acc[span, :] += product(grad_t[span, pl.ds(first, BLOCK)], chances.astype(BF))
        query_back[pl.ds(first, BLOCK), :] = acc.astype(BF)
        return carry

    def run(begin, end):
        lax.fori_loop(begin, end, step, 0)

    run(0, 1)
    scatter(0)
    run(1, 2)
    scatter(1)
    run(2, 3)
    scatter(2)
    collect(0)
    run(3, 4)
    scatter(3)
    collect(1)
    gather.forward(0)
    run(4, 5)
    collect(2)
    gather.forward(1)
    run(5, 6)
    collect(3)
    gather.forward(2)
    run(6, 7)
    gather.forward(3)
    run(7, blocks)
    backs = [query_back[...], key_acc[...].T.astype(BF), value_acc[...].T.astype(BF)]
    backs_t = [query_back[...].astype(F32).T.astype(BF)]
    backs_t += [key_acc[...].astype(BF), value_acc[...].astype(BF)]
    part = product(backs[0], query_w[...])
    part = part + product(backs[1], key_w[...]) + product(backs[2], value_w[...])
    normed_part[...] = part.astype(BF)
    for i in range(3):
        large[i * width : (i + 1) * width, :] = product(backs_t[i], normed[...]).astype(BF)
    inputs = rows[...].astype(F32)
    line = jnp.sum(part * inputs * inverse_rms(inputs), axis=0, keepdims=True)
    small[...] = jnp.zeros(small.shape, BF)
    small[0:experts, 0:full] = router_grad.astype(BF)
    row = lax.broadcasted_iota(jnp.int32, (16, 1), 0)
    pair = jnp.where(row == 0, gain_grad, jnp.where(row == 8, line, 0.0))
    small[32:48, 0:full] = pair.astype(BF)

    padded = buckets.shape[1]
    lines = []
    for head in range(heads):
        wide = jnp.concatenate(
            [sums[head], jnp.zeros((BLOCK, padded - sums.shape[2]), F32)], axis=1
        )
        gathered = jnp.zeros((8, padded), F32)
        for piece_at in range(0, BLOCK, 8):
            piece = wide[piece_at : piece_at + 8, :]
            gathered = gathered + pltpu.roll(piece, (BLOCK - 1 - piece_at) % padded, 1)
        line = jnp.zeros((1, padded), F32)
        for i in range(8):
            line = line + pltpu.roll(gathered, (padded - i) % padded, 1)[i : i + 1, :]
        lines.append(line)
    number = lax.broadcasted_iota(jnp.int32, (table.shape[1], padded), 0)
    matches = jnp.where(buckets[...] == number, 1.0, 0.0)
    stacked = jnp.concatenate(lines + [jnp.zeros((16 - heads, padded), F32)], axis=0)
    sums_of = lax.dot_general(
        stacked,
        matches,
        (((1,), (1,)), ((), ())),
        precision=lax.Precision.HIGHEST,
        preferred_element_type=F32,
    )
    blank = jnp.zeros((16, 128 - table.shape[1]), F32)
    small[48:64, 0:128] = jnp.concatenate([sums_of, blank], axis=1).astype(BF)
    for k in range(GROUPS):
        gather.finish(k)
    kept.wait()
    drain()


def per_device(
    layer_in, expert_ids, rel_buckets, first_gain, query_weight, key_weight, value_weight,
    proj_weight, rel_table, second_gain, router_weight, expert_in, expert_out, cotangent,
):
    tokens, width = layer_in.shape
    heads = rel_table.shape[1]
    here = query_weight.shape[1]
    head_width = here // heads
    experts = router_weight.shape[1]
    capacity = 5 * tokens // (4 * experts)
    body = 16 * experts
    packed = 2 * width + width // 2
    span = 2 * tokens - BLOCK
    ring_size = width // here
    gain_one = first_gain[None, :]
    gain_two = second_gain[None, :]
    buckets = jnp.pad(rel_buckets, (0, 1), constant_values=-1)[None, :]
    weights = (query_weight.T, key_weight.T, value_weight.T)
    table = rel_table.T
    router = router_weight.T

    wide_lanes = (packed + 128) // 4
    kept = [
        ((tokens, here), BF),
        ((tokens, width), BF),
        ((tokens, here), BF),
        ((here, tokens), BF),
        ((tokens, here), BF),
        ((here, tokens), BF),
        ((here, tokens), BF),
        ((tokens, 128), F32),
    ]
    (
        mixed, normed, query, query_t, key, key_t, value_t, logsum,
        residual, hidden, probs, slots, slots_row, gates,
    ) = call(
        functools.partial(attend_body, head_width, capacity),
        "attend",
        kept
        + [
            ((tokens, width), F32),
            ((tokens, width), BF),
            ((tokens, experts), F32),
            ((tokens, 1), jnp.int32),
            ((1, tokens), jnp.int32),
            ((tokens, 1), F32),
        ],
        [pltpu.VMEM(*entry) for entry in kept]
        + [
            pltpu.VMEM((ring_size, tokens // 2, 2 * here), BF),
            pltpu.VMEM((ring_size, here, width), BF),
            pltpu.VMEM((heads, BLOCK, span), F32),
            pltpu.VMEM((tokens, here), BF),
            sems(tokens // BLOCK // 2, 8),
            sems(1, 8),
            sems(3, 2),
            sems(len(kept)),
        ],
        layer_in, gain_one, *weights, proj_weight, buckets, table, gain_two, router,
        expert_ids.reshape(1, tokens),
        number=1,
        far_out=range(len(kept)),
    )
    value, back_sum, in_grad, out_grad = call(
        functools.partial(moe_body, experts, capacity, 384, wide_lanes),
        "experts",
        [
            ((body, packed + 128), BF),
            ((body, packed + 128), BF),
            ((width, expert_in.shape[2]), F32),
            ((expert_out.shape[1], width), F32),
        ],
        [
            pltpu.VMEM((2, body, packed), BF),
            pltpu.VMEM((2, body, packed), BF),
            pltpu.VMEM((body, packed + 128), BF),
            pltpu.VMEM((width, expert_in.shape[2]), F32),
            pltpu.VMEM((expert_out.shape[1], width), F32),
            sems(2),
            *return_scratch(experts, wide_lanes),
            sems(2),
            sems(GROUPS),
            sems(GROUPS),
            sems(GROUPS, 8),
        ],
        hidden, gates, slots_row, cotangent, expert_in[0], expert_out[0],
        number=2,
        far_out=(2, 3),
    )
    returned, residual_grad, normed_part, large, small = call(
        functools.partial(backward_body, experts, capacity, head_width, wide_lanes),
        "backward",
        [
            ((body, packed + 128), BF),
            ((tokens, width), F32),
            ((tokens, width), BF),
            ((4 * here, width), BF),
            ((64, 1024), BF),
        ],
        [
            pltpu.VMEM((tokens, width), BF),
            pltpu.VMEM((tokens, here), BF),
            pltpu.VMEM((here, tokens), BF),
            pltpu.VMEM((tokens, here), BF),
            pltpu.VMEM((here, tokens), BF),
            pltpu.VMEM((here, tokens), BF),
            pltpu.VMEM((tokens, 128), F32),
            pltpu.VMEM((tokens, width), BF),
            pltpu.VMEM((tokens, width), F32),
            sems(9),
            pltpu.VMEM((tokens, here), BF),
            pltpu.VMEM((here, tokens), BF),
            pltpu.VMEM((heads, BLOCK, span), F32),
            pltpu.VMEM((heads, BLOCK, span), F32),
            pltpu.VMEM((tokens, here), BF),
            pltpu.VMEM((here, tokens), F32),
            pltpu.VMEM((here, tokens), F32),
            *return_scratch(experts, wide_lanes),
        ],
        value, back_sum, slots, residual, hidden, probs, gain_two, router, cotangent, mixed,
        proj_weight, normed, query, query_t, key, key_t, value_t, logsum, *weights, buckets, table,
        layer_in,
        number=5,
        mib=56,
        far_in=(*range(11, 18), 23),
        far_out=(1,),
    )
    peers = experts // 2
    tall, wide = 4 * here // peers, width // 2
    summed, large_sum, small_sum, lines, output = call(
        functools.partial(final_body, experts, capacity),
        "final",
        [
            ((tokens, width), BF),
            ((4 * here, width), BF),
            ((64, 1024), BF),
            ((3, 16, 1024), BF),
            ((tokens, width), BF),
        ],
        [
            pltpu.VMEM((4 * here, wide), BF),
            pltpu.VMEM((64, 512), BF),
            pltpu.VMEM((peers, tall, wide), BF),
            pltpu.VMEM((peers, 16, 128), BF),
            pltpu.VMEM((body, packed + 128), BF),
            pltpu.VMEM((tokens, width), F32),
            pltpu.VMEM((tokens, width), BF),
            sems(3),
            *reduce_scratch(4, tokens // 32, width),
            sems(8),
            sems(8),
            sems(3, 2),
            sems(4, 8),
            sems(4, 8),
        ],
        normed_part, large, small, returned, slots, gates, residual,
        number=4,
        far_in=(3, 6),
        far_out=(4,),
    )

    def whole(array):
        return pl.BlockSpec(array.shape, lambda i: (0,) * len(array.shape))

    def strip(array):
        return pl.BlockSpec((128, array.shape[1]), lambda i: (i, 0))

    results = [
        jax.ShapeDtypeStruct(shape, F32)
        for shape in [(tokens, width)] + [(here, width)] * 4
        + [(experts, width), (1, width), (1, width), table.shape]
    ]
    passed = (output, in_grad, out_grad)
    far = pl.BlockSpec(memory_space=pltpu.HBM)
    (
        input_grad, query_grad, key_grad, value_grad, proj_total, router_total, gain_total,
        first_total, table_total, output, in_grad, out_grad,
    ) = pl.pallas_call(
        finish_body,
        name="finish",
        grid=(tokens // 128,),
        out_shape=results + [jax.ShapeDtypeStruct(one.shape, one.dtype) for one in passed],
        in_specs=[
            strip(summed), strip(layer_in), strip(residual_grad), whole(gain_one),
            whole(large_sum), whole(small_sum), whole(lines), far, far, far,
        ],
        out_specs=[strip(results[0])] + [whole(result) for result in results[1:]] + [far] * 3,
        scratch_shapes=[sems(3)],
        compiler_params=pltpu.CompilerParams(vmem_limit_bytes=32 * MIB),
    )(summed, layer_in, residual_grad, gain_one, large_sum, small_sum, lines, *passed)
    return (
        output,
        input_grad,
        first_total[0],
        query_grad.T,
        key_grad.T,
        value_grad.T,
        proj_total,
        table_total.T,
        gain_total[0],
        router_total.T,
        in_grad[None],
        out_grad[None],
    )


def solution(mesh):
    return jax.shard_map(
        per_device,
        mesh=mesh,
        in_specs=(
            P("exp", None),
            P("exp", None),
            P(),
            P(),
            P(None, "tp"),
            P(None, "tp"),
            P(None, "tp"),
            P("tp", None),
            P(None, "tp"),
            P(),
            P(),
            P("exp", None, "tp"),
            P("exp", "tp", None),
            P("exp", None),
        ),
        out_specs=(
            P("exp", None),
            P("exp", None),
            P(),
            P(None, "tp"),
            P(None, "tp"),
            P(None, "tp"),
            P("tp", None),
            P(None, "tp"),
            P(),
            P(),
            P("exp", None, "tp"),
            P("exp", "tp", None),
        ),
        check_vma=False,
    )
```

```python
import functools

import jax
import jax.numpy as jnp
from jax import lax
from jax.experimental import pallas as pl
from jax.experimental.pallas import tpu as pltpu
from jax.sharding import PartitionSpec as P

epsilon = 1e-06
gelu_root = 0.7978845608028654
gelu_cube = 0.044715
BF = jnp.bfloat16
F32 = jnp.float32
BLOCK = 128
MIB = 1024 * 1024
GROUPS = 4
MESH = pl.DeviceIdType.MESH


def product(left, right):
    return jnp.dot(left, right, preferred_element_type=F32)


def rows_product(left, right):
    return lax.dot_general(left, right, (((0,), (0,)), ((), ())), preferred_element_type=F32)


def cols_product(left, right):
    return lax.dot_general(left, right, (((1,), (1,)), ((), ())), preferred_element_type=F32)


def inverse_rms(values):
    return lax.rsqrt(jnp.mean(values * values, axis=-1, keepdims=True) + epsilon)


def call(body, name, outs, scratch, *operands, mib=48, number=None, far_in=(), far_out=()):
    vmem = pl.BlockSpec(memory_space=pltpu.VMEM)
    far = pl.BlockSpec(memory_space=pltpu.HBM)
    extra = {} if number is None else {"collective_id": number, "has_side_effects": True}
    return pl.pallas_call(
        body,
        name=name,
        out_shape=[jax.ShapeDtypeStruct(shape, dtype) for shape, dtype in outs],
        in_specs=[far if i in far_in else vmem for i in range(len(operands))],
        out_specs=[far if i in far_out else vmem for i in range(len(outs))],
        scratch_shapes=scratch,
        compiler_params=pltpu.CompilerParams(vmem_limit_bytes=mib * MIB, **extra),
    )(*operands)


def remote(source, target, send, receive, **where):
    return pltpu.make_async_remote_copy(
        src_ref=source,
        dst_ref=target,
        send_sem=send,
        recv_sem=receive,
        device_id=where,
        device_id_type=MESH,
    )


def ring(ring_size):
    here = lax.axis_index("tp")
    return here, lax.rem(here + 1, ring_size), lax.rem(here + ring_size - 1, ring_size)


def greet(ring_size, batch_size, opposite=False, same_core=False):
    barrier = pltpu.get_barrier_semaphore()
    here, right, left = ring(ring_size)
    for side in (right, left):
        pl.semaphore_signal(barrier, inc=1, device_id={"tp": side}, device_id_type=MESH)
    if opposite:
        side = lax.rem(here + 2, ring_size)
        pl.semaphore_signal(barrier, inc=1, device_id={"tp": side}, device_id_type=MESH)
    me = lax.axis_index("exp")
    if same_core:
        sibling = me + 1 - 2 * lax.rem(me, 2)
        pl.semaphore_signal(barrier, inc=1, device_id={"exp": sibling}, device_id_type=MESH)
    if not batch_size:
        return 2 + int(opposite) + int(same_core)
    stride = 2 if same_core else 1
    peers = batch_size // stride

    def hello(step, carry):
        peer = lax.rem(me + step * stride, batch_size)
        pl.semaphore_signal(barrier, inc=1, device_id={"exp": peer}, device_id_type=MESH)
        return carry

    lax.fori_loop(1, peers, hello, 0)
    return 2 + int(opposite) + peers - 1 + int(same_core)


def meet(signals):
    pl.semaphore_wait(pltpu.get_barrier_semaphore(), signals)


def place_index(device):
    z, y, core = device // 8, device // 2 % 4, device % 2
    return (z + y) % 4 * 8 + z * 2 + core


def device_at(place):
    group, z, core = place // 8, place % 8 // 2, place % 2
    return z * 8 + (group + 4 - z) % 4 * 2 + core


class Gather:
    def __init__(self, region, half, sems):
        self.region, self.half, self.sems = region, half, sems
        self.here, self.right, self.left = ring(4)
        self.far = lax.rem(self.here + 2, 4)

    def first(self, k):
        own = self.region(k, self.here)
        return (
            remote(own, own, self.sems.at[k, 0], self.sems.at[k, 1], tp=self.right),
            remote(own, own, self.sems.at[k, 2], self.sems.at[k, 3], tp=self.left),
        )

    def second(self, k):
        low, high = self.half(k, self.left, 0), self.half(k, self.right, 1)
        return (
            remote(low, low, self.sems.at[k, 4], self.sems.at[k, 5], tp=self.right),
            remote(high, high, self.sems.at[k, 6], self.sems.at[k, 7], tp=self.left),
        )

    def start(self, k):
        for copy in self.first(k):
            copy.start()

    def forward(self, k):
        for side, copy, arrived in zip(
            (self.left, self.right), self.second(k), (1, 3), strict=True
        ):
            whole = self.region(k, side)
            remote(whole, whole, self.sems.at[k, 0], self.sems.at[k, arrived], tp=self.right).wait_recv()
            copy.start()

    def finish(self, k):
        for half, sent, arrived in ((0, 4, 5), (1, 6, 7)):
            part = self.half(k, self.far, half)
            remote(part, part, self.sems.at[k, sent], self.sems.at[k, arrived], tp=self.right).wait_recv()

    def drain(self, k):
        for copy in self.first(k) + self.second(k):
            copy.wait_send()


class Reduce:
    def __init__(self, piece, in_left, in_right, out_right, out_left, mid_left, mid_right, sems):
        self.piece, self.sems = piece, sems
        self.in_left, self.in_right = in_left, in_right
        self.out_right, self.out_left = out_right, out_left
        self.mid_left, self.mid_right = mid_left, mid_right
        self.here, self.right, self.left = ring(4)
        self.far = lax.rem(self.here + 2, 4)

    def first(self, k):
        return (
            remote(self.piece(k, self.far, 0), self.in_left.at[k], self.sems.at[k, 0], self.sems.at[k, 1], tp=self.right),
            remote(self.piece(k, self.far, 1), self.in_right.at[k], self.sems.at[k, 2], self.sems.at[k, 3], tp=self.left),
        )

    def second(self, k):
        return (
            remote(self.out_right.at[k], self.mid_left.at[k], self.sems.at[k, 4], self.sems.at[k, 5], tp=self.right),
            remote(self.out_left.at[k], self.mid_right.at[k], self.sems.at[k, 6], self.sems.at[k, 7], tp=self.left),
        )

    def start(self, k):
        for copy in self.first(k):
            copy.start()

    def middle(self, k):
        by_left, by_right = self.first(k)
        to_right, to_left = self.second(k)
        by_left.wait_recv()
        summed = self.piece(k, self.right, 0)[...].astype(F32) + self.in_left[k].astype(F32)
        self.out_right[k, 0] = summed.astype(BF)
        self.out_right[k, 1] = self.piece(k, self.right, 1)[...]
        to_right.start()
        by_right.wait_recv()
        summed = self.piece(k, self.left, 1)[...].astype(F32) + self.in_right[k].astype(F32)
        self.out_left[k, 1] = summed.astype(BF)
        self.out_left[k, 0] = self.piece(k, self.left, 0)[...]
        to_left.start()

    def finish(self, k):
        for copy in self.second(k):
            copy.wait_recv()
        return [
            self.piece(k, self.here, half)[...].astype(F32)
            + self.mid_left[k, half].astype(F32)
            + self.mid_right[k, half].astype(F32)
            for half in (0, 1)
        ]

    def drain(self, k):
        for copy in self.first(k) + self.second(k):
            copy.wait_send()


def reduce_scratch(groups, rows, lanes):
    return [pltpu.VMEM((groups, rows, lanes), BF)] * 2 + [
        pltpu.VMEM((groups, 2, rows, lanes), BF)
    ] * 4


def sems(*dims):
    return pltpu.SemaphoreType.DMA(dims)


def return_parts(batch_size, lanes, source, out, stage, buffers, send, arrive, sum_sems, ring_sems):
    me = lax.axis_index("exp")
    position = place_index(me)
    here = lax.axis_index("tp")
    part = batch_size // GROUPS
    mine = pl.ds(pl.multiple_of(here * lanes, 128), lanes)
    own = pl.ds(pl.multiple_of(position * 16, 16), 16)

    def leaving(k):
        return lax.rem(position // part + GROUPS - k, GROUPS) * (part * 16)

    def arriving(k):
        return lax.rem(position // part + k, GROUPS) * (part * 16)

    def span(ref, base, who, begin, rows):
        spot = pl.ds(pl.multiple_of(base + begin, 16), rows)
        return ref.at[spot, pl.ds(pl.multiple_of(who * lanes, 128), lanes)]

    half_rows = part * 8
    reduce = Reduce(
        lambda k, who, half: span(source, leaving(k), who, half * half_rows, half_rows),
        *buffers,
        sum_sems,
    )
    gather = Gather(
        lambda k, who: span(out, arriving(k), who, 0, part * 16),
        lambda k, who, half: span(out, arriving(k), who, half * half_rows, half_rows),
        ring_sems,
    )

    def scatter(k):
        first, second = reduce.finish(k)
        spot = pl.multiple_of(leaving(k), 16)
        stage[pl.ds(spot, half_rows), :] = first.astype(BF)
        stage[pl.ds(pl.multiple_of(spot + half_rows, 16), half_rows), :] = second.astype(BF)
        if k == 0:
            out[own, mine] = stage[own, :]

        def step(j, carry):
            group = lax.rem(position // part + GROUPS - k, GROUPS)
            peer = group * part + lax.rem(position + j, part)
            rows = pl.ds(pl.multiple_of(peer * 16, 16), 16)
            remote(
                stage.at[rows, :], out.at[own, mine], send.at[0], arrive.at[k], exp=device_at(peer)
            ).start()
            return carry

        lax.fori_loop(1 if k == 0 else 0, part, step, 0)

    def collect(k):
        rows = (part - 1 if k == 0 else part) * 16
        block = span(out, arriving(k), here, 0, rows)
        remote(block, block, send.at[0], arrive.at[k], exp=me).wait_recv()
        gather.start(k)

    def drain():
        whole = stage.at[pl.ds(0, (batch_size - 1) * 16), :]
        remote(whole, whole, send.at[0], arrive.at[0], exp=me).wait_send()
        for k in range(GROUPS):
            reduce.drain(k)
            gather.drain(k)

    return reduce, gather, scatter, collect, drain


def return_scratch(batch_size, lanes):
    return [
        pltpu.VMEM((batch_size * 16, lanes), BF),
        *reduce_scratch(GROUPS, batch_size * 8 // GROUPS, lanes),
        sems(1),
        sems(GROUPS),
        sems(GROUPS, 8),
        sems(GROUPS, 8),
    ]


def final_body(
    batch_size, capacity, part_in, large, small, returned_far, slots, gates, residual_far,
    summed, large_out, small_out, lines, output_far,
    large_side, small_side, large_in, small_in, returned, residual, output, far_sems, *rest,
):
    buffers, (send, arrive, line_sems, sum_sems, ring_sems) = rest[:6], rest[6:]
    signals = greet(4, batch_size, opposite=True, same_core=True)
    me = lax.axis_index("exp")
    core = lax.rem(me, 2)
    sibling = me + 1 - 2 * core
    here, right, left = ring(4)
    tokens, width = part_in.shape
    chunk = tokens // 4
    groups = buffers[0].shape[0]
    half_rows = chunk // groups // 2
    peers, tall, wide = large_in.shape
    half_lanes = small.shape[1] // 2
    small_across = half_lanes // 128

    def spot(ref, who, k, begin, count):
        first = who * chunk + k * (2 * half_rows) + begin
        return ref.at[pl.ds(pl.multiple_of(first, 16), count), :]

    reduce = Reduce(
        lambda k, who, half: spot(part_in, who, k, half * half_rows, half_rows), *buffers, sum_sems
    )
    gather = Gather(
        lambda k, who: spot(summed, who, k, 0, 2 * half_rows),
        lambda k, who, half: spot(summed, who, k, half * half_rows, half_rows),
        ring_sems,
    )

    def large_half(ref, side):
        return ref.at[:, pl.ds(pl.multiple_of(side * wide, 128), wide)]

    def small_half(ref, side):
        return ref.at[:, pl.ds(pl.multiple_of(side * half_lanes, 128), half_lanes)]

    def large_rows(ref, who):
        return ref.at[pl.ds(pl.multiple_of(who * tall, 16), tall), :]

    def small_rows(ref, who):
        down = pl.ds(pl.multiple_of(who // small_across * 16, 16), 16)
        return ref.at[down, pl.ds(pl.multiple_of(lax.rem(who, small_across) * 128, 128), 128)]

    def large_final(who):
        down = pl.ds(pl.multiple_of(who * tall, 16), tall)
        return large_out.at[down, pl.ds(pl.multiple_of(core * wide, 128), wide)]

    def small_final(who):
        down = pl.ds(pl.multiple_of(who // small_across * 16, 16), 16)
        lane = core * half_lanes + lax.rem(who, small_across) * 128
        return small_out.at[down, pl.ds(pl.multiple_of(lane, 128), 128)]

    late = [
        pltpu.make_async_copy(returned_far, returned, far_sems.at[0]),
        pltpu.make_async_copy(residual_far, residual, far_sems.at[1]),
    ]
    for copy in late:
        copy.start()
    meet(signals)
    pair = [
        remote(large_half(large, 1 - core), large_side, send.at[0], arrive.at[0], exp=sibling),
        remote(small_half(small, 1 - core), small_side, send.at[1], arrive.at[1], exp=sibling),
    ]
    for copy in pair:
        copy.start()
    for k in range(groups):
        reduce.start(k)
    for copy in pair:
        copy.wait_recv()
    both = large_side[...].astype(F32) + large_half(large, core)[...].astype(F32)
    large_side[...] = both.astype(BF)
    both = small_side[...].astype(F32) + small_half(small, core)[...].astype(F32)
    small_side[...] = both.astype(BF)
    mine = me // 2

    def scatter(step, carry):
        peer = lax.rem(mine + step, peers)
        to = peer * 2 + core
        remote(large_rows(large_side, peer), large_in.at[step], send.at[2], arrive.at[2], exp=to).start()
        remote(small_rows(small_side, peer), small_in.at[step], send.at[3], arrive.at[3], exp=to).start()
        return carry

    lax.fori_loop(1, peers, scatter, 0)
    large_in[0] = large_rows(large_side, mine)[...]
    small_in[0] = small_rows(small_side, mine)[...]
    for k in range(groups):
        reduce.middle(k)

    experts = batch_size
    body = 16 * experts
    place = place_of(slots[...], experts, capacity, 5 * body // 2)
    for copy in late:
        copy.wait()
    token_rows = fetch(place, returned, width, experts)
    output[...] = (residual[...] + gates[...] * token_rows).astype(BF)
    kept = pltpu.make_async_copy(output, output_far, far_sems.at[2])
    kept.start()

    large_rest = large_in.at[pl.ds(1, peers - 1)]
    small_rest = small_in.at[pl.ds(1, peers - 1)]
    remote(large_rest, large_rest, send.at[2], arrive.at[2], exp=me).wait_recv()
    remote(small_rest, small_rest, send.at[3], arrive.at[3], exp=me).wait_recv()

    def add(step, carry):
        return carry[0] + large_in[step].astype(F32), carry[1] + small_in[step].astype(F32)

    zero = (jnp.zeros((tall, wide), F32), jnp.zeros((16, 128), F32))
    large_sum, small_sum = lax.fori_loop(0, peers, add, zero)
    large_final(mine)[...] = large_sum.astype(BF)
    small_final(mine)[...] = small_sum.astype(BF)

    def spread(step, carry):
        to = lax.rem(mine + step, peers) * 2 + core
        own = large_final(mine)
        remote(own, own, send.at[4], arrive.at[4], exp=to).start()
        own = small_final(mine)
        remote(own, own, send.at[5], arrive.at[5], exp=to).start()
        return carry

    lax.fori_loop(1, peers, spread, 0)
    for k in range(groups):
        pieces = reduce.finish(k)
        for half in (0, 1):
            target = spot(summed, here, k, half * half_rows, half_rows)
            target[...] = pieces[half].astype(BF)
        gather.start(k)
    remote(large_rest, large_rest, send.at[4], arrive.at[4], exp=me).wait_recv()
    remote(small_rest, small_rest, send.at[5], arrive.at[5], exp=me).wait_recv()
    back = []
    for i, half in ((6, large_half(large_out, core)), (7, small_half(small_out, core))):
        back.append(remote(half, half, send.at[i], arrive.at[i], exp=sibling))
    for copy in back:
        copy.start()
    for k in range(groups):
        gather.forward(k)
    for i, half in ((6, large_half(large_out, 1 - core)), (7, small_half(small_out, 1 - core))):
        remote(half, half, send.at[i], arrive.at[i], exp=sibling).wait_recv()
    line = small_out.at[pl.ds(32, 16), :]
    others = (right, left, lax.rem(here + 2, 4))
    copies = [
        remote(line, lines.at[i], line_sems.at[i, 0], line_sems.at[i, 1], tp=side)
        for i, side in enumerate(others)
    ]
    for copy in copies:
        copy.start()
    for k in range(groups):
        gather.finish(k)
    for copy in copies:
        copy.wait_recv()
    kept.wait()
    for copy in copies + pair + back:
        copy.wait_send()
    for i, ref in ((2, large_rest), (3, small_rest), (4, large_rest), (5, small_rest)):
        remote(ref, ref, send.at[i], arrive.at[0], exp=me).wait_send()
    for k in range(groups):
        reduce.drain(k)
        gather.drain(k)


def finish_body(
    summed, rows, residual_grad, gain, large, small, lines, output, in_grad, out_grad,
    input_grad, query_grad, key_grad, value_grad, proj_grad, router_grad, gain_grad, first_grad,
    table_grad, output_last, in_grad_last, out_grad_last,
):
    output_last[...] = output[...]
    in_grad_last[...] = in_grad[...]
    out_grad_last[...] = out_grad[...]
    inputs = rows[...].astype(F32)
    scale = inverse_rms(inputs)
    scaled = summed[...].astype(F32) * gain[...]
    middle = jnp.mean(scaled * inputs, axis=-1, keepdims=True)
    input_grad[...] = (
        residual_grad[...] + scale * scaled - inputs * (scale * scale * scale * middle)
    )

    @pl.when(pl.program_id(0) == 0)
    def _():
        high, width = query_grad.shape
        for i, ref in enumerate((query_grad, key_grad, value_grad, proj_grad)):
            ref[...] = large[i * high : (i + 1) * high, :].astype(F32)
        router_grad[...] = small[0 : router_grad.shape[0], 0:width].astype(F32)
        total = small[32:48, 0:width].astype(F32)
        gain_grad[...] = total[0]
        table_grad[...] = small[48:64, 0:128].astype(F32)[0:3, 0:32]
        for i in range(3):
            total = total + lines[i][:, 0:width].astype(F32)
        first_grad[...] = total[8]


def head_mask(head, head_width, width):
    lane = lax.broadcasted_iota(jnp.int32, (1, width), 1)
    return jnp.where(lane // head_width == head, 1.0, 0.0)


def fill_bias(bias, buckets, table):
    heads, block, width = bias.shape
    padded = buckets.shape[1]
    number = lax.broadcasted_iota(jnp.int32, (table.shape[1], padded), 0)
    hot = jnp.where(buckets[...] == number, 1.0, 0.0)
    offsets = jnp.dot(
        table[...], hot, precision=lax.Precision.HIGHEST, preferred_element_type=F32
    )
    for head in range(heads):
        spread = jnp.broadcast_to(offsets[head : head + 1, :], (block, padded))
        rolled = pltpu.roll(spread, padded - (block - 1), 1, stride=1, stride_axis=0)
        bias[head] = rolled[:, :width]


def attend_body(
    head_width, capacity,
    rows, gain, query_w, key_w, value_w, proj, buckets, table, second_gain, router_w, ids_row,
    mixed_far, normed_far, query_far, query_t_far, key_far, key_t_far, value_t_far, logsum_far,
    residual, hidden, probs, slots, slots_row, gates,
    mixed, normed, query, query_t, key, key_t, value_t, logsum,
    mixed_all, proj_all, bias, value, ring_sems, proj_sems, pair_sems, far_sems,
):
    heads = bias.shape[0]
    tokens = rows.shape[0]
    width = query.shape[1]
    blocks = tokens // BLOCK
    pairs = blocks // 2
    signals = greet(4, 0, same_core=True)
    here = lax.axis_index("tp")
    me = lax.axis_index("exp")
    core = lax.rem(me, 2)
    sibling = me + 1 - 2 * core
    inputs = rows[...].astype(F32)
    low = (inputs * inverse_rms(inputs) * gain[...]).astype(BF)
    normed[...] = low
    proj_all[here] = proj[...]
    meet(signals)
    gather = Gather(
        lambda k, who: mixed_all.at[who, pl.ds(pl.multiple_of(k * BLOCK, BLOCK), BLOCK), :],
        lambda k, who, half: mixed_all.at[
            who, pl.ds(pl.multiple_of(k * BLOCK + half * (BLOCK // 2), 16), BLOCK // 2), :
        ],
        ring_sems,
    )
    half_rows = proj.shape[0] // 2

    def proj_part(who, side, begin, count):
        spot = pl.multiple_of(side * half_rows + begin, 16)
        return proj_all.at[who, pl.ds(spot, count), :]

    weights_gather = Gather(
        lambda k, who: proj_part(who, core, 0, half_rows),
        lambda k, who, half: proj_part(who, core, half * (half_rows // 2), half_rows // 2),
        proj_sems,
    )

    def to_sibling(i, who, side):
        part = proj_part(who, side, 0, half_rows)
        return remote(part, part, pair_sems.at[i, 0], pair_sems.at[i, 1], exp=sibling)

    foreign = (weights_gather.left, weights_gather.right, weights_gather.far)
    weights_gather.start(0)
    query[...] = cols_product(low, query_w[...]).astype(BF)
    key[...] = cols_product(low, key_w[...]).astype(BF)
    value[...] = cols_product(low, value_w[...]).astype(BF)
    query_t[...] = cols_product(query_w[...], low).astype(BF)
    key_t[...] = cols_product(key_w[...], low).astype(BF)
    value_t[...] = cols_product(value_w[...], low).astype(BF)
    def keep(ref, far, i):
        copy = pltpu.make_async_copy(ref, far, far_sems.at[i])
        copy.start()
        return [copy]

    early_copies = []
    for i, (ref, far) in enumerate(
        (
            (normed, normed_far), (query, query_far), (query_t, query_t_far), (key, key_far),
            (key_t, key_t_far), (value_t, value_t_far),
        )
    ):
        early_copies += keep(ref, far, i)
    fill_bias(bias, buckets, table)
    weights_gather.forward(0)
    for i in (0, 1):
        to_sibling(i, foreign[i], core).start()

    def step(pair, carry):
        for side in (0, 1):
            block = pair + side * pairs
            first = pl.multiple_of(block * BLOCK, BLOCK)
            shift = pl.multiple_of((blocks - 1 - block) * BLOCK, BLOCK)
            query_rows = query[pl.ds(first, BLOCK), :]
            total = jnp.zeros((BLOCK, width), F32)
            for head in range(heads):
                mask = head_mask(head, head_width, width)
                scores = product(query_rows * mask.astype(BF), key_t[...])
                scores = scores + bias[head, :, pl.ds(shift, tokens)]
                highest = jnp.max(scores, axis=-1, keepdims=True)
                weights = jnp.exp(scores - highest)
                summed = jnp.sum(weights, axis=-1, keepdims=True)
                part = product(weights.astype(BF), value[...]) / summed
                total = total + part * mask
                logsum[pl.ds(first, BLOCK), head : head + 1] = highest + jnp.log(summed)
            spot = pl.ds(pl.multiple_of(pair * BLOCK, BLOCK), BLOCK)
            mixed[pl.ds(first, BLOCK), :] = total.astype(BF)
            mixed_all[here, spot, side * width : (side + 1) * width] = total.astype(BF)
        gather.start(pair)

        @pl.when(pair > 0)
        def _():
            gather.forward(pair - 1)

        return carry

    lax.fori_loop(0, pairs // 2, step, 0)
    weights_gather.finish(0)
    to_sibling(2, foreign[2], core).start()
    lax.fori_loop(pairs // 2, pairs, step, 0)
    gather.forward(pairs - 1)
    out_copies = keep(mixed, mixed_far, 6) + keep(logsum, logsum_far, 7)
    experts = router_w.shape[0]
    number = lax.broadcasted_iota(jnp.int32, (experts, tokens), 0)
    hot_t = ids_row[...] == number
    ones_t = jnp.where(hot_t, 1.0, 0.0)
    across = lax.broadcasted_iota(jnp.int32, (tokens, tokens), 0)
    along = lax.broadcasted_iota(jnp.int32, (tokens, tokens), 1)
    upper = jnp.where(across <= along, 1.0, 0.0).astype(BF)
    counts_t = product(ones_t.astype(BF), upper)
    position_t = jnp.sum(jnp.where(hot_t, counts_t - 1.0, 0.0), axis=0, keepdims=True)
    line = ids_row[...] * capacity + position_t.astype(jnp.int32)
    slots_row[...] = line
    slots[...] = jnp.broadcast_to(line.astype(F32), (128, tokens)).T[:, 0:1].astype(jnp.int32)
    for i in range(3):
        to_sibling(i, foreign[i], 1 - core).wait_recv()
    for k in range(pairs):
        gather.finish(k)
        halves = [pl.ds(side * (tokens // 2) + k * BLOCK, BLOCK) for side in (0, 1)]
        res = jnp.concatenate([rows[spot, :] for spot in halves], axis=0).astype(F32)
        for i in range(mixed_all.shape[0]):
            both = mixed_all[i, k * BLOCK : (k + 1) * BLOCK, :]
            both = jnp.concatenate([both[:, :width], both[:, width:]], axis=0)
            res = res + product(both, proj_all[i])
        low = (res * inverse_rms(res) * second_gain[...]).astype(BF)
        logits = cols_product(low, router_w[...])
        shifted = jnp.exp(logits - jnp.max(logits, axis=-1, keepdims=True))
        chances = shifted / jnp.sum(shifted, axis=-1, keepdims=True)
        for side in (0, 1):
            spot, part = halves[side], slice(side * BLOCK, (side + 1) * BLOCK)
            residual[spot, :] = res[part]
            hidden[spot, :] = low[part]
            probs[spot, :] = chances[part]
            expert = lax.broadcasted_iota(jnp.int32, (BLOCK, experts), 1)
            hot = slots[spot, :] // capacity == expert
            chosen = jnp.sum(jnp.where(hot, chances[part], 0.0), axis=1, keepdims=True)
            gates[spot, :] = chosen
    for i in range(3):
        to_sibling(i, foreign[i], core).wait_send()
    for copy in early_copies + out_copies:
        copy.wait()
    weights_gather.drain(0)
    for k in range(pairs):
        gather.drain(k)


def pack_third(third, experts):
    half = third.shape[1] // 2
    split = third.reshape(experts, 8, 2 * half)
    split = jnp.concatenate([split[:, :, :half], split[:, :, half:]], axis=1)
    return split.reshape(experts * 16, half)


def unpack_third(tail, runs):
    half = tail.shape[1]
    split = tail.astype(F32).reshape(runs, 16, half)
    return jnp.concatenate([split[:, :8], split[:, 8:]], axis=2).reshape(runs * 8, 2 * half)


def slot_of_row(row, experts, capacity):
    body = 16 * experts
    first = device_at(row // 16) * capacity + row % 16
    second = device_at((row - body) // 16) * capacity + 16 + (row - body) % 16
    third = device_at((row - 2 * body) // 8) * capacity + 32 + (row - 2 * body) % 8
    return jnp.where(row < body, first, jnp.where(row < 2 * body, second, third))


def moe_body(
    batch_size, capacity, lanes, back_lanes,
    hidden, gates, slots_row, cotangent, weight_in, weight_out,
    value, back_sum, in_grad_far, out_grad_far,
    leave, arrived, back, in_grad, out_grad, far_sems, stage, *rest,
):
    buffers, (send_back, arrive_back, sum_sems, back_sems) = rest[:6], rest[6:10]
    send, arrive, arrive_tail, ring_sems = rest[10:]
    signals = greet(4, batch_size)
    me = lax.axis_index("exp")
    here = lax.axis_index("tp")
    position = place_index(me)
    part = batch_size // GROUPS
    zone_rows = part * 16
    width = hidden.shape[1]
    slots_t = slots_row[...]
    low = hidden[...]
    gate = gates[...]
    grads = (gate * cotangent[...].astype(F32)).astype(BF)
    meet(signals)

    mine = pl.ds(pl.multiple_of(here * lanes, 128), lanes)
    tail = pl.ds(4 * lanes, leave.shape[2] - 4 * lanes)
    own = pl.ds(pl.multiple_of(position * 16, 16), 16)
    place_row = lax.broadcasted_iota(jnp.int32, (zone_rows * 5 // 2, 1), 0)
    third = place_row - 2 * zone_rows
    member = jnp.where(third < 0, place_row % zone_rows // 16, third // 8)
    inside = jnp.where(
        place_row < zone_rows,
        place_row % 16,
        jnp.where(third < 0, 16 + place_row % 16, 32 + third % 8),
    )

    def scatter_rows(k, columns, sent, landed):
        zone = lax.rem(position // part + k, GROUPS)

        def step(j, carry):
            peer = zone * part + lax.rem(position + j, part)
            block = pl.ds(pl.multiple_of(peer * 16, 16), 16)
            remote(
                leave.at[:, block, columns], arrived.at[:, own, columns],
                send.at[sent], landed.at[k], exp=device_at(peer),
            ).start()
            return carry

        lax.fori_loop(1 if k == 0 else 0, part, step, 0)

    for k in range(GROUPS):
        zone = lax.rem(position // part + k, GROUPS)
        wanted = device_at(zone * part + member) * capacity + inside
        place = jnp.where(wanted == slots_t, 1.0, 0.0).astype(BF)
        spot = pl.ds(pl.multiple_of(zone * zone_rows, 16), zone_rows)
        for array, source in ((0, low), (1, grads)):
            picked = product(place, source)
            leave[array, spot, 0:width] = picked[:zone_rows].astype(BF)
            leave[array, spot, width : 2 * width] = picked[zone_rows : 2 * zone_rows].astype(BF)
            packed = pack_third(picked[2 * zone_rows :], part)
            leave[array, spot, 2 * width :] = packed.astype(BF)
        if k == 0:
            arrived[:, own, mine] = leave[:, own, mine]
            arrived[:, own, tail] = leave[:, own, tail]
        scatter_rows(k, mine, 0, arrive)
    for k in range(GROUPS):
        scatter_rows(k, tail, 1, arrive_tail)

    def arriving(k):
        return lax.rem(position // part + GROUPS - k, GROUPS) * zone_rows

    def span(k, who, count, array=slice(None)):
        spot = pl.ds(pl.multiple_of(arriving(k), 16), count)
        return arrived.at[array, spot, pl.ds(pl.multiple_of(who * lanes, 128), lanes)]

    gather = Gather(
        lambda k, who: span(k, who, zone_rows),
        lambda k, who, side: span(k, who, zone_rows, pl.ds(side, 1)),
        ring_sems,
    )

    def quarter(k):
        block = span(k, here, zone_rows - 16 if k == 0 else zone_rows)
        remote(block, block, send.at[0], arrive.at[k], exp=me).wait_recv()
        gather.start(k)

    def whole(k):
        gather.finish(k)
        count = zone_rows - 16 if k == 0 else zone_rows
        block = arrived.at[:, pl.ds(pl.multiple_of(arriving(k), 16), count), tail]
        remote(block, block, send.at[1], arrive_tail.at[k], exp=me).wait_recv()

    def experts_on(k):
        spot = pl.ds(pl.multiple_of(arriving(k), 16), zone_rows)

        def rows_of(array):
            last = unpack_third(arrived[array, spot, 2 * width :], part).astype(BF)
            first = [arrived[array, spot, 0:width], arrived[array, spot, width : 2 * width]]
            return jnp.concatenate(first + [last], axis=0)

        x, g = rows_of(0), rows_of(1)
        pre = product(x, weight_in[...])
        inner = jnp.tanh(gelu_root * (pre + gelu_cube * pre * pre * pre))
        act = (0.5 * pre * (1.0 + inner)).astype(BF)
        slope = 0.5 * (1.0 + inner) + 0.5 * pre * (1.0 - inner * inner) * (
            gelu_root * (1.0 + 3.0 * gelu_cube * pre * pre)
        )
        act_grad = cols_product(g, weight_out[...])
        pre_grad = (act_grad * slope).astype(BF)
        rows_back = cols_product(pre_grad, weight_in[...])
        out = product(act, weight_out[...])
        dots = jnp.sum(out * g.astype(F32), axis=1, keepdims=True)
        lane = lax.broadcasted_iota(jnp.int32, (1, 128), 1)
        marks = jnp.where(lane == 0, dots[:zone_rows], 0.0)
        marks = marks + jnp.where(lane == 1, dots[zone_rows : 2 * zone_rows], 0.0)
        last = jnp.where(lane == 2, dots[2 * zone_rows :], 0.0).reshape(part, 8, 128)
        last = jnp.concatenate([last, jnp.zeros_like(last)], axis=1).reshape(zone_rows, 128)
        for ref, result, extra in (
            (back, rows_back, marks + last),
            (value, out, jnp.zeros((zone_rows, 128), F32)),
        ):
            ref[spot, 0:width] = result[:zone_rows].astype(BF)
            ref[spot, width : 2 * width] = result[zone_rows : 2 * zone_rows].astype(BF)
            packed = pack_third(result[2 * zone_rows :], part)
            ref[spot, 2 * width : 2 * width + width // 2] = packed.astype(BF)
            ref[spot, 2 * width + width // 2 :] = extra.astype(BF)
        return x, g, act, pre_grad

    def weights_on(k, held):
        x, g, act, pre_grad = held
        if k == 0:
            out_grad[...] = rows_product(act, g)
            in_grad[...] = rows_product(x, pre_grad)
        else:
            out_grad[...] += rows_product(act, g)
            in_grad[...] += rows_product(x, pre_grad)

    reduce, gather_back, scatter, collect, drain = return_parts(
        batch_size, back_lanes, back, back_sum, stage, buffers,
        send_back, arrive_back, sum_sems, back_sems,
    )

    def work(k):
        whole(k)
        held = experts_on(k)
        reduce.start(k)
        weights_on(k, held)

    quarter(0)
    quarter(1)
    gather.forward(0)
    quarter(2)
    gather.forward(1)
    work(0)
    quarter(3)
    gather.forward(2)
    reduce.middle(0)
    work(1)
    gather.forward(3)
    reduce.middle(1)
    scatter(0)
    work(2)
    reduce.middle(2)
    scatter(1)
    collect(0)
    work(3)
    far_copies = [
        pltpu.make_async_copy(in_grad, in_grad_far, far_sems.at[0]),
        pltpu.make_async_copy(out_grad, out_grad_far, far_sems.at[1]),
    ]
    for copy in far_copies:
        copy.start()
    reduce.middle(3)
    scatter(2)
    collect(1)
    gather_back.forward(0)
    scatter(3)
    collect(2)
    gather_back.forward(1)
    collect(3)
    gather_back.forward(2)
    gather_back.forward(3)
    for k in range(GROUPS):
        gather_back.finish(k)
    for copy in far_copies:
        copy.wait()
    drain()
    for k in range(GROUPS):
        gather.drain(k)
    for columns, sent in ((mine, 0), (tail, 1)):
        block = leave.at[:, pl.ds(0, (batch_size - 1) * 16), columns]
        remote(block, block, send.at[sent], arrive.at[0], exp=me).wait_send()


def place_of(slots, experts, capacity, rows):
    number = slot_of_row(lax.broadcasted_iota(jnp.int32, (1, rows), 1), experts, capacity)
    return jnp.where(slots == number, 1.0, 0.0).astype(BF)


def fetch(place, ref, width, experts):
    body = 16 * experts
    picked = product(place[:, :body], ref[:, :width])
    picked = picked + product(place[:, body : 2 * body], ref[:, width : 2 * width])
    tail = unpack_third(ref[:, 2 * width : 2 * width + width // 2], experts).astype(BF)
    return picked + product(place[:, 2 * body :], tail)


def backward_body(
    batch_size, capacity, head_width, lanes,
    value_in, back, slots, residual, hidden, probs, gain, router_w, cotangent, mixed, proj,
    normed_far, query_far, query_t_far, key_far, key_t_far, value_t_far, logsum_far,
    query_w, key_w, value_w, buckets, table, rows_far,
    returned, residual_grad_far, normed_part, large, small,
    normed, query, query_t, key, key_t, value_t, logsum, rows, residual_grad, far_sems,
    grad, grad_t, bias, sums, query_back, key_acc, value_acc, stage, *rest,
):
    buffers, (send, arrive, sum_sems, ring_sems) = rest[:6], rest[6:]
    signals = greet(4, batch_size)
    reduce, gather, scatter, collect, drain = return_parts(
        batch_size, lanes, value_in, returned, stage, buffers, send, arrive, sum_sems, ring_sems
    )
    tokens, full = residual.shape
    experts = router_w.shape[0]
    body = 16 * experts
    heads = bias.shape[0]
    width = query.shape[1]
    blocks = tokens // BLOCK
    late = [
        pltpu.make_async_copy(far, ref, far_sems.at[i])
        for i, (far, ref) in enumerate(
            (
                (query_far, query), (query_t_far, query_t), (key_far, key), (key_t_far, key_t),
                (value_t_far, value_t), (logsum_far, logsum), (normed_far, normed),
                (rows_far, rows),
            )
        )
    ]
    for copy in late:
        copy.start()
    place = place_of(slots[...], experts, capacity, 5 * body // 2)
    meet(signals)
    for k in range(GROUPS):
        reduce.start(k)

    marks = back[:, 2 * full + full // 2 :]
    lane = lax.broadcasted_iota(jnp.int32, (1, 128), 1)
    tail = marks.astype(F32).reshape(experts, 16, 128)[:, :8].reshape(experts * 8, 128).astype(BF)
    dots = jnp.where(lane == 0, product(place[:, :body], marks), 0.0)
    dots = dots + jnp.where(lane == 1, product(place[:, body : 2 * body], marks), 0.0)
    dots = dots + jnp.where(lane == 2, product(place[:, 2 * body :], tail), 0.0)
    weighted = jnp.sum(dots, axis=1, keepdims=True)
    hot = slots[...] // capacity == lax.broadcasted_iota(jnp.int32, (tokens, experts), 1)
    logit_grad = (jnp.where(hot, weighted, 0.0) - probs[...] * weighted).astype(BF)
    router_grad = rows_product(logit_grad, hidden[...])
    hidden_grad = fetch(place, back, full, experts) + product(logit_grad, router_w[...])
    for k in range(GROUPS // 2):
        reduce.middle(k)
    res = residual[...]
    scale = inverse_rms(res)
    gain_grad = jnp.sum(hidden_grad * res * scale, axis=0, keepdims=True)
    scaled = gain[...] * hidden_grad
    middle = jnp.mean(scaled * res, axis=-1, keepdims=True)
    total = cotangent[...].astype(F32) + scale * scaled - res * (scale * scale * scale * middle)
    low = total.astype(BF)
    residual_grad[...] = total
    kept = pltpu.make_async_copy(residual_grad, residual_grad_far, far_sems.at[len(late)])
    kept.start()
    for k in range(GROUPS // 2, GROUPS):
        reduce.middle(k)
    large[3 * width :, :] = rows_product(mixed[...], low).astype(BF)
    grad[...] = cols_product(low, proj[...]).astype(BF)
    grad_t[...] = cols_product(proj[...], low).astype(BF)

    for copy in late:
        copy.wait()
    fill_bias(bias, buckets, table)
    sums[...] = jnp.zeros(sums.shape, F32)
    key_acc[...] = jnp.zeros(key_acc.shape, F32)
    value_acc[...] = jnp.zeros(value_acc.shape, F32)

    def step(block, carry):
        first = pl.multiple_of(block * BLOCK, BLOCK)
        shift = pl.multiple_of((blocks - 1 - block) * BLOCK, BLOCK)
        query_rows = query[pl.ds(first, BLOCK), :]
        grad_rows = grad[pl.ds(first, BLOCK), :]
        acc = jnp.zeros((BLOCK, width), F32)
        for head in range(heads):
            mask = head_mask(head, head_width, width)
            span = slice(head * head_width, (head + 1) * head_width)
            scores = product(query_rows * mask.astype(BF), key_t[...])
            scores = scores + bias[head, :, pl.ds(shift, tokens)]
            chances = jnp.exp(scores - logsum[pl.ds(first, BLOCK), head : head + 1])
            prob_grad = product(grad_rows * mask.astype(BF), value_t[...])
            centre = jnp.sum(chances * prob_grad, axis=-1, keepdims=True)
            score_grad = chances * (prob_grad - centre)
            score_low = score_grad.astype(BF)
            sums[head, :, pl.ds(shift, tokens)] += score_grad
            acc = acc + product(score_low, key[...]) * mask
            key_acc[span, :] += product(query_t[span, pl.ds(first, BLOCK)], score_low)
            value_acc[span, :] += product(grad_t[span, pl.ds(first, BLOCK)], chances.astype(BF))
        query_back[pl.ds(first, BLOCK), :] = acc.astype(BF)
        return carry

    def run(begin, end):
        lax.fori_loop(begin, end, step, 0)

    run(0, 1)
    scatter(0)
    run(1, 2)
    scatter(1)
    run(2, 3)
    scatter(2)
    collect(0)
    run(3, 4)
    scatter(3)
    collect(1)
    gather.forward(0)
    run(4, 5)
    collect(2)
    gather.forward(1)
    run(5, 6)
    collect(3)
    gather.forward(2)
    run(6, 7)
    gather.forward(3)
    run(7, blocks)
    backs = [query_back[...], key_acc[...].T.astype(BF), value_acc[...].T.astype(BF)]
    backs_t = [query_back[...].astype(F32).T.astype(BF)]
    backs_t += [key_acc[...].astype(BF), value_acc[...].astype(BF)]
    part = product(backs[0], query_w[...])
    part = part + product(backs[1], key_w[...]) + product(backs[2], value_w[...])
    normed_part[...] = part.astype(BF)
    for i in range(3):
        large[i * width : (i + 1) * width, :] = product(backs_t[i], normed[...]).astype(BF)
    inputs = rows[...].astype(F32)
    line = jnp.sum(part * inputs * inverse_rms(inputs), axis=0, keepdims=True)
    small[...] = jnp.zeros(small.shape, BF)
    small[0:experts, 0:full] = router_grad.astype(BF)
    row = lax.broadcasted_iota(jnp.int32, (16, 1), 0)
    pair = jnp.where(row == 0, gain_grad, jnp.where(row == 8, line, 0.0))
    small[32:48, 0:full] = pair.astype(BF)

    padded = buckets.shape[1]
    lines = []
    for head in range(heads):
        wide = jnp.concatenate(
            [sums[head], jnp.zeros((BLOCK, padded - sums.shape[2]), F32)], axis=1
        )
        gathered = jnp.zeros((8, padded), F32)
        for piece_at in range(0, BLOCK, 8):
            piece = wide[piece_at : piece_at + 8, :]
            gathered = gathered + pltpu.roll(piece, (BLOCK - 1 - piece_at) % padded, 1)
        line = jnp.zeros((1, padded), F32)
        for i in range(8):
            line = line + pltpu.roll(gathered, (padded - i) % padded, 1)[i : i + 1, :]
        lines.append(line)
    number = lax.broadcasted_iota(jnp.int32, (table.shape[1], padded), 0)
    matches = jnp.where(buckets[...] == number, 1.0, 0.0)
    stacked = jnp.concatenate(lines + [jnp.zeros((16 - heads, padded), F32)], axis=0)
    sums_of = lax.dot_general(
        stacked,
        matches,
        (((1,), (1,)), ((), ())),
        precision=lax.Precision.HIGHEST,
        preferred_element_type=F32,
    )
    blank = jnp.zeros((16, 128 - table.shape[1]), F32)
    small[48:64, 0:128] = jnp.concatenate([sums_of, blank], axis=1).astype(BF)
    for k in range(GROUPS):
        gather.finish(k)
    kept.wait()
    drain()


def per_device(
    layer_in, expert_ids, rel_buckets, first_gain, query_weight, key_weight, value_weight,
    proj_weight, rel_table, second_gain, router_weight, expert_in, expert_out, cotangent,
):
    tokens, width = layer_in.shape
    heads = rel_table.shape[1]
    here = query_weight.shape[1]
    head_width = here // heads
    experts = router_weight.shape[1]
    capacity = 5 * tokens // (4 * experts)
    body = 16 * experts
    packed = 2 * width + width // 2
    span = 2 * tokens - BLOCK
    ring_size = width // here
    gain_one = first_gain
    gain_two = second_gain
    buckets = jnp.pad(rel_buckets, (0, 1), constant_values=-1)[None, :]
    weights = (query_weight.T, key_weight.T, value_weight.T)
    table = rel_table.T
    router = router_weight.T

    wide_lanes = (packed + 128) // 4
    kept = [
        ((tokens, here), BF),
        ((tokens, width), BF),
        ((tokens, here), BF),
        ((here, tokens), BF),
        ((tokens, here), BF),
        ((here, tokens), BF),
        ((here, tokens), BF),
        ((tokens, 128), F32),
    ]
    (
        mixed, normed, query, query_t, key, key_t, value_t, logsum,
        residual, hidden, probs, slots, slots_row, gates,
    ) = call(
        functools.partial(attend_body, head_width, capacity),
        "attend",
        kept
        + [
            ((tokens, width), F32),
            ((tokens, width), BF),
            ((tokens, experts), F32),
            ((tokens, 1), jnp.int32),
            ((1, tokens), jnp.int32),
            ((tokens, 1), F32),
        ],
        [pltpu.VMEM(*entry) for entry in kept]
        + [
            pltpu.VMEM((ring_size, tokens // 2, 2 * here), BF),
            pltpu.VMEM((ring_size, here, width), BF),
            pltpu.VMEM((heads, BLOCK, span), F32),
            pltpu.VMEM((tokens, here), BF),
            sems(tokens // BLOCK // 2, 8),
            sems(1, 8),
            sems(3, 2),
            sems(len(kept)),
        ],
        layer_in, gain_one, *weights, proj_weight, buckets, table, gain_two, router,
        expert_ids.reshape(1, tokens),
        mib=62,
        number=1,
        far_out=range(len(kept)),
    )
    value, back_sum, in_grad, out_grad = call(
        functools.partial(moe_body, experts, capacity, 384, wide_lanes),
        "experts",
        [
            ((body, packed + 128), BF),
            ((body, packed + 128), BF),
            ((width, expert_in.shape[2]), F32),
            ((expert_out.shape[1], width), F32),
        ],
        [
            pltpu.VMEM((2, body, packed), BF),
            pltpu.VMEM((2, body, packed), BF),
            pltpu.VMEM((body, packed + 128), BF),
            pltpu.VMEM((width, expert_in.shape[2]), F32),
            pltpu.VMEM((expert_out.shape[1], width), F32),
            sems(2),
            *return_scratch(experts, wide_lanes),
            sems(2),
            sems(GROUPS),
            sems(GROUPS),
            sems(GROUPS, 8),
        ],
        hidden, gates, slots_row, cotangent, expert_in[0], expert_out[0],
        number=2,
        far_out=(2, 3),
    )
    returned, residual_grad, normed_part, large, small = call(
        functools.partial(backward_body, experts, capacity, head_width, wide_lanes),
        "backward",
        [
            ((body, packed + 128), BF),
            ((tokens, width), F32),
            ((tokens, width), BF),
            ((4 * here, width), BF),
            ((64, 1024), BF),
        ],
        [
            pltpu.VMEM((tokens, width), BF),
            pltpu.VMEM((tokens, here), BF),
            pltpu.VMEM((here, tokens), BF),
            pltpu.VMEM((tokens, here), BF),
            pltpu.VMEM((here, tokens), BF),
            pltpu.VMEM((here, tokens), BF),
            pltpu.VMEM((tokens, 128), F32),
            pltpu.VMEM((tokens, width), BF),
            pltpu.VMEM((tokens, width), F32),
            sems(9),
            pltpu.VMEM((tokens, here), BF),
            pltpu.VMEM((here, tokens), BF),
            pltpu.VMEM((heads, BLOCK, span), F32),
            pltpu.VMEM((heads, BLOCK, span), F32),
            pltpu.VMEM((tokens, here), BF),
            pltpu.VMEM((here, tokens), F32),
            pltpu.VMEM((here, tokens), F32),
            *return_scratch(experts, wide_lanes),
        ],
        value, back_sum, slots, residual, hidden, probs, gain_two, router, cotangent, mixed,
        proj_weight, normed, query, query_t, key, key_t, value_t, logsum, *weights, buckets, table,
        layer_in,
        mib=56,
        number=5,
        far_in=(*range(11, 18), 23),
        far_out=(1,),
    )
    peers = experts // 2
    tall, wide = 4 * here // peers, width // 2
    summed, large_sum, small_sum, lines, output = call(
        functools.partial(final_body, experts, capacity),
        "final",
        [
            ((tokens, width), BF),
            ((4 * here, width), BF),
            ((64, 1024), BF),
            ((3, 16, 1024), BF),
            ((tokens, width), BF),
        ],
        [
            pltpu.VMEM((4 * here, wide), BF),
            pltpu.VMEM((64, 512), BF),
            pltpu.VMEM((peers, tall, wide), BF),
            pltpu.VMEM((peers, 16, 128), BF),
            pltpu.VMEM((body, packed + 128), BF),
            pltpu.VMEM((tokens, width), F32),
            pltpu.VMEM((tokens, width), BF),
            sems(3),
            *reduce_scratch(4, tokens // 32, width),
            sems(8),
            sems(8),
            sems(3, 2),
            sems(4, 8),
            sems(4, 8),
        ],
        normed_part, large, small, returned, slots, gates, residual,
        number=4,
        far_in=(3, 6),
        far_out=(4,),
    )

    def whole(array):
        return pl.BlockSpec(array.shape, lambda i: (0,) * len(array.shape))

    def strip(array):
        return pl.BlockSpec((array.shape[0] // 8, array.shape[1]), lambda i: (i, 0))

    results = [
        jax.ShapeDtypeStruct(shape, F32)
        for shape in [(tokens, width)] + [(here, width)] * 4
        + [(experts, width), (width,), (width,), table.shape]
    ]
    passed = (output, in_grad, out_grad)
    strips = [strip(one) for one in passed]
    (
        input_grad, query_grad, key_grad, value_grad, proj_total, router_total, gain_total,
        first_total, table_total, output, in_grad, out_grad,
    ) = pl.pallas_call(
        finish_body,
        name="finish",
        grid=(8,),
        out_shape=results + [jax.ShapeDtypeStruct(one.shape, one.dtype) for one in passed],
        in_specs=[
            strip(summed), strip(layer_in), strip(residual_grad), whole(gain_one),
            whole(large_sum), whole(small_sum), whole(lines), *strips,
        ],
        out_specs=[strip(results[0])] + [whole(result) for result in results[1:]] + strips,
        compiler_params=pltpu.CompilerParams(vmem_limit_bytes=32 * MIB),
    )(summed, layer_in, residual_grad, gain_one, large_sum, small_sum, lines, *passed)
    return (
        output,
        input_grad,
        first_total,
        query_grad.T,
        key_grad.T,
        value_grad.T,
        proj_total,
        table_total.T,
        gain_total,
        router_total.T,
        in_grad[None],
        out_grad[None],
    )


def solution(mesh):
    return jax.shard_map(
        per_device,
        mesh=mesh,
        in_specs=(
            P("exp", None),
            P("exp", None),
            P(),
            P(),
            P(None, "tp"),
            P(None, "tp"),
            P(None, "tp"),
            P("tp", None),
            P(None, "tp"),
            P(),
            P(),
            P("exp", None, "tp"),
            P("exp", "tp", None),
            P("exp", None),
        ),
        out_specs=(
            P("exp", None),
            P("exp", None),
            P(),
            P(None, "tp"),
            P(None, "tp"),
            P(None, "tp"),
            P("tp", None),
            P(None, "tp"),
            P(),
            P(),
            P("exp", None, "tp"),
            P("exp", "tp", None),
        ),
        check_vma=False,
    )
```
